32 devices in a mesh: blk: 16 (over z, x, core), rows: 2 (over y).
Axes of the slice: x: 2, y: 2, z: 4, core: 2. Of those that a mesh axis runs over, the one named last changes fastest.
Arguments:
- residues: bfloat16 [8, 1024, 768], P('rows', 'blk'), may hold values from -6 to 6
- pair_features: bfloat16 [8, 256, 256, 256], P('rows', None, 'blk'), may hold values from -6 to 6
- chain_lengths: int32 [8, 4], P('rows'), may hold values from 0 to 1024, as said below
- time_bins: int32 [8, 4], P('rows'), may hold values from 0 to 127
- fold_class: int32 [8, 4], P('rows'), may hold values from 0 to 39
- self_flag: int32 [8, 4], P('rows'), may hold values 0 or 1
- time_table: bfloat16 [128, 256], replicated, may hold values from -6 to 6
- class_table: bfloat16 [40, 256], replicated, may hold values from -6 to 6
- modulate: bfloat16 [256, 4608], P('blk'), may hold values from -0.1875 to 0.1875
- offset: bfloat16 [4608], replicated, may hold values from 0.5 to 1.5
- heads: bfloat16 [768, 2304], P('blk'), may hold values from -0.109375 to 0.109375
- pairing: bfloat16 [256, 12], replicated, may hold values from -0.375 to 0.375
- gating: bfloat16 [768, 768], P('blk'), may hold values from -0.21875 to 0.21875
- gating_bias: bfloat16 [768], replicated, may hold values from -4 to 4
- project: bfloat16 [768, 768], P('blk'), may hold values from -0.875 to 0.875
- widen_gate: bfloat16 [768, 3072], P('blk'), may hold values from -0.21875 to 0.21875
- widen_up: bfloat16 [768, 3072], P('blk'), may hold values from -0.21875 to 0.21875
- narrow: bfloat16 [3072, 768], P('blk'), may hold values from -0.109375 to 0.109375
- coordinate: bfloat16 [768, 3], replicated, may hold values from -0.21875 to 0.21875
- recycle: bfloat16 [3, 768], replicated, may hold values from -3.5 to 3.5
- cotangent: bfloat16 [8, 1024, 768], P('rows', 'blk'), may hold values from -6 to 6
Outputs:
- layer_out: bfloat16 [8, 1024, 768], P('rows', 'blk')
- grad_residues: bfloat16 [8, 1024, 768], P('rows', 'blk')
- grad_pair: bfloat16 [8, 256, 256, 256], P('rows', None, 'blk')
- grad_time: float32 [128, 256], replicated
- grad_class: float32 [40, 256], replicated
- grad_modulate: float32 [256, 4608], P('blk')
- grad_offset: float32 [4608], replicated
- grad_heads: float32 [768, 2304], P('blk')
- grad_pairing: float32 [256, 12], replicated
- grad_gating: float32 [768, 768], P('blk')
- grad_gatebias: float32 [768], replicated
- grad_project: float32 [768, 768], P('blk')
- grad_widengate: float32 [768, 3072], P('blk')
- grad_widenup: float32 [768, 3072], P('blk')
- grad_narrow: float32 [3072, 768], P('blk')
- grad_recycle: float32 [3, 768], replicated
The draws below stay inside these ranges and needn't reach their ends.
Inputs may be any that keep to these rules, and one draw needn't show every extreme that they name: `chain_lengths`: in each row the entries sum to 1024: one to 4 chains, then zeros. In each aligned block of 4 rows that start at a multiple of 4, one row is a single chain of 1024.
All inputs are finite; a program needn't handle non-finite values. No bound on the sum of `self_flag` on one device may be relied on, other than what follows from the above.
Results may differ from the reference program's by a relative error of at most 0.022.
Values may be sent and summed in bfloat16 or wider, within the bound.
No kernel may reach another device: no remote copies, remote signals or barrier semaphores. Data moves between devices by JAX's collectives and lax.ppermute only.
A program may use at most 576 MiB of HBM per device.

```python
import jax
import jax.numpy as jnp
from jax import lax

D = 768
HEADS = 12
HEAD = 64
FF = 3072
P_SIZE = 256
C = 256
NCLASS = 40
NTIME = 128
MAXCH = 4
GRAIN = 4
ROWS_DEV = 4
ROW_LEN = 1024
ROWS = 8


def draw_chain_lengths(key, part):
    key = jax.random.fold_in(key, 17)
    count_key, share_key, pick_key = jax.random.split(key, 3)
    chain_count = jax.random.randint(count_key, (ROWS,), 1, MAXCH + 1)
    slot_ids = jnp.arange(MAXCH, dtype=jnp.int32)
    is_live = slot_ids[None, :] < chain_count[:, None]
    shares = jnp.where(is_live, jax.random.randint(share_key, (ROWS, MAXCH), 1, 1000), 0)
    floor_len = ROW_LEN // (2 * MAXCH)
    spare_len = ROW_LEN - chain_count * floor_len
    running = jnp.cumsum(shares, axis=1)
    upper_end = running * spare_len[:, None] // running[:, -1:]
    lower_end = jnp.concatenate([jnp.zeros((ROWS, 1), jnp.int32), upper_end[:, :-1]], axis=1)
    lengths = jnp.where(is_live, upper_end - lower_end + floor_len, 0)
    groups = ROWS // ROWS_DEV
    chosen = jax.random.randint(pick_key, (groups,), 0, ROWS_DEV)
    full_rows = jnp.arange(groups, dtype=jnp.int32) * ROWS_DEV + chosen
    is_full = jnp.any(jnp.arange(ROWS, dtype=jnp.int32)[:, None] == full_rows[None, :], axis=1)
    single = jnp.where(slot_ids == 0, ROW_LEN, 0)
    return jnp.where(is_full[:, None], single[None, :], lengths).astype(jnp.int32)


def touch_ends(values, rng, least, high):
    shape = values.shape
    index_at = [jax.random.randint(jax.random.fold_in(rng, axis), (), 0, shape[axis]) for axis in range(len(shape))]
    values = values.at[tuple(index_at)].set(least)
    longest = shape.index(max(shape))
    index_at[longest] = (index_at[longest] + 1) % shape[longest]
    return values.at[tuple(index_at)].set(high)


def block_levels(rng, extent, cuts, low, largest):
    loudness, own = 1.0, jax.random.fold_in(rng, 6)
    for dim, blocks in cuts:
        steps = jnp.exp(jax.random.uniform(jax.random.fold_in(own, dim), (blocks,), jnp.float32, low / len(cuts), largest / len(cuts)))
        loudness = loudness * jnp.repeat(steps, extent[dim] // blocks).reshape([-1 if axis == dim else 1 for axis in range(len(extent))])
    return loudness


def noise(stream_key, shape, deviation, limit, cuts=(), kind=jnp.bfloat16):
    level = block_levels(stream_key, shape, cuts, -0.22, 0.18) if cuts else 1.0
    array = jax.random.normal(stream_key, shape, jnp.float32) * deviation * level
    return jnp.minimum(jnp.maximum(array, -limit), limit).astype(kind)


def setup_inputs(seed: int = 0) -> dict:
    arg_keys = jax.random.split(jax.random.key(seed), 22)
    residues = noise(arg_keys[0], (ROWS, ROW_LEN, D), 1.0, 6.0, ((0, 2), (1, 16)))
    pair_features = noise(arg_keys[1], (ROWS, ROW_LEN // GRAIN, ROW_LEN // GRAIN, P_SIZE), 1.0, 6.0, ((0, 2), (2, 16)))
    chain_lengths = draw_chain_lengths(jax.random.fold_in(arg_keys[21], 71), 0)
    time_bins = touch_ends(jax.random.randint(arg_keys[3], (ROWS, MAXCH), 0, NTIME), jax.random.fold_in(arg_keys[3], 1), 0, NTIME - 1).astype(jnp.int32)
    fold_class = touch_ends(jax.random.randint(arg_keys[4], (ROWS, MAXCH), 0, NCLASS), jax.random.fold_in(arg_keys[4], 1), 0, NCLASS - 1).astype(jnp.int32)
    self_flag = touch_ends((jax.random.randint(arg_keys[5], (ROWS, MAXCH), 0, 2) < 1).astype(jnp.int32), jax.random.fold_in(arg_keys[5], 1), 0, 1)
    time_table = noise(arg_keys[6], (NTIME, C), 1.0, 6.0)
    class_table = noise(arg_keys[7], (NCLASS, C), 1.0, 6.0)
    modulate = noise(arg_keys[8], (C, 6 * D), (4 * C) ** -0.5, 0.1875, ((0, 16),))
    offset = jnp.clip(1.0 + 0.1 * jax.random.normal(arg_keys[9], (6 * D,), jnp.float32), 0.5, 1.5).astype(jnp.bfloat16)
    heads = noise(arg_keys[10], (D, 3 * D), (4 * D) ** -0.5, 0.109375, ((0, 16),))
    pairing = noise(arg_keys[11], (P_SIZE, HEADS), P_SIZE ** -0.5, 0.375)
    gating = noise(arg_keys[12], (D, D), D ** -0.5, 0.21875, ((0, 16),))
    gating_bias = noise(arg_keys[13], (D,), 1.0, 4.0)
    project = noise(arg_keys[14], (D, D), (D // 16) ** -0.5, 0.875, ((0, 16),))
    widen_gate = noise(arg_keys[15], (D, FF), D ** -0.5, 0.21875, ((0, 16),))
    widen_up = noise(arg_keys[16], (D, FF), D ** -0.5, 0.21875, ((0, 16),))
    narrow = noise(arg_keys[17], (FF, D), FF ** -0.5, 0.109375, ((0, 16),))
    coordinate = noise(arg_keys[18], (D, 3), D ** -0.5, 0.21875)
    recycle = noise(arg_keys[19], (3, D), 3 ** -0.5, 3.5)
    cotangent = noise(arg_keys[20], (ROWS, ROW_LEN, D), 1.0, 6.0, ((0, 2), (1, 16)))
    return dict(residues=residues, pair_features=pair_features, chain_lengths=chain_lengths, time_bins=time_bins, fold_class=fold_class, self_flag=self_flag, time_table=time_table, class_table=class_table, modulate=modulate, offset=offset, heads=heads, pairing=pairing, gating=gating, gating_bias=gating_bias, project=project, widen_gate=widen_gate, widen_up=widen_up, narrow=narrow, coordinate=coordinate, recycle=recycle, cotangent=cotangent)


@jax.custom_vjp
def low(v):
    return lax.optimization_barrier(v.astype(jnp.bfloat16)).astype(jnp.float32)

@jax.custom_vjp
def low_back(v):
    return v

def low_keep(v):
    return (low(v), None)

def low_pass(kept, grad):
    return (grad,)

def back_keep(v):
    return (v, None)

def back_low(kept, grad):
    return (low(grad),)
low.defvjp(low_keep, low_pass)
low_back.defvjp(back_keep, back_low)
highest = lax.Precision.HIGHEST

def product(former, latter):
    return jnp.dot(former, latter, precision=highest)

def normalize(values):
    center = values - lax.optimization_barrier(jnp.mean(values, axis=-1, keepdims=True))
    spread_sq = lax.optimization_barrier(jnp.mean(center * center, axis=-1, keepdims=True))
    return center * lax.rsqrt(spread_sq + 1e-06)

def layer_row(params, pieces):
    time_table, class_table, modulate, offset, heads, pairing, gating, gating_bias, project, widen_gate, widen_up, narrow, recycle = params
    start_row, pair_row, lengths, time_ids, classes, chain_flags, predicted = pieces
    chain_ends = jnp.cumsum(lengths.astype(jnp.int32))
    places = jnp.arange(ROW_LEN, dtype=jnp.int32)
    chain_id = lax.optimization_barrier(jnp.sum((places[:, None] >= chain_ends[None, :]).astype(jnp.int32), axis=1))
    member = (chain_id[:, None] == jnp.arange(MAXCH, dtype=jnp.int32)[None, :]).astype(jnp.float32)
    same_chain = chain_id[:, None] == chain_id[None, :]
    time_hot = (time_ids[:, None] == jnp.arange(NTIME, dtype=jnp.int32)[None, :]).astype(jnp.float32)
    class_hot = (classes[:, None] == jnp.arange(NCLASS, dtype=jnp.int32)[None, :]).astype(jnp.float32)
    condition = product(time_hot, time_table) + product(class_hot, class_table)
    smooth = low(jax.nn.silu(condition))
    per_chain = product(smooth, modulate) + offset
    modulation = product(member, per_chain)
    attend_shift, attend_scale, attend_gate, feed_shift, feed_scale, feed_gate = jnp.split(modulation, 6, axis=1)
    flag_row = product(member, chain_flags.astype(jnp.float32)[:, None])
    begin_rows = start_row + flag_row * product(low(predicted), recycle)
    hidden = low(normalize(begin_rows) * (1.0 + attend_scale) + attend_shift)
    triple = low_back(low(product(hidden, heads)))
    queries = triple[:, :D].reshape(ROW_LEN, HEADS, HEAD)
    key_rows = triple[:, D:2 * D].reshape(ROW_LEN, HEADS, HEAD)
    value_rows = triple[:, 2 * D:].reshape(ROW_LEN, HEADS, HEAD)
    tile_bias = low(low_back(jnp.einsum('qkp,ph->hqk', pair_row.astype(jnp.float32), pairing, precision=highest)))
    pair_bias = jnp.repeat(jnp.repeat(tile_bias, GRAIN, axis=1), GRAIN, axis=2)
    scores = low_back(jnp.einsum('qhe,khe->hqk', queries, key_rows, precision=highest) * HEAD ** (-0.5) + pair_bias)
    masked = jnp.where(same_chain[None], scores, -1000000000.0)
    row_max = lax.optimization_barrier(jnp.max(masked, axis=-1, keepdims=True))
    exponent = jnp.exp(masked - row_max)
    softmax_w = exponent / lax.optimization_barrier(jnp.sum(exponent, axis=-1, keepdims=True))
    probs_low = low(softmax_w)
    attended = low_back(jnp.einsum('hqk,khe->qhe', probs_low, value_rows, precision=highest).reshape(ROW_LEN, D))
    gate_logit = low_back(product(hidden, gating) + gating_bias)
    mixed_low = low(attended * jax.nn.sigmoid(gate_logit))
    attend_out = low_back(product(mixed_low, project))
    after_attend = begin_rows + attend_gate * attend_out
    hidden_two = low(normalize(after_attend) * (1.0 + feed_scale) + feed_shift)
    gate_pre = low_back(product(hidden_two, widen_gate))
    lift_pre = low_back(product(hidden_two, widen_up))
    inner_act = low(jax.nn.silu(gate_pre) * lift_pre)
    branch = low_back(product(inner_act, narrow))
    return after_attend + feed_gate * branch

def reference(residues, pair_features, chain_lengths, time_bins, fold_class, self_flag, time_table, class_table, modulate, offset, heads, pairing, gating, gating_bias, project, widen_gate, widen_up, narrow, coordinate, recycle, cotangent):
    params = jax.tree.map(lambda array_in: array_in.astype(jnp.float32), (time_table, class_table, modulate, offset, heads, pairing, gating, gating_bias, project, widen_gate, widen_up, narrow, recycle))
    start_all = residues.astype(jnp.float32)
    pair_all = pair_features.astype(jnp.float32)
    no_coords = jnp.zeros((ROWS, ROW_LEN, 3), jnp.float32)

    def layer_rows(params_in, start_in, pair_in, predicted):
        row_step = jax.checkpoint(lambda pieces: layer_row(params_in, pieces))
        return lax.map(row_step, (start_in, pair_in, chain_lengths, time_bins, fold_class, self_flag, predicted))
    first_pass = low(layer_rows(params, start_all, pair_all, no_coords))
    predicted = low(jnp.einsum('rtd,dc->rtc', first_pass, coordinate.astype(jnp.float32), precision=highest))

    def second_pass(params_in, start_in, pair_in):
        return layer_rows(params_in, start_in, pair_in, predicted)
    result, pullback = jax.vjp(second_pass, params, start_all, pair_all)
    grad_params, grad_start, grad_pairs = pullback(cotangent.astype(jnp.float32))
    return (result.astype(jnp.bfloat16), grad_start.astype(jnp.bfloat16), grad_pairs.astype(jnp.bfloat16), grad_params[0], grad_params[1], grad_params[2], grad_params[3], grad_params[4], grad_params[5], grad_params[6], grad_params[7], grad_params[8], grad_params[9], grad_params[10], grad_params[11], grad_params[12])
```

```python
import functools

import jax
import jax.numpy as jnp
from jax import lax
from jax.experimental import pallas as pl
from jax.experimental.pallas import tpu as pltpu
from jax.sharding import PartitionSpec as P

TEAM = 4
F32, BF16 = jnp.float32, jnp.bfloat16
HIGHEST = lax.Precision.HIGHEST
VMEM_BYTES = 58 * 1024 * 1024


def dot(former, latter, contract=((1,), (0,))):
    return lax.dot_general(former, latter, (contract, ((), ())), preferred_element_type=F32)


NT, TN = ((1,), (1,)), ((0,), (0,))


def normalize(values):
    center = values - jnp.mean(values, axis=-1, keepdims=True)
    inverse = lax.rsqrt(jnp.mean(center * center, axis=-1, keepdims=True) + 1e-06)
    return center * inverse, inverse


def norm_back(grad, normed, inverse):
    first = jnp.mean(grad, axis=-1, keepdims=True)
    second = jnp.mean(grad * normed, axis=-1, keepdims=True)
    return inverse * (grad - first - normed * second)


def call(kernel, grid, ins, outs, out_shape, scratch=(), flops=0, moved=0, prefetch=0):
    return pl.pallas_call(
        kernel,
        grid_spec=pltpu.PrefetchScalarGridSpec(
            num_scalar_prefetch=prefetch,
            grid=grid,
            in_specs=ins,
            out_specs=outs,
            scratch_shapes=list(scratch),
        ),
        out_shape=out_shape,
        cost_estimate=pl.CostEstimate(flops=flops, bytes_accessed=moved, transcendentals=0),
        compiler_params=pltpu.CompilerParams(vmem_limit_bytes=VMEM_BYTES),
    )


def whole(shape):
    return pl.BlockSpec(shape, lambda *_: (0,) * len(shape), pipeline_mode=pl.Buffered(buffer_count=1))


def held(shape):
    return pl.BlockSpec(shape, lambda *_: (0,) * len(shape))


def pair_bias(pair_features, pairing):
    rows, q_tiles, k_tiles, width = pair_features.shape
    heads = pairing.shape[1]
    padded = jnp.pad(pairing, ((0, 0), (0, 128 - heads)))

    def kernel(pair_ref, weight_ref, out_ref, flat, turned):
        flat[...] = dot(pair_ref[0].reshape(q_tiles * k_tiles, width), weight_ref[...])
        for k in range(k_tiles):
            turned[:, k, :] = flat[pl.ds(k, q_tiles, stride=k_tiles), :].T[:heads]
        out_ref[0] = turned[...].astype(BF16)

    return call(
        kernel,
        (rows,),
        [
            pl.BlockSpec((1, q_tiles, k_tiles, width), lambda r: (r, 0, 0, 0)),
            whole((width, 128)),
        ],
        pl.BlockSpec((1, heads, k_tiles, q_tiles), lambda r: (r, 0, 0, 0)),
        jax.ShapeDtypeStruct((rows, heads, k_tiles, q_tiles), BF16),
        [pltpu.VMEM((q_tiles * k_tiles, 128), F32), pltpu.VMEM((heads, k_tiles, q_tiles), F32)],
        flops=2 * pair_features.size * 128,
        moved=2 * pair_features.size,
    )(pair_features, padded)


def pair_back(pair_features, pairing, grad_bias):
    rows, q_tiles, k_tiles, width = pair_features.shape
    heads = pairing.shape[1]
    padded = jnp.pad(pairing.T, ((0, 128 - heads), (0, 0)))

    def kernel(pair_ref, weight_ref, grad_ref, out_ref, sum_ref, flat):
        @pl.when(pl.program_id(0) == 0)
        def _():
            sum_ref[...] = jnp.zeros_like(sum_ref)

        grads = grad_ref[0].astype(F32)
        blank = jnp.zeros((128 - heads, q_tiles), F32)
        for k in range(k_tiles):
            piece = jnp.concatenate([grads[:, k, :], blank], axis=0)
            flat[pl.ds(k, q_tiles, stride=k_tiles), :] = piece.T
        low = flat[...].astype(BF16)
        out_ref[0] = dot(low, weight_ref[...]).astype(BF16).reshape(q_tiles, k_tiles, width)
        sum_ref[...] += dot(low, pair_ref[0].reshape(q_tiles * k_tiles, width), TN)

    return call(
        kernel,
        (rows,),
        [
            pl.BlockSpec((1, q_tiles, k_tiles, width), lambda r: (r, 0, 0, 0)),
            whole((128, width)),
            pl.BlockSpec((1, heads, k_tiles, q_tiles), lambda r: (r, 0, 0, 0)),
        ],
        [pl.BlockSpec((1, q_tiles, k_tiles, width), lambda r: (r, 0, 0, 0)), held((128, width))],
        [
            jax.ShapeDtypeStruct(pair_features.shape, BF16),
            jax.ShapeDtypeStruct((128, width), F32),
        ],
        [pltpu.VMEM((q_tiles * k_tiles, 128), F32)],
        flops=4 * pair_features.size * 128,
        moved=4 * pair_features.size,
    )(pair_features, padded, grad_bias)


def assemble(team, chunks, scratch):
    rows, tiles = chunks[0].shape[0], chunks[0].shape[2]
    for d, chunk in enumerate(chunks):
        for r in range(rows):
            start = pl.multiple_of((r * TEAM + (team ^ d)) * tiles, tiles)
            scratch[pl.ds(start, tiles), :] = chunk[r, 0]


def project_rows(begin, member, table_ref, weight_ref, bias_ref, outs, hidden_ref, width, head):
    mods = dot(member, table_ref[:, : 2 * width])
    normed, _ = normalize(begin)
    hidden = (normed * (1.0 + mods[:, width:]) + mods[:, :width]).astype(BF16)
    if hidden_ref is not None:
        hidden_ref[...] = hidden
    both = dot(hidden, weight_ref[...])
    part = both.shape[1] // 4
    turned = both.T
    count = part // head
    q_ref, k_ref, v_ref, key_ref, value_ref, gate_ref = outs
    scaled = turned[:part].astype(BF16) * BF16(head**-0.5)
    q_ref[...] = scaled.reshape(count, head, -1)
    k_ref[...] = turned[part : 2 * part].astype(BF16).reshape(count, head, -1)
    v_ref[...] = turned[2 * part : 3 * part].astype(BF16).reshape(count, head, -1)
    for h in range(count):
        key_ref[h] = both[:, part + h * head : part + (h + 1) * head].astype(BF16)
        value_ref[h] = both[:, 2 * part + h * head : 2 * part + (h + 1) * head].astype(BF16)
    gate_ref[...] = (turned[3 * part :] + bias_ref[:, :1]).reshape(count, head, -1)


def qkv_specs(count, head, tokens, block):
    wide = pl.BlockSpec((count, head, block), lambda j, *_: (0, 0, j))
    tall = pl.BlockSpec((count, block, head), lambda j, *_: (0, j, 0))
    shapes = [jax.ShapeDtypeStruct((count, head, tokens), BF16)] * 3
    shapes += [jax.ShapeDtypeStruct((count, tokens, head), BF16)] * 2
    shapes += [jax.ShapeDtypeStruct((count, head, tokens), F32)]
    return [wide, wide, wide, tall, tall, wide], shapes


def first_rows(team, chunks, member, table, weight, gate_bias, count, head):
    rows, grain, tiles, width = chunks[0].shape
    tokens = rows * grain * tiles * TEAM
    block = tokens // grain

    def kernel(team_ref, c0, c1, c2, c3, member_ref, table_ref, weight_ref, bias_ref, row_ref, *rest):
        *outs, scratch = rest
        assemble(team_ref[0], (c0, c1, c2, c3), scratch)
        row_ref[...] = scratch[...]
        begin = scratch[...].astype(F32)
        project_rows(
            begin, member_ref[...], table_ref, weight_ref, bias_ref, outs, None, width, head
        )

    specs, shapes = qkv_specs(count, head, tokens, block)
    by_token = pl.BlockSpec((block, width), lambda j, *_: (j, 0))
    return call(
        kernel,
        (grain,),
        [pl.BlockSpec((rows, 1, tiles, width), lambda j, *_: (0, j, 0, 0))] * 4
        + [
            pl.BlockSpec((block, member.shape[1]), lambda j, *_: (j, 0)),
            whole(table.shape),
            whole(weight.shape),
            whole(gate_bias.shape),
        ],
        [by_token] + specs,
        [jax.ShapeDtypeStruct((tokens, width), BF16)] + shapes,
        [pltpu.VMEM((block, width), BF16)],
        flops=2 * tokens * weight.size,
        moved=2 * weight.size + 10 * tokens * width,
        prefetch=1,
    )(team, *chunks, member, table, weight, gate_bias)


def begin_of(row_ref, point_ref, recycle_ref):
    return row_ref[...].astype(F32) + dot(point_ref[...].astype(BF16), recycle_ref[...], TN)


def second_rows(row, points, recycle, member, table, weight, gate_bias, count, head, block):
    tokens, width = row.shape

    def kernel(row_ref, point_ref, recycle_ref, member_ref, table_ref, weight_ref, bias_ref, hidden_ref, *outs):
        begin = begin_of(row_ref, point_ref, recycle_ref)
        project_rows(
            begin, member_ref[...], table_ref, weight_ref, bias_ref, outs, hidden_ref, width, head
        )

    specs, shapes = qkv_specs(count, head, tokens, block)
    by_token = pl.BlockSpec((block, width), lambda j: (j, 0))
    return call(
        kernel,
        (tokens // block,),
        [
            by_token,
            pl.BlockSpec((8, block), lambda j: (0, j)),
            whole(recycle.shape),
            pl.BlockSpec((block, member.shape[1]), lambda j: (j, 0)),
            whole(table.shape),
            whole(weight.shape),
            whole(gate_bias.shape),
        ],
        [by_token] + specs,
        [jax.ShapeDtypeStruct((tokens, width), BF16)] + shapes,
        flops=2 * tokens * weight.size,
        moved=2 * weight.size + 10 * tokens * width,
    )(row, points, recycle, member, table, weight, gate_bias)


def attend(queries, keys, values, gate, bias, q_chain, k_chain, place, block, keep):
    count, head, tokens = queries.shape
    key_tokens = keys.shape[1]
    sources, _, tiles, _ = bias.shape
    folds = key_tokens // block
    grain = tokens // block

    def kernel(q_ref, k_ref, v_ref, gate_ref, bias_ref, qc_ref, kc_ref, mixed_ref, *rest):
        if keep:
            attended_ref, probs_ref, spread = rest
        else:
            (spread,) = rest

        @pl.when(pl.program_id(1) == 0)
        def _():
            for b in range(sources):
                spread[place[b] * tiles : (place[b] + 1) * tiles, :] = bias_ref[b, 0].astype(F32)

        q = q_ref[0]
        q_chain = qc_ref[0:1, :]
        scores = []
        for f in range(folds):
            lines = slice(f * block, (f + 1) * block)
            part = f // grain
            s = dot(k_ref[0, lines, :], q) + spread[part * block : (part + 1) * block, :]
            kc = kc_ref[lines, :]
            same = jnp.concatenate([kc] * (block // 128), axis=1) == q_chain
            scores.append(jnp.where(same, s, -1000000000.0))
        top = functools.reduce(jnp.maximum, [jnp.max(s, axis=0, keepdims=True) for s in scores])
        powers = [jnp.exp(s - top) for s in scores]
        total = functools.reduce(jnp.add, [jnp.sum(e, axis=0, keepdims=True) for e in powers])
        share = 1.0 / total
        attended = jnp.zeros((head, block), F32)
        for f in range(folds):
            lines = slice(f * block, (f + 1) * block)
            probs = (powers[f] * share).astype(BF16)
            if keep:
                probs_ref[0, lines, :] = probs
            attended += dot(v_ref[0, :, lines], probs)
        mixed_ref[0] = (attended * jax.nn.sigmoid(gate_ref[0])).astype(BF16)
        if keep:
            attended_ref[0] = attended

    by_query = pl.BlockSpec((1, head, block), lambda h, i: (h, 0, i))
    outs = [by_query]
    shapes = [jax.ShapeDtypeStruct((count, head, tokens), BF16)]
    if keep:
        outs += [by_query, pl.BlockSpec((1, key_tokens, block), lambda h, i: (h, 0, i))]
        shapes += [
            jax.ShapeDtypeStruct((count, head, tokens), F32),
            jax.ShapeDtypeStruct((count, key_tokens, tokens), BF16),
        ]
    return call(
        kernel,
        (count, grain),
        [
            by_query,
            pl.BlockSpec((1, key_tokens, head), lambda h, i: (h, 0, 0)),
            pl.BlockSpec((1, head, key_tokens), lambda h, i: (h, 0, 0)),
            by_query,
            pl.BlockSpec((sources, 1, tiles, block), lambda h, i: (0, h, 0, 0)),
            pl.BlockSpec((8, block), lambda h, i: (0, i)),
            whole(k_chain.shape),
        ],
        outs,
        shapes,
        [pltpu.VMEM((sources * tiles, block), F32)],
        flops=8 * count * tokens * key_tokens * head,
        moved=2 * count * tokens * key_tokens,
    )(queries, keys, values, gate, bias, q_chain, k_chain)


def attend_back(queries, keys, value_rows, gate, attended, probs, own, other, place, tiles, block):
    count, head, tokens = queries.shape
    key_tokens = value_rows.shape[1]
    folds, grain = key_tokens // block, tokens // block
    sources = len(place)

    def kernel(
        q_ref, k_ref, v_ref, gate_ref, attended_ref, probs_ref, own_ref, other_ref,
        dq_ref, dk_ref, dv_ref, logit_ref, bias_ref, key_sum, value_sum, bias_sum,
    ):
        step = pl.program_id(1)

        @pl.when(step == 0)
        def _():
            key_sum[...] = jnp.zeros_like(key_sum)
            value_sum[...] = jnp.zeros_like(value_sum)
            bias_sum[...] = jnp.zeros_like(bias_sum)

        grad_mixed = own_ref[0].astype(F32) + other_ref[0].astype(F32)
        sigma = jax.nn.sigmoid(gate_ref[0])
        through = grad_mixed * sigma
        upper = through.astype(BF16)
        logit_ref[0] = (through * attended_ref[0] * (1.0 - sigma)).astype(BF16)
        q = q_ref[0]
        weights, products = [], []
        for f in range(folds):
            lines = slice(f * block, (f + 1) * block)
            p = probs_ref[0, lines, :]
            value_sum[:, lines] += dot(upper, p, NT)
            weights.append(p.astype(F32))
            products.append(weights[f] * dot(v_ref[0, lines, :], upper))
        inner = functools.reduce(jnp.add, [jnp.sum(x, axis=0, keepdims=True) for x in products])
        grad_q = jnp.zeros((head, block), F32)
        for f in range(folds):
            lines = slice(f * block, (f + 1) * block)
            part = f // grain
            low = (products[f] - weights[f] * inner).astype(BF16)
            grad_q += dot(k_ref[0, :, lines], low)
            key_sum[:, lines] += dot(q, low, NT)
            bias_sum[part * block : (part + 1) * block, :] += low.astype(F32)
        dq_ref[0] = (grad_q * head**-0.5).astype(BF16)

        @pl.when(step == grain - 1)
        def _():
            dk_ref[0] = key_sum[...].astype(BF16)
            dv_ref[0] = value_sum[...].astype(BF16)
            for b in range(sources):
                lines = slice(place[b] * tiles, (place[b] + 1) * tiles)
                bias_ref[b, 0] = bias_sum[lines, :].astype(BF16)

    by_query = pl.BlockSpec((1, head, block), lambda h, i: (h, 0, i))
    by_head = pl.BlockSpec((1, head, key_tokens), lambda h, i: (h, 0, 0))
    narrow = jax.ShapeDtypeStruct((count, head, tokens), BF16)
    broad = jax.ShapeDtypeStruct((count, head, key_tokens), BF16)
    return call(
        kernel,
        (count, grain),
        [
            by_query,
            by_head,
            pl.BlockSpec((1, key_tokens, head), lambda h, i: (h, 0, 0)),
            by_query,
            by_query,
            pl.BlockSpec((1, key_tokens, block), lambda h, i: (h, 0, i)),
            by_query,
            by_query,
        ],
        [
            by_query,
            by_head,
            by_head,
            by_query,
            pl.BlockSpec((sources, 1, tiles, block), lambda h, i: (0, h, 0, 0)),
        ],
        [narrow, broad, broad, narrow, jax.ShapeDtypeStruct((sources, count, tiles, block), BF16)],
        [
            pltpu.VMEM((head, key_tokens), F32),
            pltpu.VMEM((head, key_tokens), F32),
            pltpu.VMEM((sources * tiles, block), F32),
        ],
        flops=8 * count * tokens * key_tokens * head,
        moved=2 * count * tokens * key_tokens,
    )(queries, keys, value_rows, gate, attended, probs, own, other)


def unpack(team, bundle_ref, mixed_refs, weights, mixed, first):
    groups, _, part, _ = bundle_ref.shape

    @pl.when(first)
    def _():
        for g in range(groups):
            for k in range(3):
                weights[k, g * part : (g + 1) * part, :] = bundle_ref[g, k]

    count, head, _ = mixed_refs[0].shape
    size = count * head
    for d, ref in enumerate(mixed_refs):
        start = pl.multiple_of((team ^ d) * size, size)
        mixed[pl.ds(start, size), :] = ref[...].reshape(size, -1)


def feed_first(team, mixed_chunks, row, member, table, project, bundle, coordinate, block):
    tokens, width = row.shape
    count, head, _ = mixed_chunks[0].shape

    def kernel(team_ref, m0, m1, m2, m3, row_ref, member_ref, table_ref, project_ref, bundle_ref, coord_ref,
               out_ref, weights, mixed):
        unpack(team_ref[0], bundle_ref, (m0, m1, m2, m3), weights, mixed, pl.program_id(0) == 0)
        mods = dot(member_ref[...], table_ref[:, 2 * width :])
        attend_gate, feed_shift = mods[:, :width], mods[:, width : 2 * width]
        feed_scale, feed_gate = mods[:, 2 * width : 3 * width], mods[:, 3 * width :]
        attend_out = dot(mixed[...], project_ref[...], TN)
        after = row_ref[...].astype(F32) + attend_gate * attend_out
        normed, _ = normalize(after)
        hidden = (normed * (1.0 + feed_scale) + feed_shift).astype(BF16)
        gate_pre, lift_pre = dot(hidden, weights[0]), dot(hidden, weights[1])
        inner = (gate_pre * jax.nn.sigmoid(gate_pre) * lift_pre).astype(BF16)
        share = after * (1.0 / TEAM) + feed_gate * dot(inner, weights[2])
        out_ref[...] = dot(coord_ref[...], share.astype(BF16), NT)

    by_token = pl.BlockSpec((block, width), lambda j, *_: (j, 0))
    return call(
        kernel,
        (tokens // block,),
        [pl.BlockSpec((count, head, block), lambda j, *_: (0, 0, j))] * 4
        + [
            by_token,
            pl.BlockSpec((block, member.shape[1]), lambda j, *_: (j, 0)),
            whole(table.shape),
            whole(project.shape),
            whole(bundle.shape),
            whole(coordinate.shape),
        ],
        pl.BlockSpec((8, block), lambda j, *_: (0, j)),
        jax.ShapeDtypeStruct((8, tokens), F32),
        [pltpu.VMEM((3, width, width), BF16), pltpu.VMEM((width, block), BF16)],
        flops=2 * tokens * width * width * 4,
        moved=8 * width * width + 4 * tokens * width,
        prefetch=1,
    )(team, *mixed_chunks, row, member, table, project, bundle, coordinate)


def feed_both(team, mixed_chunks, row, points, recycle, cotangent, member, chains, table, project, bundle, block):
    tokens, width = row.shape
    count, head, _ = mixed_chunks[0].shape
    groups = bundle.shape[0]
    part = width // groups
    rows, grain, tiles, _ = cotangent[0].shape
    last = tokens // block - 1
    size = count * head

    def kernel(team_ref, m0, m1, m2, m3, row_ref, point_ref, recycle_ref, c0, c1, c2, c3, member_ref, chain_ref,
               table_ref, project_ref, bundle_ref,
               out_ref, after_ref, near_ref, far_ref, weight_ref, chain_sum_ref,
               weights, mixed, upstream, sums, turned):
        team = team_ref[0]
        first = pl.program_id(0) == 0
        unpack(team, bundle_ref, (m0, m1, m2, m3), weights, mixed, first)
        assemble(team, (c0, c1, c2, c3), upstream)

        @pl.when(first)
        def _():
            sums[...] = jnp.zeros_like(sums)
            chain_sum_ref[...] = jnp.zeros_like(chain_sum_ref)

        mods = dot(member_ref[...], table_ref[:, 2 * width :])
        attend_gate, feed_shift = mods[:, :width], mods[:, width : 2 * width]
        feed_scale, feed_gate = mods[:, 2 * width : 3 * width], mods[:, 3 * width :]
        attend_out = dot(mixed[...], project_ref[...], TN)
        after = begin_of(row_ref, point_ref, recycle_ref) + attend_gate * attend_out
        normed, inverse = normalize(after)
        hidden = (normed * (1.0 + feed_scale) + feed_shift).astype(BF16)
        gate_pre, lift_pre = dot(hidden, weights[0]), dot(hidden, weights[1])
        sigma = jax.nn.sigmoid(gate_pre)
        silu = gate_pre * sigma
        inner = (silu * lift_pre).astype(BF16)
        branch = dot(inner, weights[2])
        out_ref[...] = (after * (1.0 / TEAM) + feed_gate * branch).astype(BF16)

        chain = chain_ref[...]

        def by_chain(place, grad):
            chain_sum_ref[:, place * width : (place + 1) * width] += dot(chain, grad.astype(BF16))

        g = upstream[...].astype(F32)
        by_chain(3, g * branch)
        grad_branch = (g * feed_gate).astype(BF16)
        sums[0] += dot(inner, grad_branch, TN)
        grad_inner = dot(grad_branch, weights[2], NT)
        grad_gate = (grad_inner * lift_pre * sigma * (1.0 + gate_pre * (1.0 - sigma))).astype(BF16)
        grad_lift = (grad_inner * silu).astype(BF16)
        sums[1] += dot(hidden, grad_gate, TN)
        sums[2] += dot(hidden, grad_lift, TN)
        grad_hidden = dot(grad_gate, weights[0], NT) + dot(grad_lift, weights[1], NT)
        by_chain(1, grad_hidden)
        by_chain(2, grad_hidden * normed)
        grad_after = g * (1.0 / TEAM) + norm_back(grad_hidden * (1.0 + feed_scale), normed, inverse)
        after_ref[...] = grad_after
        by_chain(0, grad_after * attend_out)
        grad_out = (grad_after * attend_gate).astype(BF16)
        sums[3] += dot(mixed[...], grad_out)
        turned[...] = dot(grad_out, project_ref[...], NT).T.astype(BF16)
        for d in range(TEAM):
            start = pl.multiple_of((team ^ d) * size, size)
            piece = turned[pl.ds(start, size), :].reshape(count, head, block)
            (far_ref if d % 2 else near_ref)[d // 2] = piece

        @pl.when(pl.program_id(0) == last)
        def _():
            for k in range(4):
                for n in range(groups):
                    weight_ref[n, k] = sums[k, n * part : (n + 1) * part, :].astype(BF16)

    by_token = pl.BlockSpec((block, width), lambda j, *_: (j, 0))
    by_lane = pl.BlockSpec((8, block), lambda j, *_: (0, j))
    halves = pl.BlockSpec((2, count, head, block), lambda j, *_: (0, 0, 0, j))
    half = jax.ShapeDtypeStruct((2, count, head, tokens), BF16)
    return call(
        kernel,
        (tokens // block,),
        [pl.BlockSpec((count, head, block), lambda j, *_: (0, 0, j))] * 4
        + [by_token, by_lane, whole(recycle.shape)]
        + [pl.BlockSpec((rows, 1, tiles, width), lambda j, *_: (0, j, 0, 0))] * 4
        + [
            pl.BlockSpec((block, member.shape[1]), lambda j, *_: (j, 0)),
            by_lane,
            whole(table.shape),
            whole(project.shape),
            whole(bundle.shape),
        ],
        [by_token, by_token, halves, halves, held((groups, 4, part, width)), held((8, 4 * width))],
        [
            jax.ShapeDtypeStruct((tokens, width), BF16),
            jax.ShapeDtypeStruct((tokens, width), F32),
            half,
            half,
            jax.ShapeDtypeStruct((groups, 4, part, width), BF16),
            jax.ShapeDtypeStruct((8, 4 * width), F32),
        ],
        [
            pltpu.VMEM((3, width, width), BF16),
            pltpu.VMEM((width, block), BF16),
            pltpu.VMEM((block, width), BF16),
            pltpu.VMEM((4, width, width), F32),
            pltpu.VMEM((width, block), BF16),
        ],
        flops=2 * tokens * width * width * 12,
        moved=16 * width * width + 10 * tokens * width,
        prefetch=1,
    )(team, *mixed_chunks, row, points, recycle, *cotangent, member, chains, table, project, bundle)


def finish(hidden, row, points, recycle, grad_after, grads, member, chains, table, weight, groups, block):
    tokens, width = row.shape
    count, head, _ = grads[0].shape
    size = count * head
    part = width // groups
    last = tokens // block - 1

    def kernel(hidden_ref, row_ref, point_ref, recycle_ref, after_ref, q_ref, k_ref, v_ref, gate_ref, member_ref,
               chain_ref, table_ref, weight_ref,
               out_ref, sum_ref, chain_sum_ref, recycle_sum_ref, gate_sum_ref, sums):
        first = pl.program_id(0) == 0

        @pl.when(first)
        def _():
            sums[...] = jnp.zeros_like(sums)
            chain_sum_ref[...] = jnp.zeros_like(chain_sum_ref)
            recycle_sum_ref[...] = jnp.zeros_like(recycle_sum_ref)
            gate_sum_ref[...] = jnp.zeros_like(gate_sum_ref)

        stacked = jnp.concatenate(
            [ref[...].reshape(size, block) for ref in (q_ref, k_ref, v_ref, gate_ref)], axis=0
        ).astype(F32)
        turned = stacked.T
        gate_sum_ref[...] += jnp.sum(turned[:, 3 * size :], axis=0, keepdims=True)
        low = turned.astype(BF16)
        sums[...] += dot(hidden_ref[...], low, TN)
        grad_hidden = dot(low, weight_ref[...], NT)
        mods = dot(member_ref[...], table_ref[:, width : 2 * width])
        normed, inverse = normalize(begin_of(row_ref, point_ref, recycle_ref))
        chain = chain_ref[...]
        chain_sum_ref[:, :width] += dot(chain, grad_hidden.astype(BF16))
        chain_sum_ref[:, width:] += dot(chain, (grad_hidden * normed).astype(BF16))
        grad = after_ref[...] + norm_back(grad_hidden * (1.0 + mods), normed, inverse)
        low_grad = grad.astype(BF16)
        out_ref[...] = low_grad
        recycle_sum_ref[...] += dot(point_ref[...].astype(BF16), low_grad)

        @pl.when(pl.program_id(0) == last)
        def _():
            for n in range(groups):
                sum_ref[n] = sums[n * part : (n + 1) * part, :].astype(BF16)

    by_token = pl.BlockSpec((block, width), lambda j: (j, 0))
    by_lane = pl.BlockSpec((8, block), lambda j: (0, j))
    by_query = pl.BlockSpec((count, head, block), lambda j: (0, 0, j))
    return call(
        kernel,
        (tokens // block,),
        [by_token, by_token, by_lane, whole(recycle.shape), by_token]
        + [by_query] * 4
        + [
            pl.BlockSpec((block, member.shape[1]), lambda j: (j, 0)),
            by_lane,
            whole(table.shape),
            whole(weight.shape),
        ],
        [
            by_token,
            held((groups, part, 4 * size)),
            held((8, 2 * width)),
            held((8, width)),
            held((1, size)),
        ],
        [
            jax.ShapeDtypeStruct((tokens, width), BF16),
            jax.ShapeDtypeStruct((groups, part, 4 * size), BF16),
            jax.ShapeDtypeStruct((8, 2 * width), F32),
            jax.ShapeDtypeStruct((8, width), F32),
            jax.ShapeDtypeStruct((1, size), F32),
        ],
        [pltpu.VMEM((width, 4 * size), F32)],
        flops=4 * tokens * weight.size,
        moved=4 * weight.size + 12 * tokens * width,
    )(hidden, row, points, recycle, grad_after, *grads, member, chains, table, weight)


def per_device(
    residues,
    pair_features,
    chain_lengths,
    time_bins,
    fold_class,
    self_flag,
    time_table,
    class_table,
    modulate,
    offset,
    heads,
    pairing,
    gating,
    gating_bias,
    project,
    widen_gate,
    widen_up,
    narrow,
    coordinate,
    recycle,
    cotangent,
):
    blocks = lax.axis_size("blk")
    planes = lax.axis_size("rows")
    myself = lax.axis_index("blk")
    rows, local, width = residues.shape
    row_len = local * blocks
    grain = row_len // pair_features.shape[1]
    tiles = local // grain
    head_count = pairing.shape[1]
    head = width // head_count
    count = head_count // TEAM
    size = count * head
    span = blocks // rows
    parts = span // TEAM
    groups = blocks // TEAM
    tokens = row_len // parts
    block = tokens // grain
    max_chains = chain_lengths.shape[1]
    my_row = myself // span
    my_part = (myself % span) // TEAM
    team = myself % TEAM
    team_ref = team.astype(jnp.int32).reshape(1)
    place = []
    for b in range(blocks):
        r, u, t = b // span, (b % span) // TEAM, b % TEAM
        place.append((u * rows + r) * TEAM + t)

    row_groups = [[r * span + s for r in range(rows)] for s in range(span)]
    same_team = [[g * TEAM + t for g in range(groups)] for t in range(TEAM)]
    teams = [[g * TEAM + t for t in range(TEAM)] for g in range(groups)]
    part_groups = [
        [r * span + u * TEAM + t for u in range(parts)] for r in range(rows) for t in range(TEAM)
    ]

    def swap(x, k):
        return lax.ppermute(x, "blk", [(b, b ^ k) for b in range(blocks)])

    def team_gather(x):
        far = swap(x, 2)
        return x, swap(x, 1), far, swap(far, 1)

    def group_sum(x):
        k = 1
        while k < span:
            x = x + swap(x, k)
            k *= 2
        return x

    def plane_sum(x):
        if planes == 2:
            return x + lax.ppermute(x, "rows", [(0, 1), (1, 0)])
        return lax.psum(x, "rows")

    def exchange(x, members=None):
        return lax.all_to_all(x, "blk", 0, 0, tiled=True, axis_index_groups=members)

    def to_group(x):
        x = x.reshape(rows, tiles, grain, width).transpose(0, 2, 1, 3)
        return team_gather(exchange(x, row_groups))

    row_chunks = to_group(residues)

    tile_bias = pair_bias(pair_features, pairing)
    bias_out = tile_bias.reshape(rows, TEAM, count, tiles, rows, parts, TEAM * tiles)
    bias_out = bias_out.transpose(0, 5, 1, 2, 3, 4, 6).reshape(blocks, count, tiles, block)
    bias = exchange(bias_out)

    depth = heads.shape[0]
    attend_w = jnp.concatenate(
        [heads.reshape(depth, 3, TEAM, size), gating.reshape(depth, 1, TEAM, size)], axis=1
    )
    attend_w = attend_w.transpose(2, 0, 1, 3).reshape(TEAM, depth, 4 * size)
    attend_w = jnp.broadcast_to(attend_w[None], (groups,) + attend_w.shape)
    attend_w = exchange(attend_w.reshape(blocks, depth, 4 * size)).reshape(width, 4 * size)
    project_full = lax.all_gather(project, "blk", axis=0, tiled=True)
    units = narrow.shape[0]
    widen = jnp.stack([widen_gate, widen_up], axis=0).reshape(2, depth, groups, TEAM, units)
    widen = widen.transpose(3, 0, 1, 2, 4).reshape(TEAM, 2, depth, groups * units)
    widen = exchange(widen, teams).transpose(1, 0, 2, 3).reshape(2, TEAM * depth, groups * units)
    bundle = jnp.concatenate([widen, narrow[None]], axis=0)
    bundle = lax.all_gather(bundle[None], "blk", axis=0, tiled=True, axis_index_groups=same_team)

    hot = lambda ids, n: (ids[:, :, None] == jnp.arange(n, dtype=jnp.int32)).astype(F32)
    time_hot = hot(time_bins, time_table.shape[0])
    class_hot = hot(fold_class, class_table.shape[0])
    condition = jnp.einsum(
        "rcn,nd->rcd", time_hot, time_table.astype(F32), precision=HIGHEST
    ) + jnp.einsum("rcn,nd->rcd", class_hot, class_table.astype(F32), precision=HIGHEST)
    smooth = jax.nn.silu(condition).astype(BF16)
    cond_local = modulate.shape[0]
    my_smooth = lax.dynamic_slice_in_dim(smooth, myself * cond_local, cond_local, axis=2)
    per_chain = jnp.einsum("rcd,dm->rcm", my_smooth, modulate, preferred_element_type=F32)
    per_chain = group_sum(jnp.sum(exchange(per_chain, row_groups), axis=0)) + offset.astype(F32)
    upper = lax.reduce_precision(per_chain, 8, 7)
    table = jnp.concatenate(
        [upper, per_chain - upper, jnp.zeros((16 - 2 * max_chains, per_chain.shape[1]), F32)],
        axis=0,
    ).astype(BF16)

    ends = jnp.cumsum(lax.dynamic_index_in_dim(chain_lengths, my_row, 0, False))
    flags = lax.dynamic_index_in_dim(self_flag, my_row, 0, False)

    def slots(part):
        r = jnp.arange(rows, dtype=jnp.int32)[None, :, None, None]
        t = jnp.arange(TEAM, dtype=jnp.int32)[None, None, :, None]
        j = jnp.arange(grain, dtype=jnp.int32)[:, None, None, None]
        a = jnp.arange(tiles, dtype=jnp.int32)[None, None, None, :]
        return (((r * span + part * TEAM + t) * tiles + a) * grain + j).reshape(tokens)

    def chain_of(places):
        return jnp.sum((places[:, None] >= ends[None, :]).astype(jnp.int32), axis=1)

    q_chain = chain_of(slots(my_part))
    k_chain = chain_of(jnp.concatenate([slots(u) for u in range(parts)]))
    q_lines = jnp.broadcast_to(q_chain[None, :], (8, tokens))
    k_lines = jnp.broadcast_to(k_chain[:, None], (parts * tokens, 128))
    ids = jnp.arange(16, dtype=jnp.int32)
    ids = jnp.where(ids < 2 * max_chains, ids % max_chains, -1)
    member = (q_chain[:, None] == ids[None, :]).astype(BF16)
    chain_hot = q_chain[None, :] == jnp.arange(8, dtype=jnp.int32)[:, None]
    chains = chain_hot.astype(BF16)
    flag_lines = jnp.sum(
        jnp.where(chain_hot[:max_chains], flags.astype(F32)[:, None], 0.0), axis=0, keepdims=True
    )
    gate_bias = lax.dynamic_slice_in_dim(gating_bias, team * size, size).astype(F32)
    gate_bias = jnp.broadcast_to(gate_bias[:, None], (size, 128))
    points_w = jnp.pad(coordinate.T, ((0, 8 - coordinate.shape[1]), (0, 0)))
    recycle_w = jnp.pad(recycle, ((0, 8 - recycle.shape[0]), (0, 0)))

    def all_keys(keys, values):
        if parts == 1:
            return keys, values
        keys = lax.all_gather(keys, "blk", axis=0, axis_index_groups=part_groups)
        values = lax.all_gather(values, "blk", axis=0, axis_index_groups=part_groups)
        keys = keys.transpose(1, 0, 2, 3).reshape(count, parts * tokens, head)
        values = values.transpose(1, 2, 0, 3).reshape(count, head, parts * tokens)
        return keys, values

    row, q_one, _, v_one, key_one, _, gate_one = first_rows(
        team_ref, row_chunks, member, table, attend_w, gate_bias, count, head
    )
    key_one, v_one = all_keys(key_one, v_one)
    (mixed_one,) = attend(q_one, key_one, v_one, gate_one, bias, q_lines, k_lines, place, block, False)
    shares = feed_first(
        team_ref, team_gather(mixed_one), row, member, table, project_full, bundle, points_w, block
    )
    shares = shares + swap(shares, 1)
    shares = shares + swap(shares, 2)
    points = lax.reduce_precision(shares, 8, 7) * flag_lines

    hidden, q_two, k_two, v_two, key_two, value_two, gate_two = second_rows(
        row, points, recycle_w, member, table, attend_w, gate_bias, count, head, block
    )
    key_two, v_all = all_keys(key_two, v_two)
    value_two, k_two = all_keys(value_two, k_two)
    mixed_two, attended, probs = attend(
        q_two, key_two, v_all, gate_two, bias, q_lines, k_lines, place, block, True
    )
    result, grad_after, near, far, feed_grads, chain_feed = feed_both(
        team_ref, team_gather(mixed_two), row, points, recycle_w, to_group(cotangent), member, chains, table,
        project_full, bundle, block,
    )

    halves = (near.astype(F32) + swap(far, 1).astype(F32)).astype(BF16)
    grad_q, grad_k, grad_v, grad_logit, bias_grad = attend_back(
        q_two, k_two, value_two, gate_two, attended, probs, halves[0], swap(halves[1], 2), place, tiles, block
    )
    if parts > 1:
        key_value = jnp.stack([grad_k, grad_v]).reshape(2, count, head, parts, tokens)
        key_value = lax.psum_scatter(
            key_value.transpose(3, 0, 1, 2, 4), "blk", scatter_dimension=0, axis_index_groups=part_groups
        )
        grad_k, grad_v = key_value[0], key_value[1]
    grad_begin, attend_grads, chain_attend, recycle_sum, gate_sum = finish(
        hidden, row, points, recycle_w, grad_after, (grad_q, grad_k, grad_v, grad_logit), member, chains, table,
        attend_w, groups, block,
    )

    bias_grad = exchange(bias_grad).reshape(rows, parts, TEAM, count, tiles, rows, TEAM * tiles)
    bias_grad = bias_grad.transpose(0, 2, 3, 4, 5, 1, 6).reshape(rows, head_count, tiles, parts * block)
    grad_pair, pairing_sum = pair_back(pair_features, pairing, bias_grad)

    def to_owner(x):
        x = x.reshape(grain, rows, TEAM, tiles, width).transpose(2, 1, 0, 3, 4)
        pick = lambda d: lax.dynamic_index_in_dim(x, team ^ d, 0, False)
        mine = jnp.stack([pick(0), pick(2)]).astype(F32)
        mine = mine + swap(jnp.stack([pick(1), pick(3)]), 1).astype(F32)
        total = mine[0] + swap(mine[1].astype(BF16), 2).astype(F32)
        back = exchange(total.astype(BF16), row_groups)
        return back.transpose(0, 2, 1, 3).reshape(rows, local, width)

    layer_out = to_owner(result)
    grad_residues = to_owner(grad_begin)

    def scatter(x):
        return lax.psum_scatter(x, "blk", scatter_dimension=0, axis_index_groups=same_team)

    feed_own = scatter(feed_grads)
    attend_own = scatter(attend_grads)
    by_owner = jnp.concatenate([feed_own[1], feed_own[2], feed_own[3], attend_own], axis=1)
    by_owner = exchange(by_owner.reshape(TEAM, depth, 3 * width + 4 * size), teams)
    wide = by_owner[:, :, : 2 * width].reshape(TEAM, depth, 2, groups, units)
    wide = wide.transpose(2, 1, 3, 0, 4).reshape(2, depth, TEAM * groups * units)
    inner = by_owner[:, :, 3 * width :].reshape(TEAM, depth, 4, size).transpose(1, 2, 0, 3)
    inner = inner.reshape(depth, 4 * width)
    own_project = jnp.sum(by_owner[:, :, 2 * width : 3 * width].astype(F32), axis=0).astype(BF16)
    large = (feed_own[0], wide, inner, own_project)
    if planes == 2:
        both = [lax.ppermute(x, "rows", [(0, 1), (1, 0)]) for x in large]
        large = [x.astype(F32) + y.astype(F32) for x, y in zip(large, both)]
    else:
        large = [lax.psum(x, "rows").astype(F32) for x in large]
    grad_narrow, wide, inner, grad_project = large

    chain_sum = jnp.concatenate([chain_attend, chain_feed], axis=1)[:max_chains]
    chain_sum = group_sum(chain_sum)
    every = exchange(jnp.broadcast_to(chain_sum[None], (rows,) + chain_sum.shape), row_groups)
    grad_modulate = jnp.einsum(
        "rcd,rcm->dm", my_smooth.astype(F32), every, precision=HIGHEST
    )
    grad_smooth = jnp.einsum("rcm,dm->rcd", every, modulate.astype(F32), precision=HIGHEST)
    grad_smooth = lax.dynamic_update_slice_in_dim(
        jnp.zeros(condition.shape, F32), grad_smooth, myself * cond_local, axis=2
    )
    gate_line = lax.dynamic_update_slice_in_dim(
        jnp.zeros((width,), F32), gate_sum[0], team * size, axis=0
    )
    small = jnp.concatenate(
        [
            grad_smooth.reshape(-1),
            pairing_sum[:head_count].reshape(-1),
            gate_line,
            recycle_sum[: recycle.shape[0]].reshape(-1),
        ]
    )
    small = small.reshape(-1, 128)
    k = 1
    while k < blocks:
        small = small + swap(small, k)
        k *= 2
    small = small.reshape(-1)
    ends_at = condition.size
    grad_smooth = small[:ends_at].reshape(condition.shape)
    sigma = jax.nn.sigmoid(condition)
    grad_condition = grad_smooth * sigma * (1.0 + condition * (1.0 - sigma))
    grad_time = jnp.einsum("rcn,rcd->nd", time_hot, grad_condition, precision=HIGHEST)
    grad_class = jnp.einsum("rcn,rcd->nd", class_hot, grad_condition, precision=HIGHEST)
    pieces = [
        grad_modulate,
        grad_time,
        grad_class,
        jnp.sum(every, axis=(0, 1)),
        small[ends_at:],
    ]
    line = jnp.concatenate([x.reshape(-1) for x in pieces])
    line = plane_sum(line.reshape(-1, 128)).reshape(-1)
    found, at = [], 0
    for x in pieces:
        found.append(line[at : at + x.size].reshape(x.shape))
        at += x.size
    grad_modulate, grad_time, grad_class, grad_offset, rest = found
    cut = head_count * pairing.shape[0]
    grad_pairing = rest[:cut].reshape(head_count, pairing.shape[0]).T
    grad_gatebias = rest[cut : cut + width]
    grad_recycle = rest[cut + width :].reshape(recycle.shape)
    return (
        layer_out,
        grad_residues,
        grad_pair,
        grad_time,
        grad_class,
        grad_modulate,
        grad_offset,
        inner[:, : 3 * width],
        grad_pairing,
        inner[:, 3 * width :],
        grad_gatebias,
        grad_project,
        wide[0],
        wide[1],
        grad_narrow,
        grad_recycle,
    )


def solution(mesh):
    in_specs = (
        P("rows", "blk", None),
        P("rows", None, "blk", None),
        P("rows", None),
        P("rows", None),
        P("rows", None),
        P("rows", None),
        P(),
        P(),
        P("blk", None),
        P(),
        P("blk", None),
        P(),
        P("blk", None),
        P(),
        P("blk", None),
        P("blk", None),
        P("blk", None),
        P("blk", None),
        P(),
        P(),
        P("rows", "blk", None),
    )
    out_specs = (
        P("rows", "blk", None),
        P("rows", "blk", None),
        P("rows", None, "blk", None),
        P(),
        P(),
        P("blk", None),
        P(),
        P("blk", None),
        P(),
        P("blk", None),
        P(),
        P("blk", None),
        P("blk", None),
        P("blk", None),
        P("blk", None),
        P(),
    )
    return jax.shard_map(
        per_device, mesh=mesh, in_specs=in_specs, out_specs=out_specs, check_vma=False
    )
```

```python
import functools

import jax
import jax.numpy as jnp
from jax import lax
from jax.experimental import pallas as pl
from jax.experimental.pallas import tpu as pltpu
from jax.sharding import PartitionSpec as P

TEAM = 4
F32, BF16 = jnp.float32, jnp.bfloat16
HIGHEST = lax.Precision.HIGHEST
VMEM_BYTES = 58 * 1024 * 1024


def dot(former, latter, contract=((1,), (0,))):
    return lax.dot_general(former, latter, (contract, ((), ())), preferred_element_type=F32)


NT, TN = ((1,), (1,)), ((0,), (0,))


def normalize(values):
    center = values - jnp.mean(values, axis=-1, keepdims=True)
    inverse = lax.rsqrt(jnp.mean(center * center, axis=-1, keepdims=True) + 1e-06)
    return center * inverse, inverse


def norm_back(grad, normed, inverse):
    first = jnp.mean(grad, axis=-1, keepdims=True)
    second = jnp.mean(grad * normed, axis=-1, keepdims=True)
    return inverse * (grad - first - normed * second)


def call(kernel, grid, ins, outs, out_shape, scratch=(), micros=0, prefetch=0):
    return pl.pallas_call(
        kernel,
        grid_spec=pltpu.PrefetchScalarGridSpec(
            num_scalar_prefetch=prefetch,
            grid=grid,
            in_specs=ins,
            out_specs=outs,
            scratch_shapes=list(scratch),
        ),
        out_shape=out_shape,
        cost_estimate=pl.CostEstimate(flops=micros * 1100000000, bytes_accessed=0, transcendentals=0),
        compiler_params=pltpu.CompilerParams(vmem_limit_bytes=VMEM_BYTES),
    )


def whole(shape):
    return pl.BlockSpec(shape, lambda *_: (0,) * len(shape), pipeline_mode=pl.Buffered(buffer_count=1))


def held(shape):
    return pl.BlockSpec(shape, lambda *_: (0,) * len(shape))


def pair_bias(pair_features, pairing):
    rows, q_tiles, k_tiles, width = pair_features.shape
    heads = pairing.shape[1]
    padded = jnp.pad(pairing, ((0, 0), (0, 128 - heads)))

    def kernel(pair_ref, weight_ref, out_ref, flat, turned):
        flat[...] = dot(pair_ref[0].reshape(q_tiles * k_tiles, width), weight_ref[...])
        for k in range(k_tiles):
            turned[:, k, :] = flat[pl.ds(k, q_tiles, stride=k_tiles), :].T[:heads]
        out_ref[0] = turned[...].astype(BF16)

    return call(
        kernel,
        (rows,),
        [
            pl.BlockSpec((1, q_tiles, k_tiles, width), lambda r: (r, 0, 0, 0)),
            whole((width, 128)),
        ],
        pl.BlockSpec((1, heads, k_tiles, q_tiles), lambda r: (r, 0, 0, 0)),
        jax.ShapeDtypeStruct((rows, heads, k_tiles, q_tiles), BF16),
        [pltpu.VMEM((q_tiles * k_tiles, 128), F32), pltpu.VMEM((heads, k_tiles, q_tiles), F32)],
        micros=9,
    )(pair_features, padded)


def pair_back(pair_features, pairing, grad_bias):
    rows, q_tiles, k_tiles, width = pair_features.shape
    heads = pairing.shape[1]
    padded = jnp.pad(pairing.T, ((0, 128 - heads), (0, 0)))

    def kernel(pair_ref, weight_ref, grad_ref, out_ref, sum_ref, flat):
        @pl.when(pl.program_id(0) == 0)
        def _():
            sum_ref[...] = jnp.zeros_like(sum_ref)

        grads = grad_ref[0].astype(F32)
        blank = jnp.zeros((128 - heads, q_tiles), F32)
        for k in range(k_tiles):
            piece = jnp.concatenate([grads[:, k, :], blank], axis=0)
            flat[pl.ds(k, q_tiles, stride=k_tiles), :] = piece.T
        low = flat[...].astype(BF16)
        out_ref[0] = dot(low, weight_ref[...]).astype(BF16).reshape(q_tiles, k_tiles, width)
        sum_ref[...] += dot(low, pair_ref[0].reshape(q_tiles * k_tiles, width), TN)

    return call(
        kernel,
        (rows,),
        [
            pl.BlockSpec((1, q_tiles, k_tiles, width), lambda r: (r, 0, 0, 0)),
            whole((128, width)),
            pl.BlockSpec((1, heads, k_tiles, q_tiles), lambda r: (r, 0, 0, 0)),
        ],
        [pl.BlockSpec((1, q_tiles, k_tiles, width), lambda r: (r, 0, 0, 0)), held((128, width))],
        [
            jax.ShapeDtypeStruct(pair_features.shape, BF16),
            jax.ShapeDtypeStruct((128, width), F32),
        ],
        [pltpu.VMEM((q_tiles * k_tiles, 128), F32)],
        micros=10,
    )(pair_features, padded, grad_bias)


def assemble(spot, chunks, scratch):
    rows, tiles = chunks[0].shape[0], chunks[0].shape[2]
    team, mine = spot[0], spot[1]
    for d, chunk in enumerate(chunks):
        for r in range(rows):
            source = lax.rem(mine + rows - r, rows)
            start = pl.multiple_of((source * TEAM + (team ^ d)) * tiles, tiles)
            scratch[pl.ds(start, tiles), :] = chunk[r, 0]


def by_owner(spot, kind, tokens, near_ref, far_ref):
    rows, tiles = near_ref.shape[1], near_ref.shape[4]
    for d in range(TEAM):
        for r in range(rows):
            start = (lax.rem(spot[1] + r, rows) * TEAM + (spot[0] ^ d)) * tiles
            piece = tokens[pl.ds(pl.multiple_of(start, tiles), tiles), :]
            (far_ref if d % 2 else near_ref)[d // 2, r, kind, 0] = piece


def project_rows(begin, member, table_ref, weight_ref, bias_ref, outs, hidden_ref, width, head):
    mods = dot(member, table_ref[:, : 2 * width])
    normed, _ = normalize(begin)
    hidden = (normed * (1.0 + mods[:, width:]) + mods[:, :width]).astype(BF16)
    if hidden_ref is not None:
        hidden_ref[...] = hidden
    both = dot(hidden, weight_ref[...])
    part = both.shape[1] // 4
    turned = both.T
    count = part // head
    q_ref, k_ref, v_ref, key_ref, value_ref, gate_ref = outs
    scaled = turned[:part].astype(BF16) * BF16(head**-0.5)
    q_ref[...] = scaled.reshape(count, head, -1)
    k_ref[...] = turned[part : 2 * part].astype(BF16).reshape(count, head, -1)
    v_ref[...] = turned[2 * part : 3 * part].astype(BF16).reshape(count, head, -1)
    for h in range(count):
        key_ref[h] = both[:, part + h * head : part + (h + 1) * head].astype(BF16)
        value_ref[h] = both[:, 2 * part + h * head : 2 * part + (h + 1) * head].astype(BF16)
    gate_ref[...] = (turned[3 * part :] + bias_ref[:, :1]).reshape(count, head, -1)


def qkv_specs(count, head, tokens, block):
    wide = pl.BlockSpec((count, head, block), lambda j, *_: (0, 0, j))
    tall = pl.BlockSpec((count, block, head), lambda j, *_: (0, j, 0))
    shapes = [jax.ShapeDtypeStruct((count, head, tokens), BF16)] * 3
    shapes += [jax.ShapeDtypeStruct((count, tokens, head), BF16)] * 2
    shapes += [jax.ShapeDtypeStruct((count, head, tokens), F32)]
    return [wide, wide, wide, tall, tall, wide], shapes


def first_rows(team, chunks, member, table, weight, gate_bias, count, head):
    rows, grain, tiles, width = chunks[0].shape
    tokens = rows * grain * tiles * TEAM
    block = tokens // grain

    def kernel(team_ref, c0, c1, c2, c3, member_ref, table_ref, weight_ref, bias_ref, row_ref, *rest):
        *outs, scratch = rest
        assemble(team_ref, (c0, c1, c2, c3), scratch)
        row_ref[...] = scratch[...]
        begin = scratch[...].astype(F32)
        project_rows(
            begin, member_ref[...], table_ref, weight_ref, bias_ref, outs, None, width, head
        )

    specs, shapes = qkv_specs(count, head, tokens, block)
    by_token = pl.BlockSpec((block, width), lambda j, *_: (j, 0))
    return call(
        kernel,
        (grain,),
        [pl.BlockSpec((rows, 1, tiles, width), lambda j, *_: (0, j, 0, 0))] * 4
        + [
            pl.BlockSpec((block, member.shape[1]), lambda j, *_: (j, 0)),
            whole(table.shape),
            whole(weight.shape),
            whole(gate_bias.shape),
        ],
        [by_token] + specs,
        [jax.ShapeDtypeStruct((tokens, width), BF16)] + shapes,
        [pltpu.VMEM((block, width), BF16)],
        micros=8,
        prefetch=1,
    )(team, *chunks, member, table, weight, gate_bias)


def begin_of(row_ref, point_ref, recycle_ref):
    return row_ref[...].astype(F32) + dot(point_ref[...].astype(BF16), recycle_ref[...], TN)


def second_rows(row, points, recycle, member, table, weight, gate_bias, count, head, block):
    tokens, width = row.shape

    def kernel(row_ref, point_ref, recycle_ref, member_ref, table_ref, weight_ref, bias_ref, hidden_ref, *outs):
        begin = begin_of(row_ref, point_ref, recycle_ref)
        project_rows(
            begin, member_ref[...], table_ref, weight_ref, bias_ref, outs, hidden_ref, width, head
        )

    specs, shapes = qkv_specs(count, head, tokens, block)
    by_token = pl.BlockSpec((block, width), lambda j: (j, 0))
    return call(
        kernel,
        (tokens // block,),
        [
            by_token,
            pl.BlockSpec((8, block), lambda j: (0, j)),
            whole(recycle.shape),
            pl.BlockSpec((block, member.shape[1]), lambda j: (j, 0)),
            whole(table.shape),
            whole(weight.shape),
            whole(gate_bias.shape),
        ],
        [by_token] + specs,
        [jax.ShapeDtypeStruct((tokens, width), BF16)] + shapes,
        micros=8,
    )(row, points, recycle, member, table, weight, gate_bias)


def attend(queries, keys, values, gate, bias, q_chain, k_chain, place, tiles, block, keep):
    count, head, tokens = queries.shape
    key_tokens = keys.shape[1]
    sources = len(place)
    folds = key_tokens // block
    grain = tokens // block

    def kernel(q_ref, k_ref, v_ref, gate_ref, bias_ref, qc_ref, kc_ref, mixed_ref, *rest):
        if keep:
            attended_ref, probs_ref, spread = rest
        else:
            (spread,) = rest

        @pl.when(pl.program_id(1) == 0)
        def _():
            for b in range(sources):
                spread[place[b] * tiles : (place[b] + 1) * tiles, :] = bias_ref[b, 0].astype(F32)

        q = q_ref[0]
        q_chain = qc_ref[0:1, :]
        scores = []
        for f in range(folds):
            lines = slice(f * block, (f + 1) * block)
            part = f // grain
            s = dot(k_ref[0, lines, :], q) + spread[part * block : (part + 1) * block, :]
            kc = kc_ref[lines, :]
            same = jnp.concatenate([kc] * (block // 128), axis=1) == q_chain
            scores.append(jnp.where(same, s, -1000000000.0))
        top = functools.reduce(jnp.maximum, [jnp.max(s, axis=0, keepdims=True) for s in scores])
        powers = [jnp.exp(s - top) for s in scores]
        total = functools.reduce(jnp.add, [jnp.sum(e, axis=0, keepdims=True) for e in powers])
        share = 1.0 / total
        attended = jnp.zeros((head, block), F32)
        for f in range(folds):
            lines = slice(f * block, (f + 1) * block)
            probs = (powers[f] * share).astype(BF16)
            if keep:
                probs_ref[0, lines, :] = probs
            attended += dot(v_ref[0, :, lines], probs)
        mixed_ref[0] = (attended * jax.nn.sigmoid(gate_ref[0])).astype(BF16)
        if keep:
            attended_ref[0] = attended

    by_query = pl.BlockSpec((1, head, block), lambda h, i: (h, 0, i))
    outs = [by_query]
    shapes = [jax.ShapeDtypeStruct((count, head, tokens), BF16)]
    if keep:
        outs += [by_query, pl.BlockSpec((1, key_tokens, block), lambda h, i: (h, 0, i))]
        shapes += [
            jax.ShapeDtypeStruct((count, head, tokens), F32),
            jax.ShapeDtypeStruct((count, key_tokens, tokens), BF16),
        ]
    return call(
        kernel,
        (count, grain),
        [
            by_query,
            pl.BlockSpec((1, key_tokens, head), lambda h, i: (h, 0, 0)),
            pl.BlockSpec((1, head, key_tokens), lambda h, i: (h, 0, 0)),
            by_query,
            pl.BlockSpec((sources, 1, tiles, block), lambda h, i: (0, h, 0, 0)),
            pl.BlockSpec((8, block), lambda h, i: (0, i)),
            whole(k_chain.shape),
        ],
        outs,
        shapes,
        [pltpu.VMEM((sources * tiles, block), F32)],
        micros=13,
    )(queries, keys, values, gate, bias, q_chain, k_chain)


def attend_back(queries, keys, value_rows, gate, attended, probs, own, other, place, tiles, block):
    count, head, tokens = queries.shape
    key_tokens = value_rows.shape[1]
    folds, grain = key_tokens // block, tokens // block
    sources = len(place)

    def kernel(
        q_ref, k_ref, v_ref, gate_ref, attended_ref, probs_ref, own_ref, other_ref,
        dq_ref, dk_ref, dv_ref, logit_ref, bias_ref, key_sum, value_sum, bias_sum,
    ):
        step = pl.program_id(1)

        @pl.when(step == 0)
        def _():
            key_sum[...] = jnp.zeros_like(key_sum)
            value_sum[...] = jnp.zeros_like(value_sum)
            bias_sum[...] = jnp.zeros_like(bias_sum)

        grad_mixed = own_ref[0].astype(F32) + other_ref[0].astype(F32)
        sigma = jax.nn.sigmoid(gate_ref[0])
        through = grad_mixed * sigma
        upper = through.astype(BF16)
        logit_ref[0] = (through * attended_ref[0] * (1.0 - sigma)).astype(BF16)
        q = q_ref[0]
        weights, products = [], []
        for f in range(folds):
            lines = slice(f * block, (f + 1) * block)
            p = probs_ref[0, lines, :]
            value_sum[:, lines] += dot(upper, p, NT)
            weights.append(p.astype(F32))
            products.append(weights[f] * dot(v_ref[0, lines, :], upper))
        inner = functools.reduce(jnp.add, [jnp.sum(x, axis=0, keepdims=True) for x in products])
        grad_q = jnp.zeros((head, block), F32)
        for f in range(folds):
            lines = slice(f * block, (f + 1) * block)
            part = f // grain
            low = (products[f] - weights[f] * inner).astype(BF16)
            grad_q += dot(k_ref[0, :, lines], low)
            key_sum[:, lines] += dot(q, low, NT)
            bias_sum[part * block : (part + 1) * block, :] += low.astype(F32)
        dq_ref[0] = (grad_q * head**-0.5).astype(BF16)

        @pl.when(step == grain - 1)
        def _():
            dk_ref[0] = key_sum[...].astype(BF16)
            dv_ref[0] = value_sum[...].astype(BF16)
            for b in range(sources):
                lines = slice(place[b] * tiles, (place[b] + 1) * tiles)
                bias_ref[b, 0] = bias_sum[lines, :].astype(BF16)

    by_query = pl.BlockSpec((1, head, block), lambda h, i: (h, 0, i))
    by_head = pl.BlockSpec((1, head, key_tokens), lambda h, i: (h, 0, 0))
    narrow = jax.ShapeDtypeStruct((count, head, tokens), BF16)
    broad = jax.ShapeDtypeStruct((count, head, key_tokens), BF16)
    return call(
        kernel,
        (count, grain),
        [
            by_query,
            by_head,
            pl.BlockSpec((1, key_tokens, head), lambda h, i: (h, 0, 0)),
            by_query,
            by_query,
            pl.BlockSpec((1, key_tokens, block), lambda h, i: (h, 0, i)),
            by_query,
            by_query,
        ],
        [
            by_query,
            by_head,
            by_head,
            by_query,
            pl.BlockSpec((sources, 1, tiles, block), lambda h, i: (0, h, 0, 0)),
        ],
        [narrow, broad, broad, narrow, jax.ShapeDtypeStruct((sources, count, tiles, block), BF16)],
        [
            pltpu.VMEM((head, key_tokens), F32),
            pltpu.VMEM((head, key_tokens), F32),
            pltpu.VMEM((sources * tiles, block), F32),
        ],
        micros=15,
    )(queries, keys, value_rows, gate, attended, probs, own, other)


def unpack(spot, bundle_refs, mixed_refs, weights, mixed, first):
    near, tail, *far = bundle_refs
    groups, _, part, wide = near.shape

    @pl.when(first)
    def _():
        mine = pl.multiple_of(spot[2] * wide, wide)
        other = pl.multiple_of((1 - spot[2]) * wide, wide)
        for g in range(groups):
            lines = slice(g * part, (g + 1) * part)
            for k in range(2):
                weights[k, lines, pl.ds(mine, wide)] = near[g, k]
                if far:
                    weights[k, lines, pl.ds(other, wide)] = far[0][g, k]
            weights[2, lines, pl.ds(mine, wide)] = tail[g, :, :wide]
            if far:
                weights[2, lines, pl.ds(other, wide)] = far[1][g]
            weights[3, lines, :] = tail[g, :, wide:]

    count, head, _ = mixed_refs[0].shape
    size = count * head
    for d, ref in enumerate(mixed_refs):
        start = pl.multiple_of((spot[0] ^ d) * size, size)
        mixed[pl.ds(start, size), :] = ref[...].reshape(size, -1)


def feed_first(team, mixed_chunks, row, member, table, bundle, coordinate, block):
    tokens, width = row.shape
    count, head, _ = mixed_chunks[0].shape

    def kernel(team_ref, m0, m1, m2, m3, row_ref, member_ref, table_ref, coord_ref, *rest):
        *bundle_refs, out_ref, weights, mixed = rest
        unpack(team_ref, bundle_refs, (m0, m1, m2, m3), weights, mixed, pl.program_id(0) == 0)
        mods = dot(member_ref[...], table_ref[:, 2 * width :])
        attend_gate, feed_shift = mods[:, :width], mods[:, width : 2 * width]
        feed_scale, feed_gate = mods[:, 2 * width : 3 * width], mods[:, 3 * width :]
        attend_out = dot(mixed[...], weights[0], TN)
        after = row_ref[...].astype(F32) + attend_gate * attend_out
        normed, _ = normalize(after)
        hidden = (normed * (1.0 + feed_scale) + feed_shift).astype(BF16)
        gate_pre, lift_pre = dot(hidden, weights[1]), dot(hidden, weights[2])
        inner = (gate_pre * jax.nn.sigmoid(gate_pre) * lift_pre).astype(BF16)
        share = after * (1.0 / TEAM) + feed_gate * dot(inner, weights[3])
        out_ref[...] = dot(coord_ref[...], share.astype(BF16), NT)

    by_token = pl.BlockSpec((block, width), lambda j, *_: (j, 0))
    return call(
        kernel,
        (tokens // block,),
        [pl.BlockSpec((count, head, block), lambda j, *_: (0, 0, j))] * 4
        + [
            by_token,
            pl.BlockSpec((block, member.shape[1]), lambda j, *_: (j, 0)),
            whole(table.shape),
            whole(coordinate.shape),
        ]
        + [whole(x.shape) for x in bundle],
        pl.BlockSpec((8, block), lambda j, *_: (0, j)),
        jax.ShapeDtypeStruct((8, tokens), F32),
        [pltpu.VMEM((4, width, width), BF16), pltpu.VMEM((width, block), BF16)],
        micros=14,
        prefetch=1,
    )(team, *mixed_chunks, row, member, table, coordinate, *bundle)


def feed_both(team, mixed_chunks, row, points, recycle, cotangent, member, chains, table, bundle, block):
    tokens, width = row.shape
    count, head, _ = mixed_chunks[0].shape
    groups = bundle[0].shape[0]
    part = width // groups
    wide = bundle[0].shape[3]
    sides = width // wide
    rows, grain, tiles, _ = cotangent[0].shape
    last = tokens // block - 1
    size = count * head

    def kernel(team_ref, m0, m1, m2, m3, row_ref, point_ref, recycle_ref, c0, c1, c2, c3, member_ref, chain_ref,
               table_ref, *rest):
        bundle_refs, rest = rest[: len(bundle)], rest[len(bundle) :]
        share_ref, after_ref, near_ref, far_ref, chain_sum_ref, down_ref = rest[:6]
        grad_refs, (weights, mixed, upstream, sums, turned) = rest[6:-5], rest[-5:]
        team = team_ref[0]
        first = pl.program_id(0) == 0
        unpack(team_ref, bundle_refs, (m0, m1, m2, m3), weights, mixed, first)
        assemble(team_ref, (c0, c1, c2, c3), upstream)

        @pl.when(first)
        def _():
            sums[...] = jnp.zeros_like(sums)
            chain_sum_ref[...] = jnp.zeros_like(chain_sum_ref)

        mods = dot(member_ref[...], table_ref[:, 2 * width :])
        attend_gate, feed_shift = mods[:, :width], mods[:, width : 2 * width]
        feed_scale, feed_gate = mods[:, 2 * width : 3 * width], mods[:, 3 * width :]
        attend_out = dot(mixed[...], weights[0], TN)
        after = begin_of(row_ref, point_ref, recycle_ref) + attend_gate * attend_out
        normed, inverse = normalize(after)
        hidden = (normed * (1.0 + feed_scale) + feed_shift).astype(BF16)
        gate_pre, lift_pre = dot(hidden, weights[1]), dot(hidden, weights[2])
        sigma = jax.nn.sigmoid(gate_pre)
        silu = gate_pre * sigma
        inner = (silu * lift_pre).astype(BF16)
        branch = dot(inner, weights[3])

        chain = chain_ref[...]

        def by_chain(place, grad):
            chain_sum_ref[:, place * width : (place + 1) * width] += dot(chain, grad.astype(BF16))

        g = upstream[...].astype(F32)
        share_ref[...] = (after * (1.0 / TEAM) + feed_gate * branch).astype(BF16)
        by_chain(3, g * branch)
        grad_branch = (g * feed_gate).astype(BF16)
        sums[0] += dot(inner, grad_branch, TN)
        grad_inner = dot(grad_branch, weights[3], NT)
        grad_gate = (grad_inner * lift_pre * sigma * (1.0 + gate_pre * (1.0 - sigma))).astype(BF16)
        grad_lift = (grad_inner * silu).astype(BF16)
        sums[1] += dot(hidden, grad_gate, TN)
        sums[2] += dot(hidden, grad_lift, TN)
        grad_hidden = dot(grad_gate, weights[1], NT) + dot(grad_lift, weights[2], NT)
        by_chain(1, grad_hidden)
        by_chain(2, grad_hidden * normed)
        grad_after = g * (1.0 / TEAM) + norm_back(grad_hidden * (1.0 + feed_scale), normed, inverse)
        after_ref[...] = grad_after
        by_chain(0, grad_after * attend_out)
        grad_out = (grad_after * attend_gate).astype(BF16)
        sums[3] += dot(mixed[...], grad_out)
        turned[...] = dot(grad_out, weights[0], NT).T.astype(BF16)
        for d in range(TEAM):
            start = pl.multiple_of((team ^ d) * size, size)
            piece = turned[pl.ds(start, size), :].reshape(count, head, block)
            (far_ref if d % 2 else near_ref)[d // 2] = piece

        @pl.when(pl.program_id(0) == last)
        def _():
            for g in range(groups):
                lines = slice(g * part, (g + 1) * part)
                down_ref[g] = sums[0, lines, :].astype(BF16)
                for side, ref in enumerate(grad_refs):
                    start = pl.multiple_of((team_ref[2] ^ side) * wide, wide)
                    for k in range(3):
                        ref[g, k] = sums[1 + k, lines, pl.ds(start, wide)].astype(BF16)

    by_token = pl.BlockSpec((block, width), lambda j, *_: (j, 0))
    by_lane = pl.BlockSpec((8, block), lambda j, *_: (0, j))
    halves = pl.BlockSpec((2, count, head, block), lambda j, *_: (0, 0, 0, j))
    half = jax.ShapeDtypeStruct((2, count, head, tokens), BF16)
    return call(
        kernel,
        (tokens // block,),
        [pl.BlockSpec((count, head, block), lambda j, *_: (0, 0, j))] * 4
        + [by_token, by_lane, whole(recycle.shape)]
        + [pl.BlockSpec((rows, 1, tiles, width), lambda j, *_: (0, j, 0, 0))] * 4
        + [
            pl.BlockSpec((block, member.shape[1]), lambda j, *_: (j, 0)),
            by_lane,
            whole(table.shape),
        ]
        + [whole(x.shape) for x in bundle],
        [by_token, by_token, halves, halves, held((8, 4 * width)), held((groups, part, width))]
        + [held((groups, 3, part, wide))] * sides,
        [
            jax.ShapeDtypeStruct((tokens, width), BF16),
            jax.ShapeDtypeStruct((tokens, width), F32),
            half,
            half,
            jax.ShapeDtypeStruct((8, 4 * width), F32),
            jax.ShapeDtypeStruct((groups, part, width), BF16),
        ]
        + [jax.ShapeDtypeStruct((groups, 3, part, wide), BF16)] * sides,
        [
            pltpu.VMEM((4, width, width), BF16),
            pltpu.VMEM((width, block), BF16),
            pltpu.VMEM((block, width), BF16),
            pltpu.VMEM((4, width, width), F32),
            pltpu.VMEM((width, block), BF16),
        ],
        micros=33,
        prefetch=1,
    )(team, *mixed_chunks, row, points, recycle, *cotangent, member, chains, table, *bundle)


def finish(spot, share, hidden, row, points, recycle, grad_after, grads, member, chains, table, weight, rows, tiles, groups, sides, block):
    tokens, width = row.shape
    count, head, _ = grads[0].shape
    size = count * head
    part = width // groups
    wide = 4 * size // sides
    last = tokens // block - 1

    def kernel(spot_ref, share_ref, hidden_ref, row_ref, point_ref, recycle_ref, after_ref, q_ref, k_ref, v_ref, gate_ref,
               member_ref, chain_ref, table_ref, weight_ref,
               near_ref, far_ref, chain_sum_ref, recycle_sum_ref, gate_sum_ref, *rest):
        *sum_refs, sums, owners = rest
        first = pl.program_id(0) == 0

        @pl.when(first)
        def _():
            sums[...] = jnp.zeros_like(sums)
            chain_sum_ref[...] = jnp.zeros_like(chain_sum_ref)
            recycle_sum_ref[...] = jnp.zeros_like(recycle_sum_ref)
            gate_sum_ref[...] = jnp.zeros_like(gate_sum_ref)

        stacked = jnp.concatenate(
            [ref[...].reshape(size, block) for ref in (q_ref, k_ref, v_ref, gate_ref)], axis=0
        ).astype(F32)
        turned = stacked.T
        gate_sum_ref[...] += jnp.sum(turned[:, 3 * size :], axis=0, keepdims=True)
        low = turned.astype(BF16)
        sums[...] += dot(hidden_ref[...], low, TN)
        grad_hidden = dot(low, weight_ref[...], NT)
        mods = dot(member_ref[...], table_ref[:, width : 2 * width])
        normed, inverse = normalize(begin_of(row_ref, point_ref, recycle_ref))
        chain = chain_ref[...]
        chain_sum_ref[:, :width] += dot(chain, grad_hidden.astype(BF16))
        chain_sum_ref[:, width:] += dot(chain, (grad_hidden * normed).astype(BF16))
        grad = after_ref[...] + norm_back(grad_hidden * (1.0 + mods), normed, inverse)
        low_grad = grad.astype(BF16)
        owners[...] = low_grad
        by_owner(spot_ref, 0, share_ref, near_ref, far_ref)
        by_owner(spot_ref, 1, owners, near_ref, far_ref)
        recycle_sum_ref[...] += dot(point_ref[...].astype(BF16), low_grad)

        @pl.when(pl.program_id(0) == last)
        def _():
            for side, ref in enumerate(sum_refs):
                start = pl.multiple_of((spot_ref[2] ^ side) * wide, wide)
                for g in range(groups):
                    ref[g] = sums[g * part : (g + 1) * part, pl.ds(start, wide)].astype(BF16)

    by_token = pl.BlockSpec((block, width), lambda j, *_: (j, 0))
    by_lane = pl.BlockSpec((8, block), lambda j, *_: (0, j))
    by_query = pl.BlockSpec((count, head, block), lambda j, *_: (0, 0, j))
    owned = pl.BlockSpec((2, rows, 2, 1, tiles, width), lambda j, *_: (0, 0, 0, j, 0, 0))
    return call(
        kernel,
        (tokens // block,),
        [by_token, by_token, by_token, by_lane, whole(recycle.shape), by_token]
        + [by_query] * 4
        + [
            pl.BlockSpec((block, member.shape[1]), lambda j, *_: (j, 0)),
            by_lane,
            whole(table.shape),
            whole(weight.shape),
        ],
        [
            owned,
            owned,
            held((8, 2 * width)),
            held((8, width)),
            held((1, size)),
        ]
        + [held((groups, part, wide))] * sides,
        [
            jax.ShapeDtypeStruct((2, rows, 2, tokens // block, tiles, width), BF16),
            jax.ShapeDtypeStruct((2, rows, 2, tokens // block, tiles, width), BF16),
            jax.ShapeDtypeStruct((8, 2 * width), F32),
            jax.ShapeDtypeStruct((8, width), F32),
            jax.ShapeDtypeStruct((1, size), F32),
        ]
        + [jax.ShapeDtypeStruct((groups, part, wide), BF16)] * sides,
        [pltpu.VMEM((width, 4 * size), F32), pltpu.VMEM((block, width), BF16)],
        micros=12,
        prefetch=1,
    )(spot, share, hidden, row, points, recycle, grad_after, *grads, member, chains, table, weight)


def per_device(
    residues,
    pair_features,
    chain_lengths,
    time_bins,
    fold_class,
    self_flag,
    time_table,
    class_table,
    modulate,
    offset,
    heads,
    pairing,
    gating,
    gating_bias,
    project,
    widen_gate,
    widen_up,
    narrow,
    coordinate,
    recycle,
    cotangent,
):
    blocks = lax.axis_size("blk")
    planes = lax.axis_size("rows")
    myself = lax.axis_index("blk")
    rows, local, width = residues.shape
    row_len = local * blocks
    grain = row_len // pair_features.shape[1]
    tiles = local // grain
    head_count = pairing.shape[1]
    head = width // head_count
    count = head_count // TEAM
    size = count * head
    span = blocks // rows
    parts = span // TEAM
    groups = blocks // TEAM
    tokens = row_len // parts
    block = tokens // grain
    max_chains = chain_lengths.shape[1]
    my_row = myself // span
    my_part = (myself % span) // TEAM
    team = myself % TEAM
    sides = 2 if planes % 2 == 0 else 1
    my_side = lax.axis_index("rows") % sides
    team_ref = jnp.stack([team, my_row, my_side]).astype(jnp.int32)
    place = []
    for b in range(blocks):
        r, u, t = b // span, (b % span) // TEAM, b % TEAM
        place.append((u * rows + r) * TEAM + t)

    row_groups = [[r * span + s for r in range(rows)] for s in range(span)]
    same_team = [[g * TEAM + t for g in range(groups)] for t in range(TEAM)]
    teams = [[g * TEAM + t for t in range(TEAM)] for g in range(groups)]
    part_groups = [
        [r * span + u * TEAM + t for u in range(parts)] for r in range(rows) for t in range(TEAM)
    ]

    def swap(x, k):
        return lax.ppermute(x, "blk", [(b, b ^ k) for b in range(blocks)])

    def team_gather(x):
        far = swap(x, 2)
        return x, swap(x, 1), far, swap(far, 1)

    def group_sum(x):
        k = 1
        while k < span:
            x = x + swap(x, k)
            k *= 2
        return x

    def exchange(x, members=None):
        return lax.all_to_all(x, "blk", 0, 0, tiled=True, axis_index_groups=members)

    def pick(x, d):
        return lax.dynamic_index_in_dim(x, team ^ d, 0, False)

    def ordered(x):
        x = list(x)
        for bit in (1, 2):
            moved = (team & bit) != 0
            x = [jnp.where(moved, x[d ^ bit], x[d]) for d in range(TEAM)]
        return x

    def across(x):
        return lax.ppermute(x, "rows", [(p, p ^ 1) for p in range(planes)])

    def my_half(x, axis, other=0):
        wide = x.shape[axis] // sides
        return lax.dynamic_slice_in_dim(x, (my_side ^ other) * wide, wide, axis)

    def unite(x, axis):
        if sides == 1:
            return x
        y = across(x)
        return jnp.concatenate([jnp.where(my_side == 0, x, y), jnp.where(my_side == 0, y, x)], axis)

    def add_planes(x):
        if planes > 2:
            x = lax.psum(x, "rows", axis_index_groups=[list(range(p, planes, 2)) for p in range(2)])
        return x

    def pair_sum(x):
        if sides == 1:
            return x[0]
        return (x[0].astype(F32) + across(x[1]).astype(F32)).astype(BF16)

    def scatter(x):
        x = lax.psum_scatter(
            x, "blk", scatter_dimension=0, axis_index_groups=same_team, tiled=True
        )
        return add_planes(x)

    def after(x, *others):
        return lax.optimization_barrier((x, *others))[0]

    def by_group(found):
        turned = [found[-d % groups] for d in range(groups)]
        turned = jnp.stack(turned + turned)
        return lax.dynamic_slice_in_dim(turned, (groups - myself // TEAM) % groups, groups)

    def row_shift(x):
        found = [lax.dynamic_index_in_dim(x, my_row, 0, False)]
        for d in range(1, rows):
            piece = lax.dynamic_index_in_dim(x, (my_row + d) % rows, 0, False)
            pairs = [(b, (b + d * span) % blocks) for b in range(blocks)]
            found.append(lax.ppermute(piece, "blk", pairs))
        return found

    def by_row(found):
        turned = [found[-d % rows] for d in range(rows)]
        return lax.dynamic_slice_in_dim(jnp.stack(turned + turned), (rows - my_row) % rows, rows)

    def fold(x):
        return x.reshape(rows, tiles, grain, width).transpose(0, 2, 1, 3)

    depth = heads.shape[0]
    attend_w = jnp.concatenate(
        [heads.reshape(depth, 3, TEAM, size), gating.reshape(depth, 1, TEAM, size)], axis=1
    )
    attend_w = my_half(attend_w.transpose(2, 0, 1, 3).reshape(TEAM, depth, 4 * size), 1)
    attend_w = jnp.broadcast_to(attend_w[None], (groups,) + attend_w.shape)
    attend_w = exchange(attend_w.reshape(blocks, depth // sides, 4 * size))

    units = narrow.shape[0]
    widen = jnp.stack([widen_gate, widen_up], axis=0).reshape(2, depth, groups, TEAM, units)
    widen = my_half(widen, 2).transpose(3, 0, 1, 2, 4).reshape(TEAM, 2, depth, width // sides)
    out_w = my_half(project, 1)[None]
    widen = [pick(widen, d) for d in range(TEAM)]
    widen = [widen[0]] + [swap(widen[d], d) for d in range(1, TEAM)]
    widen = jnp.stack(ordered(widen), axis=1).reshape(2, TEAM * depth, width // sides)
    out_w = jnp.stack(ordered(team_gather(out_w)), axis=1).reshape(1, TEAM * depth, width // sides)
    def gather(x):
        return lax.all_gather(x, "blk", axis=0, axis_index_groups=same_team)

    first_bundle = jnp.concatenate([out_w, widen[:1]], axis=0)
    bundle = [gather(first_bundle)]
    bundle.append(gather(jnp.concatenate([widen[1], narrow], axis=1)))
    if sides == 2:
        bundle += [across(bundle[0]), across(bundle[1][:, :, : width // sides])]

    hot = lambda ids, n: (ids[:, :, None] == jnp.arange(n, dtype=jnp.int32)).astype(F32)
    ids = jnp.concatenate([time_bins, fold_class], axis=1)
    if planes == 2:
        ids = jnp.concatenate([ids, across(ids)], axis=0)
    time_hot = hot(ids[:, :max_chains], time_table.shape[0])
    class_hot = hot(ids[:, max_chains:], class_table.shape[0])
    condition = jnp.einsum(
        "rcn,nd->rcd", time_hot, time_table.astype(F32), precision=HIGHEST
    ) + jnp.einsum("rcn,nd->rcd", class_hot, class_table.astype(F32), precision=HIGHEST)
    smooth = jax.nn.silu(condition).astype(BF16)
    cond_local = modulate.shape[0]
    my_smooth = lax.dynamic_slice_in_dim(smooth, myself * cond_local, cond_local, axis=2)
    per_chain = jnp.einsum("rcd,dm->rcm", my_smooth[:rows], modulate, preferred_element_type=F32)
    upper = lax.reduce_precision(per_chain, 8, 7)
    both = jnp.stack([upper, per_chain - upper], axis=1).astype(BF16).reshape(rows, -1, width)
    moved = jnp.stack(row_shift(jnp.concatenate([fold(residues).reshape(rows, local, width), both], axis=1)))
    row_chunks = team_gather(moved[:, :local].reshape(rows, grain, tiles, width))
    per_chain = moved[:, local:].reshape(2 * rows, max_chains, 6 * width).astype(F32)
    per_chain = group_sum(jnp.sum(per_chain, axis=0)) + offset.astype(F32)
    upper = lax.reduce_precision(per_chain, 8, 7)
    table = jnp.concatenate(
        [upper, per_chain - upper, jnp.zeros((16 - 2 * max_chains, per_chain.shape[1]), F32)],
        axis=0,
    ).astype(BF16)

    tile_bias = pair_bias(pair_features, after(pairing, first_bundle))
    bias_out = tile_bias.reshape(rows, TEAM, count, tiles, rows, parts, TEAM * tiles)
    bias_out = bias_out.transpose(0, 5, 1, 2, 3, 4, 6).reshape(blocks, count, tiles, block)
    attend_w = unite(attend_w, 1).reshape(width, 4 * size)
    bias = exchange(after(bias_out, attend_w))

    ends = jnp.cumsum(lax.dynamic_index_in_dim(chain_lengths, my_row, 0, False))
    flags = lax.dynamic_index_in_dim(self_flag, my_row, 0, False)

    def slots(part):
        r = jnp.arange(rows, dtype=jnp.int32)[None, :, None, None]
        t = jnp.arange(TEAM, dtype=jnp.int32)[None, None, :, None]
        j = jnp.arange(grain, dtype=jnp.int32)[:, None, None, None]
        a = jnp.arange(tiles, dtype=jnp.int32)[None, None, None, :]
        return (((r * span + part * TEAM + t) * tiles + a) * grain + j).reshape(tokens)

    def chain_of(places):
        return jnp.sum((places[:, None] >= ends[None, :]).astype(jnp.int32), axis=1)

    q_chain = chain_of(slots(my_part))
    k_chain = chain_of(jnp.concatenate([slots(u) for u in range(parts)]))
    q_lines = jnp.broadcast_to(q_chain[None, :], (8, tokens))
    k_lines = jnp.broadcast_to(k_chain[:, None], (parts * tokens, 128))
    ids = jnp.arange(16, dtype=jnp.int32)
    ids = jnp.where(ids < 2 * max_chains, ids % max_chains, -1)
    member = (q_chain[:, None] == ids[None, :]).astype(BF16)
    chain_hot = q_chain[None, :] == jnp.arange(8, dtype=jnp.int32)[:, None]
    chains = chain_hot.astype(BF16)
    flag_lines = jnp.sum(
        jnp.where(chain_hot[:max_chains], flags.astype(F32)[:, None], 0.0), axis=0, keepdims=True
    )
    gate_bias = lax.dynamic_slice_in_dim(gating_bias, team * size, size).astype(F32)
    gate_bias = jnp.broadcast_to(gate_bias[:, None], (size, 128))
    points_w = jnp.pad(coordinate.T, ((0, 8 - coordinate.shape[1]), (0, 0)))
    recycle_w = jnp.pad(recycle, ((0, 8 - recycle.shape[0]), (0, 0)))

    def all_keys(keys, values):
        if parts == 1:
            return keys, values
        keys = lax.all_gather(keys, "blk", axis=0, axis_index_groups=part_groups)
        values = lax.all_gather(values, "blk", axis=0, axis_index_groups=part_groups)
        keys = keys.transpose(1, 0, 2, 3).reshape(count, parts * tokens, head)
        values = values.transpose(1, 2, 0, 3).reshape(count, head, parts * tokens)
        return keys, values

    row, q_one, _, v_one, key_one, _, gate_one = first_rows(
        team_ref, row_chunks, member, table, attend_w, gate_bias, count, head
    )
    key_one, v_one = all_keys(key_one, v_one)
    upstream = jnp.stack(row_shift(fold(after(cotangent, row))))
    q_lines_one = after(q_lines, bundle[-sides])
    (mixed_one,) = attend(q_one, key_one, v_one, gate_one, bias, q_lines_one, k_lines, place, tiles, block, False)
    mixed_one = team_gather(after(mixed_one, bundle[1]))
    shares = feed_first(
        team_ref, mixed_one, row, member, table, bundle, points_w, block
    )
    shares = shares + swap(shares, 1)
    shares = shares + swap(shares, 2)
    points = lax.reduce_precision(shares, 8, 7) * flag_lines

    modulate_full = lax.all_gather(after(modulate, row), "blk", axis=0, tiled=True)
    hidden, q_two, k_two, v_two, key_two, value_two, gate_two = second_rows(
        row, points, after(recycle_w, modulate_full, upstream), member, table, attend_w, gate_bias, count, head, block
    )
    key_two, v_all = all_keys(key_two, v_two)
    value_two, k_two = all_keys(value_two, k_two)
    mixed_two, attended, probs = attend(
        q_two, key_two, v_all, gate_two, bias, q_lines, k_lines, place, tiles, block, True
    )
    far = swap(after(upstream, points), 2)
    upstream = upstream, swap(upstream, 1), far, swap(after(far, q_two), 1)
    result, grad_after, near, far, chain_feed, down_grads, *feed_grads = feed_both(
        team_ref, team_gather(after(mixed_two, upstream[3])), row, points, recycle_w, upstream, member, chains, table,
        bundle, block,
    )

    def near_sum(near, far):
        return (near.astype(F32) + swap(far, 1).astype(F32)).astype(BF16)

    def team_total(both):
        return (both[0].astype(F32) + swap(both[1], 2).astype(F32)).astype(BF16)

    def to_owner(total):
        found = [total[0]]
        for d in range(1, rows):
            pairs = [(b, (b + d * span) % blocks) for b in range(blocks)]
            found.append(lax.ppermute(total[d], "blk", pairs))
        found = by_row(found).transpose(1, 0, 3, 2, 4)
        return found.reshape(2, rows, local, width)

    halves = (near.astype(F32) + swap(far, 1).astype(F32)).astype(BF16)
    other_half = swap(halves[1], 2)
    grad_q, grad_k, grad_v, grad_logit, bias_grad = attend_back(
        q_two, k_two, value_two, gate_two, attended, probs, halves[0], other_half, place, tiles, block
    )
    bias_grad = exchange(bias_grad)
    if parts > 1:
        key_value = jnp.stack([grad_k, grad_v]).reshape(2, count, head, parts, tokens)
        key_value = lax.psum_scatter(
            key_value.transpose(3, 0, 1, 2, 4), "blk", scatter_dimension=0, axis_index_groups=part_groups
        )
        grad_k, grad_v = key_value[0], key_value[1]
    feed_grads = pair_sum(feed_grads)
    down_own = scatter(down_grads)[0]
    wide_own = scatter(feed_grads)[0].reshape(3, TEAM, depth, width // sides)
    begin_near, begin_far, chain_attend, recycle_sum, gate_sum, *attend_grads = finish(
        after(team_ref, feed_grads, bias_grad, down_own), result, hidden, row, points, recycle_w, grad_after, (grad_q, grad_k, grad_v, grad_logit), member, chains, table,
        attend_w, rows, tiles, groups, sides, block,
    )

    begin_both = near_sum(begin_near, begin_far)
    layer_out, grad_residues = to_owner(team_total(begin_both))

    bias_grad = bias_grad.reshape(rows, parts, TEAM, count, tiles, rows, TEAM * tiles)
    bias_grad = bias_grad.transpose(0, 2, 3, 4, 5, 1, 6).reshape(rows, head_count, tiles, parts * block)
    grad_pair, pairing_sum = pair_back(pair_features, pairing, after(bias_grad, begin_both))

    if planes == 2:
        grad_narrow = down_own.astype(F32) + across(after(down_own, pairing_sum)).astype(F32)
    else:
        grad_narrow = lax.psum(down_own, "rows").astype(F32)
    attend_grads = pair_sum([after(attend_grads[0], wide_own), *attend_grads[1:]])
    wide = exchange(wide_own.transpose(1, 0, 2, 3), teams)
    attend_own = exchange(after(attend_grads, wide).reshape(blocks, depth, 4 * size // sides))
    inner = jnp.sum(attend_own.astype(F32).reshape(groups, TEAM, depth, 4 // sides, size), axis=0).astype(BF16)
    inner = add_planes(inner).transpose(1, 2, 0, 3).reshape(depth, 4 * width // sides)
    inner = unite(inner, 1).astype(F32)
    own_project = jnp.sum(wide[:, 2].astype(F32), axis=0).astype(BF16)
    wide = wide[:, :2].reshape(TEAM, 2, depth, groups // sides, units).transpose(1, 2, 3, 0, 4)
    wide = unite(wide.reshape(2, depth, TEAM * width // sides), 2).astype(F32)
    grad_project = unite(own_project, 1).astype(F32)

    chain_sum = jnp.concatenate([chain_attend, chain_feed], axis=1)
    gate_line = lax.dynamic_update_slice_in_dim(
        jnp.zeros((width,), F32), gate_sum[0], team * size, axis=0
    )
    pieces = [pairing_sum[:head_count], recycle_sum[: recycle.shape[0]], gate_line]
    line = jnp.concatenate([x.reshape(-1) for x in pieces])
    extra = -(-line.size // (6 * width))
    line = jnp.pad(line, (0, extra * 6 * width - line.size)).reshape(extra, 6 * width)
    line = jnp.pad(line, ((max_chains, 8 - max_chains - extra), (0, 0))) + chain_sum
    line = after(line, attend_grads)
    line = line + swap(line, 1)
    line = (line + swap(line, 2)).astype(BF16)
    if planes == 2:
        line = jnp.concatenate([line, across(line)], axis=0)
    views = line.shape[0] // 8
    found = [line]
    for d in range(1, groups):
        pairs = [(b, (b + d * TEAM) % blocks) for b in range(blocks)]
        found.append(lax.ppermute(line, "blk", pairs))
    lines = jnp.concatenate(found, axis=0)
    which = [(myself // TEAM + groups - d) % groups // parts for d in range(groups)]
    smooth_rows = smooth.reshape(views, rows, max_chains, -1)
    weights = jnp.stack([lax.dynamic_index_in_dim(smooth_rows, r, 1, False) for r in which])
    weights = jnp.pad(weights, ((0, 0), (0, 0), (0, 8 - max_chains), (0, 0)))
    weights = lax.dynamic_slice_in_dim(weights, myself * cond_local, cond_local, axis=3)
    weights = weights.reshape(groups * views * 8, cond_local)
    kind = jnp.arange(groups * views * 8) % 8
    masks = [(kind < max_chains)] + [kind == max_chains + k for k in range(extra)]
    weights = jnp.concatenate([weights] + [x.astype(BF16)[:, None] for x in masks], axis=1)
    sums = lax.dot_general(weights, lines, (((0,), (0,)), ((), ())), preferred_element_type=F32)
    grad_modulate, grad_offset = sums[:cond_local], sums[cond_local]
    rest, at = sums[cond_local + 1 :].reshape(-1), 0
    found = []
    for x in pieces:
        found.append(rest[at : at + x.size].reshape(x.shape))
        at += x.size
    grad_pairing, grad_recycle, grad_gatebias = found[0].T, found[1], found[2]
    grad_smooth = dot(lines, modulate_full, NT).reshape(groups, views, 8, -1)[:, :, :max_chains]
    grad_smooth = by_group(grad_smooth).reshape(rows, parts, views, max_chains, -1).sum(axis=1)
    grad_smooth = grad_smooth.transpose(1, 0, 2, 3).reshape(views * rows, max_chains, -1)
    sigma = jax.nn.sigmoid(condition)
    grad_condition = grad_smooth * sigma * (1.0 + condition * (1.0 - sigma))
    grad_time = jnp.einsum("rcn,rcd->nd", time_hot, grad_condition, precision=HIGHEST)
    grad_class = jnp.einsum("rcn,rcd->nd", class_hot, grad_condition, precision=HIGHEST)
    if planes != 2:
        found = (grad_time, grad_class, grad_modulate, grad_offset, grad_pairing, grad_gatebias, grad_recycle)
        found = lax.psum(found, "rows")
        grad_time, grad_class, grad_modulate, grad_offset, grad_pairing, grad_gatebias, grad_recycle = found
    return (
        layer_out,
        grad_residues,
        grad_pair,
        grad_time,
        grad_class,
        grad_modulate,
        grad_offset,
        inner[:, : 3 * width],
        grad_pairing,
        inner[:, 3 * width :],
        grad_gatebias,
        grad_project,
        wide[0],
        wide[1],
        grad_narrow,
        grad_recycle,
    )


def solution(mesh):
    in_specs = (
        P("rows", "blk", None),
        P("rows", None, "blk", None),
        P("rows", None),
        P("rows", None),
        P("rows", None),
        P("rows", None),
        P(),
        P(),
        P("blk", None),
        P(),
        P("blk", None),
        P(),
        P("blk", None),
        P(),
        P("blk", None),
        P("blk", None),
        P("blk", None),
        P("blk", None),
        P(),
        P(),
        P("rows", "blk", None),
    )
    out_specs = (
        P("rows", "blk", None),
        P("rows", "blk", None),
        P("rows", None, "blk", None),
        P(),
        P(),
        P("blk", None),
        P(),
        P("blk", None),
        P(),
        P("blk", None),
        P(),
        P("blk", None),
        P("blk", None),
        P("blk", None),
        P("blk", None),
        P(),
    )
    return jax.shard_map(
        per_device, mesh=mesh, in_specs=in_specs, out_specs=out_specs, check_vma=False
    )
```

```python
import functools

import jax
import jax.numpy as jnp
from jax import lax
from jax.experimental import pallas as pl
from jax.experimental.pallas import tpu as pltpu
from jax.sharding import PartitionSpec as P

TEAM = 4
F32, BF16 = jnp.float32, jnp.bfloat16
HIGHEST = lax.Precision.HIGHEST
GRADS, RECYCLE = 4, 5


def dot(former, latter, contract=((1,), (0,))):
    return lax.dot_general(former, latter, (contract, ((), ())), preferred_element_type=F32)


NT, TN = ((1,), (1,)), ((0,), (0,))


def normalize(values):
    center = values - jnp.mean(values, axis=-1, keepdims=True)
    inverse = lax.rsqrt(jnp.mean(center * center, axis=-1, keepdims=True) + 1e-06)
    return center * inverse, inverse


def norm_back(grad, normed, inverse):
    first = jnp.mean(grad, axis=-1, keepdims=True)
    second = jnp.mean(grad * normed, axis=-1, keepdims=True)
    return inverse * (grad - first - normed * second)


def call(kernel, grid, ins, outs, out_shape, scratch=(), micros=0, prefetch=0, mib=32):
    return pl.pallas_call(
        kernel,
        grid_spec=pltpu.PrefetchScalarGridSpec(
            num_scalar_prefetch=prefetch,
            grid=grid,
            in_specs=ins,
            out_specs=outs,
            scratch_shapes=list(scratch),
        ),
        out_shape=out_shape,
        cost_estimate=pl.CostEstimate(flops=micros * 1100000000, bytes_accessed=0, transcendentals=0),
        compiler_params=pltpu.CompilerParams(vmem_limit_bytes=mib * 1024 * 1024),
    )


def whole(shape):
    return pl.BlockSpec(shape, lambda *_: (0,) * len(shape), pipeline_mode=pl.Buffered(buffer_count=1))


def held(shape):
    return pl.BlockSpec(shape, lambda *_: (0,) * len(shape))


def pair_bias(pair_features, pairing):
    rows, q_tiles, k_tiles, width = pair_features.shape
    heads = pairing.shape[1]
    padded = jnp.pad(pairing, ((0, 0), (0, 128 - heads)))

    def kernel(pair_ref, weight_ref, out_ref, flat, turned):
        flat[...] = dot(pair_ref[0].reshape(q_tiles * k_tiles, width), weight_ref[...])
        for k in range(k_tiles):
            turned[:, k, :] = flat[pl.ds(k, q_tiles, stride=k_tiles), :].T[:heads]
        out_ref[0] = turned[...].astype(BF16)

    return call(
        kernel,
        (rows,),
        [
            pl.BlockSpec((1, q_tiles, k_tiles, width), lambda r: (r, 0, 0, 0)),
            whole((width, 128)),
        ],
        pl.BlockSpec((1, heads, k_tiles, q_tiles), lambda r: (r, 0, 0, 0)),
        jax.ShapeDtypeStruct((rows, heads, k_tiles, q_tiles), BF16),
        [pltpu.VMEM((q_tiles * k_tiles, 128), F32), pltpu.VMEM((heads, k_tiles, q_tiles), F32)],
        micros=9,
        mib=50,
    )(pair_features, padded)


def pair_back(pair_features, pairing, grad_bias, line):
    rows, q_tiles, k_tiles, width = pair_features.shape
    heads = pairing.shape[1]
    padded = jnp.pad(pairing.T, ((0, 128 - heads), (0, 0)))

    def kernel(pair_ref, weight_ref, grad_ref, line_in_ref, out_ref, line_ref, flat, sums):
        @pl.when(pl.program_id(0) == 0)
        def _():
            sums[...] = jnp.zeros_like(sums)

        grads = grad_ref[0].astype(F32)
        blank = jnp.zeros((128 - heads, q_tiles), F32)
        for k in range(k_tiles):
            piece = jnp.concatenate([grads[:, k, :], blank], axis=0)
            flat[pl.ds(k, q_tiles, stride=k_tiles), :] = piece.T
        low = flat[...].astype(BF16)
        out_ref[0] = dot(low, weight_ref[...]).astype(BF16).reshape(q_tiles, k_tiles, width)
        sums[...] += dot(low, pair_ref[0].reshape(q_tiles * k_tiles, width), TN)

        @pl.when(pl.program_id(0) == rows - 1)
        def _():
            line_ref[...] = line_in_ref[...]
            for h in range(heads):
                line_ref[GRADS : GRADS + 1, h * width : (h + 1) * width] = sums[h : h + 1, :]

    return call(
        kernel,
        (rows,),
        [
            pl.BlockSpec((1, q_tiles, k_tiles, width), lambda r: (r, 0, 0, 0)),
            whole((128, width)),
            pl.BlockSpec((1, heads, k_tiles, q_tiles), lambda r: (r, 0, 0, 0)),
            whole(line.shape),
        ],
        [pl.BlockSpec((1, q_tiles, k_tiles, width), lambda r: (r, 0, 0, 0)), held(line.shape)],
        [
            jax.ShapeDtypeStruct(pair_features.shape, BF16),
            jax.ShapeDtypeStruct(line.shape, F32),
        ],
        [pltpu.VMEM((q_tiles * k_tiles, 128), F32), pltpu.VMEM((128, width), F32)],
        micros=10,
        mib=50,
    )(pair_features, padded, grad_bias, line)


def assemble(spot, chunks, scratch):
    rows, per, tiles, _ = chunks[0].shape
    team, mine = spot[0], spot[1]
    for d, chunk in enumerate(chunks):
        for r in range(rows):
            source = lax.rem(mine + rows - r, rows)
            for j in range(per):
                start = ((j * rows + source) * TEAM + (team ^ d)) * tiles
                scratch[pl.ds(pl.multiple_of(start, tiles), tiles), :] = chunk[r, j]


def by_owner(spot, kind, tokens, near_ref, far_ref):
    _, rows, _, per, tiles, _ = near_ref.shape
    for d in range(TEAM):
        for r in range(rows):
            source = lax.rem(spot[1] + r, rows)
            for j in range(per):
                start = ((j * rows + source) * TEAM + (spot[0] ^ d)) * tiles
                piece = tokens[pl.ds(pl.multiple_of(start, tiles), tiles), :]
                (far_ref if d % 2 else near_ref)[d // 2, r, kind, j] = piece


def project_rows(begin, member, table_ref, weight_ref, bias_ref, outs, hidden_ref, width, head):
    mods = dot(member, table_ref[:, : 2 * width])
    normed, _ = normalize(begin)
    hidden = (normed * (1.0 + mods[:, width:]) + mods[:, :width]).astype(BF16)
    if hidden_ref is not None:
        hidden_ref[...] = hidden
    both = dot(hidden, weight_ref[...])
    part = both.shape[1] // 4
    low = both[:, : 3 * part].astype(BF16)
    turned = low.T
    count = part // head
    q_ref, k_ref, v_ref, key_ref, value_ref, gate_ref = outs
    q_ref[...] = (turned[:part] * BF16(head**-0.5)).reshape(count, head, -1)
    k_ref[...] = turned[part : 2 * part].reshape(count, head, -1)
    v_ref[...] = turned[2 * part :].reshape(count, head, -1)
    for h in range(count):
        key_ref[h] = low[:, part + h * head : part + (h + 1) * head]
        value_ref[h] = low[:, 2 * part + h * head : 2 * part + (h + 1) * head]
    gate_ref[...] = (both[:, 3 * part :].T + bias_ref[:, :1]).reshape(count, head, -1)


def qkv_specs(count, head, tokens, block):
    wide = pl.BlockSpec((count, head, block), lambda j, *_: (0, 0, j))
    tall = pl.BlockSpec((count, block, head), lambda j, *_: (0, j, 0))
    shapes = [jax.ShapeDtypeStruct((count, head, tokens), BF16)] * 3
    shapes += [jax.ShapeDtypeStruct((count, tokens, head), BF16)] * 2
    shapes += [jax.ShapeDtypeStruct((count, head, tokens), F32)]
    return [wide, wide, wide, tall, tall, wide], shapes


def first_rows(team, chunks, member, table, weight, gate_bias, count, head, block):
    rows, grain, tiles, width = chunks[0].shape
    tokens = rows * grain * tiles * TEAM
    per = block * grain // tokens

    def kernel(team_ref, c0, c1, c2, c3, member_ref, table_ref, weight_ref, bias_ref, row_ref, *rest):
        *outs, scratch = rest
        assemble(team_ref, (c0, c1, c2, c3), scratch)
        row_ref[...] = scratch[...]
        begin = scratch[...].astype(F32)
        project_rows(
            begin, member_ref[...], table_ref, weight_ref, bias_ref, outs, None, width, head
        )

    specs, shapes = qkv_specs(count, head, tokens, block)
    by_token = pl.BlockSpec((block, width), lambda j, *_: (j, 0))
    return call(
        kernel,
        (grain // per,),
        [pl.BlockSpec((rows, per, tiles, width), lambda j, *_: (0, j, 0, 0))] * 4
        + [
            pl.BlockSpec((block, member.shape[1]), lambda j, *_: (j, 0)),
            whole(table.shape),
            whole(weight.shape),
            whole(gate_bias.shape),
        ],
        [by_token] + specs,
        [jax.ShapeDtypeStruct((tokens, width), BF16)] + shapes,
        [pltpu.VMEM((block, width), BF16)],
        micros=8,
        mib=50,
        prefetch=1,
    )(team, *chunks, member, table, weight, gate_bias)


def begin_of(row_ref, point_ref, recycle_ref):
    return row_ref[...].astype(F32) + dot(point_ref[...].astype(BF16), recycle_ref[...], TN)


def second_rows(row, points, recycle, member, table, weight, gate_bias, count, head, block):
    tokens, width = row.shape

    def kernel(row_ref, point_ref, recycle_ref, member_ref, table_ref, weight_ref, bias_ref, hidden_ref, *outs):
        begin = begin_of(row_ref, point_ref, recycle_ref)
        project_rows(
            begin, member_ref[...], table_ref, weight_ref, bias_ref, outs, hidden_ref, width, head
        )

    specs, shapes = qkv_specs(count, head, tokens, block)
    by_token = pl.BlockSpec((block, width), lambda j: (j, 0))
    return call(
        kernel,
        (tokens // block,),
        [
            by_token,
            pl.BlockSpec((8, block), lambda j: (0, j)),
            whole(recycle.shape),
            pl.BlockSpec((block, member.shape[1]), lambda j: (j, 0)),
            whole(table.shape),
            whole(weight.shape),
            whole(gate_bias.shape),
        ],
        [by_token] + specs,
        [jax.ShapeDtypeStruct((tokens, width), BF16)] + shapes,
        micros=8,
        mib=50,
    )(row, points, recycle, member, table, weight, gate_bias)


def attend(queries, keys, values, gate, bias, q_chain, k_chain, place, tiles, block, keep):
    count, head, tokens = queries.shape
    key_tokens = keys.shape[1]
    sources = len(place)
    folds = key_tokens // block
    grain = tokens // block

    def kernel(q_ref, k_ref, v_ref, gate_ref, bias_ref, qc_ref, kc_ref, mixed_ref, *rest):
        if keep:
            attended_ref, probs_ref, share_ref, spread = rest
        else:
            (spread,) = rest

        for b in range(sources):
            spread[place[b] * tiles : (place[b] + 1) * tiles, :] = bias_ref[b, 0].astype(F32)

        def score(i):
            lanes = slice(i * block, (i + 1) * block)
            q, q_chain = q_ref[0, :, lanes], qc_ref[0:1, lanes]
            scores = []
            for f in range(folds):
                lines = slice(f * block, (f + 1) * block)
                part = f // grain
                s = dot(k_ref[0, lines, :], q) + spread[part * block : (part + 1) * block, :]
                same = jnp.concatenate([kc_ref[lines, :]] * (block // 128), axis=1) == q_chain
                scores.append(jnp.where(same, s, -1000000000.0))
            return scores

        def weigh(i, scores):
            lanes = slice(i * block, (i + 1) * block)
            top = functools.reduce(
                jnp.maximum, [jnp.max(s, axis=0, keepdims=True) for s in scores]
            )
            total = jnp.zeros((1, block), F32)
            attended = jnp.zeros((head, block), F32)
            for f in range(folds):
                lines = slice(f * block, (f + 1) * block)
                power = jnp.exp(scores[f] - top)
                total += jnp.sum(power, axis=0, keepdims=True)
                low = power.astype(BF16)
                if keep:
                    probs_ref[0, lines, lanes] = low
                attended += dot(v_ref[0, :, lines], low)
            share = 1.0 / total
            attended *= share
            mixed_ref[0, :, lanes] = (attended * jax.nn.sigmoid(gate_ref[0, :, lanes])).astype(BF16)
            if keep:
                attended_ref[0, :, lanes] = attended
                share_ref[0, :, lanes] = jnp.broadcast_to(share, (8, block))

        now = score(0)
        for i in range(grain):
            later = score(i + 1) if i + 1 < grain else None
            weigh(i, now)
            now = later

    by_head = lambda *shape: pl.BlockSpec((1,) + shape, lambda h: (h,) + (0,) * len(shape))
    outs = [by_head(head, tokens)]
    shapes = [jax.ShapeDtypeStruct((count, head, tokens), BF16)]
    if keep:
        outs += [by_head(head, tokens), by_head(key_tokens, tokens), by_head(8, tokens)]
        shapes += [
            jax.ShapeDtypeStruct((count, head, tokens), F32),
            jax.ShapeDtypeStruct((count, key_tokens, tokens), BF16),
            jax.ShapeDtypeStruct((count, 8, tokens), F32),
        ]
    return call(
        kernel,
        (count,),
        [
            by_head(head, tokens),
            by_head(key_tokens, head),
            by_head(head, key_tokens),
            by_head(head, tokens),
            pl.BlockSpec((sources, 1, tiles, block), lambda h: (0, h, 0, 0)),
            whole(q_chain.shape),
            whole(k_chain.shape),
        ],
        outs,
        shapes,
        [pltpu.VMEM((sources * tiles, block), F32)],
        micros=9 if keep else 8,
        mib=50,
    )(queries, keys, values, gate, bias, q_chain, k_chain)


def attend_back(queries, keys, value_rows, gate, attended, probs, share, own, other, place, tiles, block):
    count, head, tokens = queries.shape
    key_tokens = value_rows.shape[1]
    folds, grain = key_tokens // block, tokens // block
    sources = len(place)

    def kernel(
        q_ref, k_ref, v_ref, gate_ref, attended_ref, probs_ref, share_ref, own_ref, other_ref,
        dq_ref, dk_ref, dv_ref, logit_ref, bias_ref, bias_sum,
    ):
        grad_mixed = own_ref[0].astype(F32) + other_ref[0].astype(F32)
        sigma = jax.nn.sigmoid(gate_ref[0])
        through = grad_mixed * sigma
        upper = through.astype(BF16).astype(F32)
        attended = attended_ref[0]
        logit_ref[0] = (through * attended * (1.0 - sigma)).astype(BF16)
        share = share_ref[0, 0:1, :]
        inner = jnp.sum(upper * attended, axis=0, keepdims=True) * share
        scaled = (upper * share).astype(BF16)
        q = q_ref[0]
        grad_q = jnp.zeros((head, tokens), F32)
        tile_sums = [None] * (folds // grain)
        for f in range(folds):
            lines = slice(f * block, (f + 1) * block)
            power = probs_ref[0, lines, :]
            dv_ref[0, :, lines] = dot(scaled, power, NT).astype(BF16)
            grads = power.astype(F32) * (dot(v_ref[0, lines, :], scaled) - inner)
            low = grads.astype(BF16)
            grad_q += dot(k_ref[0, :, lines], low)
            dk_ref[0, :, lines] = dot(q, low, NT).astype(BF16)
            part = f // grain
            for i in range(grain):
                piece = grads[:, i * block : (i + 1) * block]
                tile_sums[part] = piece if tile_sums[part] is None else tile_sums[part] + piece
        dq_ref[0] = (grad_q * head**-0.5).astype(BF16)
        for part, sums in enumerate(tile_sums):
            bias_sum[part * block : (part + 1) * block, :] = sums
        for b in range(sources):
            lines = slice(place[b] * tiles, (place[b] + 1) * tiles)
            bias_ref[b, 0] = bias_sum[lines, :].astype(BF16)

    by_head = lambda *shape: pl.BlockSpec((1,) + shape, lambda h: (h,) + (0,) * len(shape))
    narrow = jax.ShapeDtypeStruct((count, head, tokens), BF16)
    broad = jax.ShapeDtypeStruct((count, head, key_tokens), BF16)
    return call(
        kernel,
        (count,),
        [
            by_head(head, tokens),
            by_head(head, key_tokens),
            by_head(key_tokens, head),
            by_head(head, tokens),
            by_head(head, tokens),
            by_head(key_tokens, tokens),
            by_head(8, tokens),
            by_head(head, tokens),
            by_head(head, tokens),
        ],
        [
            by_head(head, tokens),
            by_head(head, key_tokens),
            by_head(head, key_tokens),
            by_head(head, tokens),
            pl.BlockSpec((sources, 1, tiles, block), lambda h: (0, h, 0, 0)),
        ],
        [narrow, broad, broad, narrow, jax.ShapeDtypeStruct((sources, count, tiles, block), BF16)],
        [
            pltpu.VMEM((sources * tiles, block), F32),
        ],
        micros=10,
        mib=50,
    )(queries, keys, value_rows, gate, attended, probs, share, own, other)


def unpack(spot, bundle_refs, mixed_refs, weights, mixed, first):
    near, tail, *far = bundle_refs
    groups, _, part, wide = near.shape

    @pl.when(first)
    def _():
        mine = pl.multiple_of(spot[2] * wide, wide)
        other = pl.multiple_of((1 - spot[2]) * wide, wide)
        for g in range(groups):
            lines = slice(g * part, (g + 1) * part)
            for k in range(2):
                weights[k, lines, pl.ds(mine, wide)] = near[g, k]
                if far:
                    weights[k, lines, pl.ds(other, wide)] = far[0][g, k]
            weights[2, lines, pl.ds(mine, wide)] = tail[g, :, :wide]
            if far:
                weights[2, lines, pl.ds(other, wide)] = far[1][g]
            weights[3, lines, :] = tail[g, :, wide:]

    count, head, _ = mixed_refs[0].shape
    size = count * head
    for d, ref in enumerate(mixed_refs):
        start = pl.multiple_of((spot[0] ^ d) * size, size)
        mixed[pl.ds(start, size), :] = ref[...].reshape(size, -1)


def feed_first(team, mixed_chunks, row, member, table, bundle, coordinate, block):
    tokens, width = row.shape
    count, head, _ = mixed_chunks[0].shape

    def kernel(team_ref, m0, m1, m2, m3, row_ref, member_ref, table_ref, coord_ref, *rest):
        *bundle_refs, out_ref, weights, mixed = rest
        unpack(team_ref, bundle_refs, (m0, m1, m2, m3), weights, mixed, pl.program_id(0) == 0)
        mods = dot(member_ref[...], table_ref[:, 2 * width :])
        attend_gate, feed_shift = mods[:, :width], mods[:, width : 2 * width]
        feed_scale, feed_gate = mods[:, 2 * width : 3 * width], mods[:, 3 * width :]
        attend_out = dot(mixed[...], weights[0], TN)
        after = row_ref[...].astype(F32) + attend_gate * attend_out
        normed, _ = normalize(after)
        hidden = (normed * (1.0 + feed_scale) + feed_shift).astype(BF16)
        gate_pre, lift_pre = dot(hidden, weights[1]), dot(hidden, weights[2])
        inner = (gate_pre * jax.nn.sigmoid(gate_pre) * lift_pre).astype(BF16)
        share = after * (1.0 / TEAM) + feed_gate * dot(inner, weights[3])
        out_ref[...] = dot(coord_ref[...], share.astype(BF16), NT)

    by_token = pl.BlockSpec((block, width), lambda j, *_: (j, 0))
    return call(
        kernel,
        (tokens // block,),
        [pl.BlockSpec((count, head, block), lambda j, *_: (0, 0, j))] * 4
        + [
            by_token,
            pl.BlockSpec((block, member.shape[1]), lambda j, *_: (j, 0)),
            whole(table.shape),
            whole(coordinate.shape),
        ]
        + [whole(x.shape) for x in bundle],
        pl.BlockSpec((8, block), lambda j, *_: (0, j)),
        jax.ShapeDtypeStruct((8, tokens), F32),
        [pltpu.VMEM((4, width, width), BF16), pltpu.VMEM((width, block), BF16)],
        micros=14,
        mib=50,
        prefetch=1,
    )(team, *mixed_chunks, row, member, table, coordinate, *bundle)


def feed_both(team, mixed_chunks, row, points, recycle, cotangent, member, chains, table, bundle, block):
    tokens, width = row.shape
    count, head, _ = mixed_chunks[0].shape
    groups = bundle[0].shape[0]
    part = width // groups
    wide = bundle[0].shape[3]
    sides = width // wide
    rows, grain, tiles, _ = cotangent[0].shape
    last = tokens // block - 1
    size = count * head

    def kernel(team_ref, m0, m1, m2, m3, row_ref, point_ref, recycle_ref, c0, c1, c2, c3, member_ref, chain_ref,
               table_ref, *rest):
        bundle_refs, rest = rest[: len(bundle)], rest[len(bundle) :]
        share_ref, after_ref, near_ref, far_ref, chain_sum_ref, down_ref = rest[:6]
        grad_refs, (weights, mixed, upstream, sums, turned) = rest[6:-5], rest[-5:]
        team = team_ref[0]
        first = pl.program_id(0) == 0
        unpack(team_ref, bundle_refs, (m0, m1, m2, m3), weights, mixed, first)
        assemble(team_ref, (c0, c1, c2, c3), upstream)

        @pl.when(first)
        def _():
            sums[...] = jnp.zeros_like(sums)
            chain_sum_ref[...] = jnp.zeros_like(chain_sum_ref)

        mods = dot(member_ref[...], table_ref[:, 2 * width :])
        attend_gate, feed_shift = mods[:, :width], mods[:, width : 2 * width]
        feed_scale, feed_gate = mods[:, 2 * width : 3 * width], mods[:, 3 * width :]
        attend_out = dot(mixed[...], weights[0], TN)
        after = begin_of(row_ref, point_ref, recycle_ref) + attend_gate * attend_out
        normed, inverse = normalize(after)
        hidden = (normed * (1.0 + feed_scale) + feed_shift).astype(BF16)
        gate_pre, lift_pre = dot(hidden, weights[1]), dot(hidden, weights[2])
        sigma = jax.nn.sigmoid(gate_pre)
        silu = gate_pre * sigma
        inner = (silu * lift_pre).astype(BF16)
        branch = dot(inner, weights[3])

        chain = chain_ref[...]

        def by_chain(place, grad):
            chain_sum_ref[:, place * width : (place + 1) * width] += dot(chain, grad.astype(BF16))

        g = upstream[...].astype(F32)
        share_ref[...] = (after * (1.0 / TEAM) + feed_gate * branch).astype(BF16)
        by_chain(3, g * branch)
        grad_branch = (g * feed_gate).astype(BF16)
        sums[0] += dot(inner, grad_branch, TN)
        grad_inner = dot(grad_branch, weights[3], NT)
        grad_gate = (grad_inner * lift_pre * sigma * (1.0 + gate_pre * (1.0 - sigma))).astype(BF16)
        grad_lift = (grad_inner * silu).astype(BF16)
        sums[1] += dot(hidden, grad_gate, TN)
        sums[2] += dot(hidden, grad_lift, TN)
        grad_hidden = dot(grad_gate, weights[1], NT) + dot(grad_lift, weights[2], NT)
        by_chain(1, grad_hidden)
        by_chain(2, grad_hidden * normed)
        grad_after = g * (1.0 / TEAM) + norm_back(grad_hidden * (1.0 + feed_scale), normed, inverse)
        after_ref[...] = grad_after
        by_chain(0, grad_after * attend_out)
        grad_out = (grad_after * attend_gate).astype(BF16)
        sums[3] += dot(mixed[...], grad_out)
        turned[...] = dot(grad_out, weights[0], NT).T.astype(BF16)
        for d in range(TEAM):
            start = pl.multiple_of((team ^ d) * size, size)
            piece = turned[pl.ds(start, size), :].reshape(count, head, block)
            (far_ref if d % 2 else near_ref)[d // 2] = piece

        @pl.when(pl.program_id(0) == last)
        def _():
            for g in range(groups):
                lines = slice(g * part, (g + 1) * part)
                down_ref[g] = sums[0, lines, :].astype(BF16)
                for side, ref in enumerate(grad_refs):
                    start = pl.multiple_of((team_ref[2] ^ side) * wide, wide)
                    for k in range(3):
                        ref[g, k] = sums[1 + k, lines, pl.ds(start, wide)].astype(BF16)

    by_token = pl.BlockSpec((block, width), lambda j, *_: (j, 0))
    by_lane = pl.BlockSpec((8, block), lambda j, *_: (0, j))
    halves = pl.BlockSpec((2, count, head, block), lambda j, *_: (0, 0, 0, j))
    half = jax.ShapeDtypeStruct((2, count, head, tokens), BF16)
    return call(
        kernel,
        (tokens // block,),
        [pl.BlockSpec((count, head, block), lambda j, *_: (0, 0, j))] * 4
        + [by_token, by_lane, whole(recycle.shape)]
        + [pl.BlockSpec((rows, block * grain // tokens, tiles, width), lambda j, *_: (0, j, 0, 0))] * 4
        + [
            pl.BlockSpec((block, member.shape[1]), lambda j, *_: (j, 0)),
            by_lane,
            whole(table.shape),
        ]
        + [whole(x.shape) for x in bundle],
        [by_token, by_token, halves, halves, held((8, 4 * width)), held((groups, part, width))]
        + [held((groups, 3, part, wide))] * sides,
        [
            jax.ShapeDtypeStruct((tokens, width), BF16),
            jax.ShapeDtypeStruct((tokens, width), F32),
            half,
            half,
            jax.ShapeDtypeStruct((8, 4 * width), F32),
            jax.ShapeDtypeStruct((groups, part, width), BF16),
        ]
        + [jax.ShapeDtypeStruct((groups, 3, part, wide), BF16)] * sides,
        [
            pltpu.VMEM((4, width, width), BF16),
            pltpu.VMEM((width, block), BF16),
            pltpu.VMEM((block, width), BF16),
            pltpu.VMEM((4, width, width), F32),
            pltpu.VMEM((width, block), BF16),
        ],
        micros=33,
        mib=56,
        prefetch=1,
    )(team, *mixed_chunks, row, points, recycle, *cotangent, member, chains, table, *bundle)


def finish(spot, share, hidden, row, points, recycle, grad_after, grads, member, chains, chain_feed, table, weight, slot, rows, tiles, groups, sides, block):
    tokens, width = row.shape
    count, head, _ = grads[0].shape
    size = count * head
    part = width // groups
    wide = 4 * size // sides
    last = tokens // block - 1
    coords = 3
    grain = tokens // (rows * TEAM * tiles)
    per = block * grain // tokens

    def kernel(spot_ref, share_ref, hidden_ref, row_ref, point_ref, recycle_ref, after_ref, q_ref, k_ref, v_ref, gate_ref,
               member_ref, chain_ref, feed_ref, table_ref, weight_ref,
               near_ref, far_ref, line_ref, *rest):
        *sum_refs, sums, owners, chain_sum_ref, recycle_sum_ref, gate_sum_ref = rest
        first = pl.program_id(0) == 0

        @pl.when(first)
        def _():
            sums[...] = jnp.zeros_like(sums)
            chain_sum_ref[...] = jnp.zeros_like(chain_sum_ref)
            recycle_sum_ref[...] = jnp.zeros_like(recycle_sum_ref)
            gate_sum_ref[...] = jnp.zeros_like(gate_sum_ref)

        stacked = jnp.concatenate(
            [ref[...].reshape(size, block) for ref in (q_ref, k_ref, v_ref, gate_ref)], axis=0
        )
        low = stacked.T
        gate_sum_ref[...] += jnp.sum(low[:, 3 * size :].astype(F32), axis=0, keepdims=True)
        sums[...] += dot(hidden_ref[...], low, TN)
        grad_hidden = dot(low, weight_ref[...], NT)
        mods = dot(member_ref[...], table_ref[:, width : 2 * width])
        normed, inverse = normalize(begin_of(row_ref, point_ref, recycle_ref))
        chain = chain_ref[...]
        chain_sum_ref[:, :width] += dot(chain, grad_hidden.astype(BF16))
        chain_sum_ref[:, width:] += dot(chain, (grad_hidden * normed).astype(BF16))
        grad = after_ref[...] + norm_back(grad_hidden * (1.0 + mods), normed, inverse)
        low_grad = grad.astype(BF16)
        owners[...] = low_grad
        by_owner(spot_ref, 0, share_ref, near_ref, far_ref)
        by_owner(spot_ref, 1, owners, near_ref, far_ref)
        recycle_sum_ref[...] += dot(point_ref[...].astype(BF16), low_grad)

        @pl.when(pl.program_id(0) == last)
        def _():
            line_ref[...] = jnp.zeros_like(line_ref)
            line_ref[:, : 2 * width] = chain_sum_ref[...]
            line_ref[:, 2 * width :] = feed_ref[...]
            for k in range(coords):
                lanes = slice(k * width, (k + 1) * width)
                line_ref[RECYCLE : RECYCLE + 1, lanes] = recycle_sum_ref[k : k + 1, :]
            start = pl.multiple_of(slot + spot_ref[0] * 256, 256)
            line_ref[GRADS : GRADS + 1, pl.ds(start, size)] = gate_sum_ref[...]
            for side, ref in enumerate(sum_refs):
                start = pl.multiple_of((spot_ref[2] ^ side) * wide, wide)
                for g in range(groups):
                    ref[g] = sums[g * part : (g + 1) * part, pl.ds(start, wide)].astype(BF16)

    by_token = pl.BlockSpec((block, width), lambda j, *_: (j, 0))
    by_lane = pl.BlockSpec((8, block), lambda j, *_: (0, j))
    by_query = pl.BlockSpec((count, head, block), lambda j, *_: (0, 0, j))
    owned = pl.BlockSpec((2, rows, 2, per, tiles, width), lambda j, *_: (0, 0, 0, j, 0, 0))
    return call(
        kernel,
        (tokens // block,),
        [by_token, by_token, by_token, by_lane, whole(recycle.shape), by_token]
        + [by_query] * 4
        + [
            pl.BlockSpec((block, member.shape[1]), lambda j, *_: (j, 0)),
            by_lane,
            whole(chain_feed.shape),
            whole(table.shape),
            whole(weight.shape),
        ],
        [
            owned,
            owned,
            held((8, 6 * width)),
        ]
        + [held((groups, part, wide))] * sides,
        [
            jax.ShapeDtypeStruct((2, rows, 2, grain, tiles, width), BF16),
            jax.ShapeDtypeStruct((2, rows, 2, grain, tiles, width), BF16),
            jax.ShapeDtypeStruct((8, 6 * width), F32),
        ]
        + [jax.ShapeDtypeStruct((groups, part, wide), BF16)] * sides,
        [
            pltpu.VMEM((width, 4 * size), F32),
            pltpu.VMEM((block, width), BF16),
            pltpu.VMEM((8, 2 * width), F32),
            pltpu.VMEM((8, width), F32),
            pltpu.VMEM((1, size), F32),
        ],
        micros=12,
        mib=50,
        prefetch=1,
    )(spot, share, hidden, row, points, recycle, grad_after, *grads, member, chains, chain_feed, table, weight)


def to_slots(spot, found, grain):
    rows = len(found)
    kinds, _, tiles, width = found[0].shape
    local = grain * tiles

    def kernel(spot_ref, *refs):
        inputs, outs, spread = refs[:rows], refs[rows:-1], refs[-1]
        for d in range(rows):
            row = lax.rem(spot_ref[1] + rows - d, rows)
            for k in range(kinds):
                for c in range(width // 128):
                    lanes = slice(c * 128, (c + 1) * 128)
                    for j in range(grain):
                        spread[c, pl.ds(j, tiles, stride=grain), :] = inputs[d][k, j, :, lanes].astype(F32)
                    outs[k][pl.ds(row, 1), :, lanes] = spread[c].astype(BF16)[None]

    return call(
        kernel,
        (1,),
        [whole(found[0].shape)] * rows,
        [held((rows, local, width))] * kinds,
        [jax.ShapeDtypeStruct((rows, local, width), BF16)] * kinds,
        [pltpu.VMEM((width // 128, local, 128), F32)],
        micros=3,
        mib=50,
        prefetch=1,
    )(spot, *found)


def chain_products(spot, lines, weights, modulate, first):
    many, long = lines[0].shape
    count = len(lines)
    width = modulate.shape[0]

    def kernel(spot_ref, *refs):
        line_refs, (weight_ref, modulate_ref, first_ref, rest_ref, back_ref) = refs[:count], refs[count:]
        total = None
        for n, ref in enumerate(line_refs):
            part = dot(weight_ref[n], ref[...])
            total = part if total is None else total + part
            group = lax.rem(spot_ref[3] + count - n, count)
            back_ref[pl.ds(group, 1)] = dot(ref[...], modulate_ref[...], NT)[None]
        first_ref[...] = total[:first]
        rest_ref[...] = total[first:]

    rest = weights.shape[1] - first
    return call(
        kernel,
        (1,),
        [whole((many, long))] * count + [whole(weights.shape), whole(modulate.shape)],
        [held((first, long)), held((rest, long)), held((count, many, width))],
        [
            jax.ShapeDtypeStruct((first, long), F32),
            jax.ShapeDtypeStruct((rest, long), F32),
            jax.ShapeDtypeStruct((count, many, width), F32),
        ],
        micros=5,
        mib=50,
        prefetch=1,
    )(spot, *lines, weights, modulate)


def per_device(
    residues,
    pair_features,
    chain_lengths,
    time_bins,
    fold_class,
    self_flag,
    time_table,
    class_table,
    modulate,
    offset,
    heads,
    pairing,
    gating,
    gating_bias,
    project,
    widen_gate,
    widen_up,
    narrow,
    coordinate,
    recycle,
    cotangent,
):
    blocks = lax.axis_size("blk")
    planes = lax.axis_size("rows")
    myself = lax.axis_index("blk")
    rows, local, width = residues.shape
    row_len = local * blocks
    grain = row_len // pair_features.shape[1]
    tiles = local // grain
    head_count = pairing.shape[1]
    head = width // head_count
    count = head_count // TEAM
    size = count * head
    span = blocks // rows
    parts = span // TEAM
    groups = blocks // TEAM
    tokens = row_len // parts
    block = tokens // grain
    max_chains = chain_lengths.shape[1]
    my_row = myself // span
    my_part = (myself % span) // TEAM
    team = myself % TEAM
    sides = 2 if planes % 2 == 0 else 1
    my_side = lax.axis_index("rows") % sides
    team_ref = jnp.stack([team, my_row, my_side, myself // TEAM]).astype(jnp.int32)
    place = []
    for b in range(blocks):
        r, u, t = b // span, (b % span) // TEAM, b % TEAM
        place.append((u * rows + r) * TEAM + t)

    row_groups = [[r * span + s for r in range(rows)] for s in range(span)]
    same_team = [[g * TEAM + t for g in range(groups)] for t in range(TEAM)]
    teams = [[g * TEAM + t for t in range(TEAM)] for g in range(groups)]
    part_groups = [
        [r * span + u * TEAM + t for u in range(parts)] for r in range(rows) for t in range(TEAM)
    ]

    def swap(x, k):
        return lax.ppermute(x, "blk", [(b, b ^ k) for b in range(blocks)])

    def team_gather(x):
        far = swap(x, 2)
        return x, swap(x, 1), far, swap(far, 1)

    def group_sum(x):
        k = 1
        while k < span:
            x = x + swap(x, k)
            k *= 2
        return x

    def exchange(x, members=None):
        return lax.all_to_all(x, "blk", 0, 0, tiled=True, axis_index_groups=members)

    def pick(x, d):
        return lax.dynamic_index_in_dim(x, team ^ d, 0, False)

    def ordered(x):
        x = list(x)
        for bit in (1, 2):
            moved = (team & bit) != 0
            x = [jnp.where(moved, x[d ^ bit], x[d]) for d in range(TEAM)]
        return x

    def across(x):
        return lax.ppermute(x, "rows", [(p, p ^ 1) for p in range(planes)])

    def my_half(x, axis, other=0):
        wide = x.shape[axis] // sides
        return lax.dynamic_slice_in_dim(x, (my_side ^ other) * wide, wide, axis)

    def unite(x, axis):
        if sides == 1:
            return x
        y = across(x)
        return jnp.concatenate([jnp.where(my_side == 0, x, y), jnp.where(my_side == 0, y, x)], axis)

    def add_planes(x):
        if planes > 2:
            x = lax.psum(x, "rows", axis_index_groups=[list(range(p, planes, 2)) for p in range(2)])
        return x

    def pair_sum(x):
        if sides == 1:
            return x[0]
        return (x[0].astype(F32) + across(x[1]).astype(F32)).astype(BF16)

    def scatter(x):
        x = lax.psum_scatter(
            x, "blk", scatter_dimension=0, axis_index_groups=same_team, tiled=True
        )
        return add_planes(x)

    def after(x, *others):
        return lax.optimization_barrier((x, *others))[0]

    def row_shift(x):
        found = [lax.dynamic_index_in_dim(x, my_row, 0, False)]
        for d in range(1, rows):
            piece = lax.dynamic_index_in_dim(x, (my_row + d) % rows, 0, False)
            pairs = [(b, (b + d * span) % blocks) for b in range(blocks)]
            found.append(lax.ppermute(piece, "blk", pairs))
        return found

    def fold(x):
        return x.reshape(rows, tiles, grain, width).transpose(0, 2, 1, 3)

    depth = heads.shape[0]
    attend_w = jnp.concatenate(
        [heads.reshape(depth, 3, TEAM, size), gating.reshape(depth, 1, TEAM, size)], axis=1
    )
    attend_w = my_half(attend_w.transpose(2, 0, 1, 3).reshape(TEAM, depth, 4 * size), 1)
    attend_w = jnp.broadcast_to(attend_w[None], (groups,) + attend_w.shape)
    attend_w = exchange(attend_w.reshape(blocks, depth // sides, 4 * size))

    units = narrow.shape[0]
    widen = jnp.stack([widen_gate, widen_up], axis=0).reshape(2, depth, groups, TEAM, units)
    widen = my_half(widen, 2).transpose(3, 0, 1, 2, 4).reshape(TEAM, 2, depth, width // sides)
    out_w = my_half(project, 1)[None]
    widen = [pick(widen, d) for d in range(TEAM)]
    widen = [widen[0]] + [swap(widen[d], d) for d in range(1, TEAM)]
    widen = jnp.stack(ordered(widen), axis=1).reshape(2, TEAM * depth, width // sides)
    out_w = jnp.stack(ordered(team_gather(out_w)), axis=1).reshape(1, TEAM * depth, width // sides)
    def gather(x):
        return lax.all_gather(x, "blk", axis=0, axis_index_groups=same_team)

    first_bundle = jnp.concatenate([out_w, widen[:1]], axis=0)
    bundle = [gather(first_bundle)]
    bundle.append(gather(jnp.concatenate([widen[1], narrow], axis=1)))
    if sides == 2:
        bundle += [across(bundle[0]), across(bundle[1][:, :, : width // sides])]

    tile_bias = pair_bias(pair_features, after(pairing, first_bundle))

    hot = lambda ids, n: (ids[:, :, None] == jnp.arange(n, dtype=jnp.int32)).astype(F32)
    ids = jnp.concatenate([time_bins, fold_class], axis=1)
    if planes == 2:
        ids = jnp.concatenate([ids, across(ids)], axis=0)
    time_hot = hot(ids[:, :max_chains], time_table.shape[0])
    class_hot = hot(ids[:, max_chains:], class_table.shape[0])
    condition = jnp.einsum(
        "rcn,nd->rcd", time_hot, time_table.astype(F32), precision=HIGHEST
    ) + jnp.einsum("rcn,nd->rcd", class_hot, class_table.astype(F32), precision=HIGHEST)
    smooth = jax.nn.silu(condition).astype(BF16)
    cond_local = modulate.shape[0]
    my_smooth = lax.dynamic_slice_in_dim(smooth, myself * cond_local, cond_local, axis=2)
    per_chain = jnp.einsum("rcd,dm->rcm", my_smooth[:rows], modulate, preferred_element_type=F32)
    upper = lax.reduce_precision(per_chain, 8, 7)
    both = jnp.stack([upper, per_chain - upper], axis=1).astype(BF16).reshape(rows, -1, width)
    moved = jnp.stack(row_shift(jnp.concatenate([fold(residues).reshape(rows, local, width), both], axis=1)))
    moved = after(moved, tile_bias)
    row_chunks = team_gather(moved[:, :local].reshape(rows, grain, tiles, width))
    per_chain = moved[:, local:].reshape(2 * rows, max_chains, 6 * width).astype(F32)
    per_chain = group_sum(jnp.sum(per_chain, axis=0)) + offset.astype(F32)
    upper = lax.reduce_precision(per_chain, 8, 7)
    table = jnp.concatenate(
        [upper, per_chain - upper, jnp.zeros((16 - 2 * max_chains, per_chain.shape[1]), F32)],
        axis=0,
    ).astype(BF16)

    bias_out = tile_bias.reshape(rows, TEAM, count, tiles, rows, parts, TEAM * tiles)
    bias_out = bias_out.transpose(0, 5, 1, 2, 3, 4, 6).reshape(blocks, count, tiles, block)
    attend_w = unite(attend_w, 1).reshape(width, 4 * size)
    bias = exchange(after(bias_out, attend_w))

    ends = jnp.cumsum(lax.dynamic_index_in_dim(chain_lengths, my_row, 0, False))
    flags = lax.dynamic_index_in_dim(self_flag, my_row, 0, False)

    def slots(part):
        r = jnp.arange(rows, dtype=jnp.int32)[None, :, None, None]
        t = jnp.arange(TEAM, dtype=jnp.int32)[None, None, :, None]
        j = jnp.arange(grain, dtype=jnp.int32)[:, None, None, None]
        a = jnp.arange(tiles, dtype=jnp.int32)[None, None, None, :]
        return (((r * span + part * TEAM + t) * tiles + a) * grain + j).reshape(tokens)

    def chain_of(places):
        return jnp.sum((places[:, None] >= ends[None, :]).astype(jnp.int32), axis=1)

    q_chain = chain_of(slots(my_part))
    k_chain = chain_of(jnp.concatenate([slots(u) for u in range(parts)]))
    q_lines = jnp.broadcast_to(q_chain[None, :], (8, tokens))
    k_lines = jnp.broadcast_to(k_chain[:, None], (parts * tokens, 128))
    ids = jnp.arange(16, dtype=jnp.int32)
    ids = jnp.where(ids < 2 * max_chains, ids % max_chains, -1)
    member = (q_chain[:, None] == ids[None, :]).astype(BF16)
    chain_hot = q_chain[None, :] == jnp.arange(8, dtype=jnp.int32)[:, None]
    chains = chain_hot.astype(BF16)
    flag_lines = jnp.sum(
        jnp.where(chain_hot[:max_chains], flags.astype(F32)[:, None], 0.0), axis=0, keepdims=True
    )
    gate_bias = lax.dynamic_slice_in_dim(gating_bias, team * size, size).astype(F32)
    gate_bias = jnp.broadcast_to(gate_bias[:, None], (size, 128))
    points_w = jnp.pad(coordinate.T, ((0, 8 - coordinate.shape[1]), (0, 0)))
    recycle_w = jnp.pad(recycle, ((0, 8 - recycle.shape[0]), (0, 0)))

    def all_keys(keys, values):
        if parts == 1:
            return keys, values
        keys = lax.all_gather(keys, "blk", axis=0, axis_index_groups=part_groups)
        values = lax.all_gather(values, "blk", axis=0, axis_index_groups=part_groups)
        keys = keys.transpose(1, 0, 2, 3).reshape(count, parts * tokens, head)
        values = values.transpose(1, 2, 0, 3).reshape(count, head, parts * tokens)
        return keys, values

    row, q_one, _, v_one, key_one, _, gate_one = first_rows(
        team_ref, row_chunks, member, table, attend_w, gate_bias, count, head, tokens // 2
    )
    key_one, v_one = all_keys(key_one, v_one)
    upstream = jnp.stack(row_shift(fold(after(cotangent, row))))
    q_lines_one = after(q_lines, bundle[-sides])
    (mixed_one,) = attend(q_one, key_one, v_one, gate_one, bias, q_lines_one, k_lines, place, tiles, block, False)
    mixed_one = team_gather(after(mixed_one, bundle[1]))
    shares = feed_first(
        team_ref, mixed_one, row, member, table, bundle, points_w, block
    )
    shares = shares + swap(shares, 1)
    shares = shares + swap(shares, 2)
    points = lax.reduce_precision(shares, 8, 7) * flag_lines

    views = 2 if planes == 2 else 1
    which = [(myself // TEAM + groups - d) % groups // parts for d in range(groups)]
    smooth_rows = smooth.reshape(views, rows, max_chains, -1)
    weights = jnp.stack([lax.dynamic_index_in_dim(smooth_rows, r, 1, False) for r in which])
    weights = jnp.pad(weights, ((0, 0), (0, 0), (0, 8 - max_chains), (0, 0)))
    weights = lax.dynamic_slice_in_dim(weights, myself * cond_local, cond_local, axis=3)
    weights = weights.reshape(groups, views * 8, cond_local)
    kind = jnp.arange(views * 8) % 8
    masks = jnp.stack([kind < max_chains, kind == GRADS, kind == RECYCLE], axis=1).astype(BF16)
    masks = jnp.broadcast_to(masks[None], (groups,) + masks.shape)
    weights = jnp.concatenate([weights, masks], axis=2).transpose(0, 2, 1)
    weights = jnp.pad(weights, ((0, 0), (0, -weights.shape[1] % 8), (0, 0)))

    modulate_full = lax.all_gather(after(modulate, row), "blk", axis=0, tiled=True)
    hidden, q_two, k_two, v_two, key_two, value_two, gate_two = second_rows(
        row, points, after(recycle_w, modulate_full, upstream, weights), member, table, attend_w, gate_bias, count, head, block
    )
    key_two, v_all = all_keys(key_two, v_two)
    value_two, k_two = all_keys(value_two, k_two)
    mixed_two, attended, probs, share = attend(
        q_two, key_two, v_all, gate_two, bias, q_lines, k_lines, place, tiles, block, True
    )
    far = swap(after(upstream, points), 2)
    upstream = upstream, swap(upstream, 1), far, swap(after(far, q_two), 1)
    result, grad_after, near, far, chain_feed, down_grads, *feed_grads = feed_both(
        team_ref, team_gather(after(mixed_two, upstream[3])), row, points, recycle_w, upstream, member, chains, table,
        bundle, block,
    )

    def near_sum(near, far):
        return (near.astype(F32) + swap(far, 1).astype(F32)).astype(BF16)

    halves = (near.astype(F32) + swap(far, 1).astype(F32)).astype(BF16)
    other_half = swap(halves[1], 2)
    grad_q, grad_k, grad_v, grad_logit, bias_grad = attend_back(
        q_two, k_two, value_two, gate_two, attended, probs, share, halves[0], other_half, place, tiles, block
    )
    bias_grad = exchange(bias_grad)
    if parts > 1:
        key_value = jnp.stack([grad_k, grad_v]).reshape(2, count, head, parts, tokens)
        key_value = lax.psum_scatter(
            key_value.transpose(3, 0, 1, 2, 4), "blk", scatter_dimension=0, axis_index_groups=part_groups
        )
        grad_k, grad_v = key_value[0], key_value[1]
    feed_grads = pair_sum(feed_grads)
    down_own = scatter(down_grads)[0]
    wide_own = scatter(feed_grads)[0].reshape(3, TEAM, depth, width // sides)
    gate_slot = head_count * pair_features.shape[3]
    begin_near, begin_far, line, *attend_grads = finish(
        team_ref, result, hidden, row, points, recycle_w, grad_after, (grad_q, grad_k, grad_v, grad_logit), member, chains, chain_feed,
        table, attend_w, gate_slot, rows, tiles, groups, sides, block,
    )

    stage = lax.optimization_barrier
    both = near_sum(begin_near, after(begin_far, bias_grad))
    both_far = swap(both[1], 2)
    bias_grad = bias_grad.reshape(rows, parts, TEAM, count, tiles, rows, TEAM * tiles)
    bias_grad = bias_grad.transpose(0, 2, 3, 4, 5, 1, 6).reshape(rows, head_count, tiles, parts * block)
    grad_pair, line = pair_back(pair_features, pairing, after(bias_grad, both), line)
    attend_far = across(attend_grads[1]) if sides == 2 else attend_grads[0]
    line, attend_far, both_far, down_own = stage((line, attend_far, both_far, down_own))
    attend_own = attend_grads[0]
    if sides == 2:
        attend_own = (attend_own.astype(F32) + attend_far.astype(F32)).astype(BF16)
    attend_own = exchange(attend_own.reshape(blocks, depth, 4 * size // sides))

    line = line + swap(line, 1)
    line_far = swap(line, 2)
    total = (both[0].astype(F32) + both_far.astype(F32)).astype(BF16)
    by_shift = [total[0]]
    for d in range(1, rows):
        pairs = [(b, (b + d * span) % blocks) for b in range(blocks)]
        by_shift.append(lax.ppermute(total[d], "blk", pairs))
    line = (line + line_far).astype(BF16)
    line_far = across(line) if planes == 2 else line
    line_far, wide_own = stage((line_far, wide_own))
    if planes == 2:
        line = jnp.concatenate([line, line_far], axis=0)
    lines = [line]
    for d in range(1, groups):
        pairs = [(b, (b + d * TEAM) % blocks) for b in range(blocks)]
        lines.append(lax.ppermute(line, "blk", pairs))
    wide = exchange(after(wide_own, attend_own).transpose(1, 0, 2, 3), teams)
    attend_own, wide, by_shift, lines = stage((attend_own, wide, by_shift, lines))

    inner = jnp.sum(attend_own.astype(F32).reshape(groups, TEAM, depth, 4 // sides, size), axis=0)
    inner = add_planes(inner.astype(BF16)).transpose(1, 2, 0, 3).reshape(depth, 4 * width // sides)
    inner = unite(inner, 1).astype(F32)
    if planes == 2:
        grad_narrow = down_own.astype(F32) + across(down_own).astype(F32)
    else:
        grad_narrow = lax.psum(down_own, "rows").astype(F32)
    own_project = jnp.sum(wide[:, 2].astype(F32), axis=0).astype(BF16)
    wide = wide[:, :2].reshape(TEAM, 2, depth, groups // sides, units).transpose(1, 2, 3, 0, 4)
    wide = unite(wide.reshape(2, depth, TEAM * width // sides), 2).astype(F32)
    grad_project = unite(own_project, 1).astype(F32)

    layer_out, grad_residues = to_slots(team_ref, by_shift, grain)

    grad_modulate, sums, back = chain_products(team_ref, lines, weights, modulate_full, cond_local)
    grad_offset = sums[0]
    grad_pairing = sums[1, :gate_slot].reshape(head_count, -1).T
    grad_gatebias = sums[1, gate_slot : gate_slot + 256 * TEAM].reshape(TEAM, 256)[:, :size].reshape(width)
    grad_recycle = sums[2, : recycle.size].reshape(recycle.shape)
    grad_smooth = back.reshape(rows, parts, views, 8, -1)[:, :, :, :max_chains].sum(axis=1)
    grad_smooth = grad_smooth.transpose(1, 0, 2, 3).reshape(views * rows, max_chains, -1)
    sigma = jax.nn.sigmoid(condition)
    grad_condition = grad_smooth * sigma * (1.0 + condition * (1.0 - sigma))
    grad_time = jnp.einsum("rcn,rcd->nd", time_hot, grad_condition, precision=HIGHEST)
    grad_class = jnp.einsum("rcn,rcd->nd", class_hot, grad_condition, precision=HIGHEST)
    if planes != 2:
        found = (grad_time, grad_class, grad_modulate, grad_offset, grad_pairing, grad_gatebias, grad_recycle)
        found = lax.psum(found, "rows")
        grad_time, grad_class, grad_modulate, grad_offset, grad_pairing, grad_gatebias, grad_recycle = found
    return (
        layer_out,
        grad_residues,
        grad_pair,
        grad_time,
        grad_class,
        grad_modulate,
        grad_offset,
        inner[:, : 3 * width],
        grad_pairing,
        inner[:, 3 * width :],
        grad_gatebias,
        grad_project,
        wide[0],
        wide[1],
        grad_narrow,
        grad_recycle,
    )


def solution(mesh):
    in_specs = (
        P("rows", "blk", None),
        P("rows", None, "blk", None),
        P("rows", None),
        P("rows", None),
        P("rows", None),
        P("rows", None),
        P(),
        P(),
        P("blk", None),
        P(),
        P("blk", None),
        P(),
        P("blk", None),
        P(),
        P("blk", None),
        P("blk", None),
        P("blk", None),
        P("blk", None),
        P(),
        P(),
        P("rows", "blk", None),
    )
    out_specs = (
        P("rows", "blk", None),
        P("rows", "blk", None),
        P("rows", None, "blk", None),
        P(),
        P(),
        P("blk", None),
        P(),
        P("blk", None),
        P(),
        P("blk", None),
        P(),
        P("blk", None),
        P("blk", None),
        P("blk", None),
        P("blk", None),
        P(),
    )
    return jax.shard_map(
        per_device, mesh=mesh, in_specs=in_specs, out_specs=out_specs, check_vma=False
    )
```

```python
import functools

import jax
import jax.numpy as jnp
from jax import lax
from jax.experimental import pallas as pl
from jax.experimental.pallas import tpu as pltpu
from jax.sharding import PartitionSpec as P

TEAM = 4
F32, BF16 = jnp.float32, jnp.bfloat16
HIGHEST = lax.Precision.HIGHEST
GRADS, RECYCLE = 4, 5


def dot(former, latter, contract=((1,), (0,))):
    return lax.dot_general(former, latter, (contract, ((), ())), preferred_element_type=F32)


NT, TN = ((1,), (1,)), ((0,), (0,))


def normalize(values):
    center = values - jnp.mean(values, axis=-1, keepdims=True)
    inverse = lax.rsqrt(jnp.mean(center * center, axis=-1, keepdims=True) + 1e-06)
    return center * inverse, inverse


def norm_back(grad, normed, inverse):
    first = jnp.mean(grad, axis=-1, keepdims=True)
    second = jnp.mean(grad * normed, axis=-1, keepdims=True)
    return inverse * (grad - first - normed * second)


def call(kernel, grid, ins, outs, out_shape, scratch=(), micros=0, prefetch=0, mib=32):
    return pl.pallas_call(
        kernel,
        grid_spec=pltpu.PrefetchScalarGridSpec(
            num_scalar_prefetch=prefetch,
            grid=grid,
            in_specs=ins,
            out_specs=outs,
            scratch_shapes=list(scratch),
        ),
        out_shape=out_shape,
        cost_estimate=pl.CostEstimate(flops=micros * 1100000000, bytes_accessed=0, transcendentals=0),
        compiler_params=pltpu.CompilerParams(vmem_limit_bytes=mib * 1024 * 1024),
    )


def whole(shape):
    return pl.BlockSpec(shape, lambda *_: (0,) * len(shape), pipeline_mode=pl.Buffered(buffer_count=1))


def held(shape):
    return pl.BlockSpec(shape, lambda *_: (0,) * len(shape))


def pair_bias(pair_features, pairing):
    rows, q_tiles, k_tiles, width = pair_features.shape
    heads = pairing.shape[1]
    padded = jnp.pad(pairing, ((0, 0), (0, 128 - heads)))

    def kernel(pair_ref, weight_ref, out_ref, flat, turned):
        flat[...] = dot(pair_ref[0].reshape(q_tiles * k_tiles, width), weight_ref[...])
        for k in range(k_tiles):
            turned[:, k, :] = flat[pl.ds(k, q_tiles, stride=k_tiles), :].T[:heads]
        out_ref[0] = turned[...].astype(BF16)

    return call(
        kernel,
        (rows,),
        [
            pl.BlockSpec((1, q_tiles, k_tiles, width), lambda r: (r, 0, 0, 0)),
            whole((width, 128)),
        ],
        pl.BlockSpec((1, heads, k_tiles, q_tiles), lambda r: (r, 0, 0, 0)),
        jax.ShapeDtypeStruct((rows, heads, k_tiles, q_tiles), BF16),
        [pltpu.VMEM((q_tiles * k_tiles, 128), F32), pltpu.VMEM((heads, k_tiles, q_tiles), F32)],
        micros=9,
        mib=50,
    )(pair_features, padded)


def pair_back(pair_features, pairing, grad_bias, line):
    rows, q_tiles, k_tiles, width = pair_features.shape
    heads = pairing.shape[1]
    padded = jnp.pad(pairing.T, ((0, 128 - heads), (0, 0)))

    def kernel(pair_ref, weight_ref, grad_ref, line_in_ref, out_ref, line_ref, flat, sums):
        @pl.when(pl.program_id(0) == 0)
        def _():
            sums[...] = jnp.zeros_like(sums)

        grads = grad_ref[0].astype(F32)
        blank = jnp.zeros((128 - heads, q_tiles), F32)
        for k in range(k_tiles):
            piece = jnp.concatenate([grads[:, k, :], blank], axis=0)
            flat[pl.ds(k, q_tiles, stride=k_tiles), :] = piece.T
        low = flat[...].astype(BF16)
        out_ref[0] = dot(low, weight_ref[...]).astype(BF16).reshape(q_tiles, k_tiles, width)
        sums[...] += dot(low, pair_ref[0].reshape(q_tiles * k_tiles, width), TN)

        @pl.when(pl.program_id(0) == rows - 1)
        def _():
            line_ref[...] = line_in_ref[...]
            for h in range(heads):
                line_ref[GRADS : GRADS + 1, h * width : (h + 1) * width] = sums[h : h + 1, :]

    return call(
        kernel,
        (rows,),
        [
            pl.BlockSpec((1, q_tiles, k_tiles, width), lambda r: (r, 0, 0, 0)),
            whole((128, width)),
            pl.BlockSpec((1, heads, k_tiles, q_tiles), lambda r: (r, 0, 0, 0)),
            whole(line.shape),
        ],
        [pl.BlockSpec((1, q_tiles, k_tiles, width), lambda r: (r, 0, 0, 0)), held(line.shape)],
        [
            jax.ShapeDtypeStruct(pair_features.shape, BF16),
            jax.ShapeDtypeStruct(line.shape, F32),
        ],
        [pltpu.VMEM((q_tiles * k_tiles, 128), F32), pltpu.VMEM((128, width), F32)],
        micros=10,
        mib=50,
    )(pair_features, padded, grad_bias, line)


def assemble(spot, chunks, scratch):
    rows, per, tiles, _ = chunks[0].shape
    team, mine = spot[0], spot[1]
    for d, chunk in enumerate(chunks):
        for r in range(rows):
            source = lax.rem(mine + rows - r, rows)
            for j in range(per):
                start = ((j * rows + source) * TEAM + (team ^ d)) * tiles
                scratch[pl.ds(pl.multiple_of(start, tiles), tiles), :] = chunk[r, j]


def by_owner(spot, tokens, near_ref, far_ref):
    _, rows, per, tiles, _ = near_ref.shape
    for d in range(TEAM):
        for r in range(rows):
            source = lax.rem(spot[1] + r, rows)
            for j in range(per):
                start = ((j * rows + source) * TEAM + (spot[0] ^ d)) * tiles
                piece = tokens[pl.ds(pl.multiple_of(start, tiles), tiles), :]
                (far_ref if d % 2 else near_ref)[d // 2, r, j] = piece


def project_rows(begin, member, table_ref, weight_ref, bias_ref, outs, hidden_ref, width, head):
    mods = dot(member, table_ref[:, : 2 * width])
    normed, _ = normalize(begin)
    hidden = (normed * (1.0 + mods[:, width:]) + mods[:, :width]).astype(BF16)
    if hidden_ref is not None:
        hidden_ref[...] = hidden
    both = dot(hidden, weight_ref[...])
    part = both.shape[1] // 4
    low = both[:, : 3 * part].astype(BF16)
    turned = low.T
    count = part // head
    q_ref, k_ref, v_ref, key_ref, value_ref, gate_ref = outs
    q_ref[...] = (turned[:part] * BF16(head**-0.5)).reshape(count, head, -1)
    k_ref[...] = turned[part : 2 * part].reshape(count, head, -1)
    v_ref[...] = turned[2 * part :].reshape(count, head, -1)
    for h in range(count):
        key_ref[h] = low[:, part + h * head : part + (h + 1) * head]
        value_ref[h] = low[:, 2 * part + h * head : 2 * part + (h + 1) * head]
    gate_ref[...] = (both[:, 3 * part :].T + bias_ref[:, :1]).reshape(count, head, -1)


def qkv_specs(count, head, tokens, block):
    wide = pl.BlockSpec((count, head, block), lambda j, *_: (0, 0, j))
    tall = pl.BlockSpec((count, block, head), lambda j, *_: (0, j, 0))
    shapes = [jax.ShapeDtypeStruct((count, head, tokens), BF16)] * 3
    shapes += [jax.ShapeDtypeStruct((count, tokens, head), BF16)] * 2
    shapes += [jax.ShapeDtypeStruct((count, head, tokens), F32)]
    return [wide, wide, wide, tall, tall, wide], shapes


def first_rows(team, chunks, member, table, weight, gate_bias, count, head, block):
    rows, grain, tiles, width = chunks[0].shape
    tokens = rows * grain * tiles * TEAM
    per = block * grain // tokens

    def kernel(team_ref, c0, c1, c2, c3, member_ref, table_ref, weight_ref, bias_ref, row_ref, *rest):
        *outs, scratch = rest
        assemble(team_ref, (c0, c1, c2, c3), scratch)
        row_ref[...] = scratch[...]
        begin = scratch[...].astype(F32)
        project_rows(
            begin, member_ref[...], table_ref, weight_ref, bias_ref, outs, None, width, head
        )

    specs, shapes = qkv_specs(count, head, tokens, block)
    by_token = pl.BlockSpec((block, width), lambda j, *_: (j, 0))
    return call(
        kernel,
        (grain // per,),
        [pl.BlockSpec((rows, per, tiles, width), lambda j, *_: (0, j, 0, 0))] * 4
        + [
            pl.BlockSpec((block, member.shape[1]), lambda j, *_: (j, 0)),
            whole(table.shape),
            whole(weight.shape),
            whole(gate_bias.shape),
        ],
        [by_token] + specs,
        [jax.ShapeDtypeStruct((tokens, width), BF16)] + shapes,
        [pltpu.VMEM((block, width), BF16)],
        micros=8,
        mib=50,
        prefetch=1,
    )(team, *chunks, member, table, weight, gate_bias)


def begin_of(row_ref, point_ref, recycle_ref):
    return row_ref[...].astype(F32) + dot(point_ref[...].astype(BF16), recycle_ref[...], TN)


def second_rows(row, points, recycle, member, table, weight, gate_bias, count, head, block):
    tokens, width = row.shape

    def kernel(row_ref, point_ref, recycle_ref, member_ref, table_ref, weight_ref, bias_ref, hidden_ref, *outs):
        begin = begin_of(row_ref, point_ref, recycle_ref)
        project_rows(
            begin, member_ref[...], table_ref, weight_ref, bias_ref, outs, hidden_ref, width, head
        )

    specs, shapes = qkv_specs(count, head, tokens, block)
    by_token = pl.BlockSpec((block, width), lambda j: (j, 0))
    return call(
        kernel,
        (tokens // block,),
        [
            by_token,
            pl.BlockSpec((8, block), lambda j: (0, j)),
            whole(recycle.shape),
            pl.BlockSpec((block, member.shape[1]), lambda j: (j, 0)),
            whole(table.shape),
            whole(weight.shape),
            whole(gate_bias.shape),
        ],
        [by_token] + specs,
        [jax.ShapeDtypeStruct((tokens, width), BF16)] + shapes,
        micros=8,
        mib=50,
    )(row, points, recycle, member, table, weight, gate_bias)


def attend(queries, keys, values, gate, bias, q_chain, k_chain, place, tiles, block, keep):
    count, head, tokens = queries.shape
    key_tokens = keys.shape[1]
    sources = len(place)
    folds = key_tokens // block
    grain = tokens // block

    def kernel(q_ref, k_ref, v_ref, gate_ref, bias_ref, qc_ref, kc_ref, mixed_ref, *rest):
        if keep:
            attended_ref, probs_ref, share_ref, spread = rest
        else:
            (spread,) = rest

        for b in range(sources):
            spread[place[b] * tiles : (place[b] + 1) * tiles, :] = bias_ref[b, 0].astype(F32)

        def score(i):
            lanes = slice(i * block, (i + 1) * block)
            q, q_chain = q_ref[0, :, lanes], qc_ref[0:1, lanes]
            scores = []
            for f in range(folds):
                lines = slice(f * block, (f + 1) * block)
                part = f // grain
                s = dot(k_ref[0, lines, :], q) + spread[part * block : (part + 1) * block, :]
                same = jnp.concatenate([kc_ref[lines, :]] * (block // 128), axis=1) == q_chain
                scores.append(jnp.where(same, s, -1000000000.0))
            return scores

        def weigh(i, scores):
            lanes = slice(i * block, (i + 1) * block)
            top = functools.reduce(
                jnp.maximum, [jnp.max(s, axis=0, keepdims=True) for s in scores]
            )
            total = jnp.zeros((1, block), F32)
            attended = jnp.zeros((head, block), F32)
            for f in range(folds):
                lines = slice(f * block, (f + 1) * block)
                power = jnp.exp(scores[f] - top)
                total += jnp.sum(power, axis=0, keepdims=True)
                low = power.astype(BF16)
                if keep:
                    probs_ref[0, lines, lanes] = low
                attended += dot(v_ref[0, :, lines], low)
            share = 1.0 / total
            attended *= share
            mixed_ref[0, :, lanes] = (attended * jax.nn.sigmoid(gate_ref[0, :, lanes])).astype(BF16)
            if keep:
                attended_ref[0, :, lanes] = attended
                share_ref[0, :, lanes] = jnp.broadcast_to(share, (8, block))

        now = score(0)
        for i in range(grain):
            later = score(i + 1) if i + 1 < grain else None
            weigh(i, now)
            now = later

    by_head = lambda *shape: pl.BlockSpec((1,) + shape, lambda h: (h,) + (0,) * len(shape))
    outs = [by_head(head, tokens)]
    shapes = [jax.ShapeDtypeStruct((count, head, tokens), BF16)]
    if keep:
        outs += [by_head(head, tokens), by_head(key_tokens, tokens), by_head(8, tokens)]
        shapes += [
            jax.ShapeDtypeStruct((count, head, tokens), F32),
            jax.ShapeDtypeStruct((count, key_tokens, tokens), BF16),
            jax.ShapeDtypeStruct((count, 8, tokens), F32),
        ]
    return call(
        kernel,
        (count,),
        [
            by_head(head, tokens),
            by_head(key_tokens, head),
            by_head(head, key_tokens),
            by_head(head, tokens),
            pl.BlockSpec((sources, 1, tiles, block), lambda h: (0, h, 0, 0)),
            whole(q_chain.shape),
            whole(k_chain.shape),
        ],
        outs,
        shapes,
        [pltpu.VMEM((sources * tiles, block), F32)],
        micros=9 if keep else 8,
        mib=50,
    )(queries, keys, values, gate, bias, q_chain, k_chain)


def attend_back(queries, keys, value_rows, gate, attended, probs, share, own, other, place, tiles, block):
    count, head, tokens = queries.shape
    key_tokens = value_rows.shape[1]
    folds, grain = key_tokens // block, tokens // block
    sources = len(place)

    def kernel(
        q_ref, k_ref, v_ref, gate_ref, attended_ref, probs_ref, share_ref, own_ref, other_ref,
        dq_ref, dk_ref, dv_ref, logit_ref, bias_ref, bias_sum,
    ):
        grad_mixed = own_ref[0].astype(F32) + other_ref[0].astype(F32)
        sigma = jax.nn.sigmoid(gate_ref[0])
        through = grad_mixed * sigma
        upper = through.astype(BF16).astype(F32)
        attended = attended_ref[0]
        logit_ref[0] = (through * attended * (1.0 - sigma)).astype(BF16)
        share = share_ref[0, 0:1, :]
        inner = jnp.sum(upper * attended, axis=0, keepdims=True) * share
        scaled = (upper * share).astype(BF16)
        q = q_ref[0]
        grad_q = jnp.zeros((head, tokens), F32)
        tile_sums = [None] * (folds // grain)
        for f in range(folds):
            lines = slice(f * block, (f + 1) * block)
            power = probs_ref[0, lines, :]
            dv_ref[0, :, lines] = dot(scaled, power, NT).astype(BF16)
            grads = power.astype(F32) * (dot(v_ref[0, lines, :], scaled) - inner)
            low = grads.astype(BF16)
            grad_q += dot(k_ref[0, :, lines], low)
            dk_ref[0, :, lines] = dot(q, low, NT).astype(BF16)
            part = f // grain
            for i in range(grain):
                piece = grads[:, i * block : (i + 1) * block]
                tile_sums[part] = piece if tile_sums[part] is None else tile_sums[part] + piece
        dq_ref[0] = (grad_q * head**-0.5).astype(BF16)
        for part, sums in enumerate(tile_sums):
            bias_sum[part * block : (part + 1) * block, :] = sums
        for b in range(sources):
            lines = slice(place[b] * tiles, (place[b] + 1) * tiles)
            bias_ref[b, 0] = bias_sum[lines, :].astype(BF16)

    by_head = lambda *shape: pl.BlockSpec((1,) + shape, lambda h: (h,) + (0,) * len(shape))
    narrow = jax.ShapeDtypeStruct((count, head, tokens), BF16)
    broad = jax.ShapeDtypeStruct((count, head, key_tokens), BF16)
    return call(
        kernel,
        (count,),
        [
            by_head(head, tokens),
            by_head(head, key_tokens),
            by_head(key_tokens, head),
            by_head(head, tokens),
            by_head(head, tokens),
            by_head(key_tokens, tokens),
            by_head(8, tokens),
            by_head(head, tokens),
            by_head(head, tokens),
        ],
        [
            by_head(head, tokens),
            by_head(head, key_tokens),
            by_head(head, key_tokens),
            by_head(head, tokens),
            pl.BlockSpec((sources, 1, tiles, block), lambda h: (0, h, 0, 0)),
        ],
        [narrow, broad, broad, narrow, jax.ShapeDtypeStruct((sources, count, tiles, block), BF16)],
        [
            pltpu.VMEM((sources * tiles, block), F32),
        ],
        micros=10,
        mib=50,
    )(queries, keys, value_rows, gate, attended, probs, share, own, other)


def unpack(spot, bundle_refs, mixed_refs, weights, mixed, first):
    near, tail, *far = bundle_refs
    groups, _, part, wide = near.shape

    @pl.when(first)
    def _():
        mine = pl.multiple_of(spot[2] * wide, wide)
        other = pl.multiple_of((1 - spot[2]) * wide, wide)
        for g in range(groups):
            lines = slice(g * part, (g + 1) * part)
            for k in range(2):
                weights[k, lines, pl.ds(mine, wide)] = near[g, k]
                if far:
                    weights[k, lines, pl.ds(other, wide)] = far[0][g, k]
            weights[2, lines, pl.ds(mine, wide)] = tail[g, :, :wide]
            if far:
                weights[2, lines, pl.ds(other, wide)] = far[1][g]
            weights[3, lines, :] = tail[g, :, wide:]

    count, head, _ = mixed_refs[0].shape
    size = count * head
    for d, ref in enumerate(mixed_refs):
        start = pl.multiple_of((spot[0] ^ d) * size, size)
        mixed[pl.ds(start, size), :] = ref[...].reshape(size, -1)


def feed_first(team, mixed_chunks, row, member, table, bundle, coordinate, block):
    tokens, width = row.shape
    count, head, _ = mixed_chunks[0].shape

    def kernel(team_ref, m0, m1, m2, m3, row_ref, member_ref, table_ref, coord_ref, *rest):
        *bundle_refs, out_ref, weights, mixed = rest
        unpack(team_ref, bundle_refs, (m0, m1, m2, m3), weights, mixed, pl.program_id(0) == 0)
        mods = dot(member_ref[...], table_ref[:, 2 * width :])
        attend_gate, feed_shift = mods[:, :width], mods[:, width : 2 * width]
        feed_scale, feed_gate = mods[:, 2 * width : 3 * width], mods[:, 3 * width :]
        attend_out = dot(mixed[...], weights[0], TN)
        after = row_ref[...].astype(F32) + attend_gate * attend_out
        normed, _ = normalize(after)
        hidden = (normed * (1.0 + feed_scale) + feed_shift).astype(BF16)
        gate_pre, lift_pre = dot(hidden, weights[1]), dot(hidden, weights[2])
        inner = (gate_pre * jax.nn.sigmoid(gate_pre) * lift_pre).astype(BF16)
        share = after * (1.0 / TEAM) + feed_gate * dot(inner, weights[3])
        out_ref[...] = dot(coord_ref[...], share.astype(BF16), NT)

    by_token = pl.BlockSpec((block, width), lambda j, *_: (j, 0))
    return call(
        kernel,
        (tokens // block,),
        [pl.BlockSpec((count, head, block), lambda j, *_: (0, 0, j))] * 4
        + [
            by_token,
            pl.BlockSpec((block, member.shape[1]), lambda j, *_: (j, 0)),
            whole(table.shape),
            whole(coordinate.shape),
        ]
        + [whole(x.shape) for x in bundle],
        pl.BlockSpec((8, block), lambda j, *_: (0, j)),
        jax.ShapeDtypeStruct((8, tokens), F32),
        [pltpu.VMEM((4, width, width), BF16), pltpu.VMEM((width, block), BF16)],
        micros=14,
        mib=50,
        prefetch=1,
    )(team, *mixed_chunks, row, member, table, coordinate, *bundle)


def feed_both(team, mixed_chunks, row, points, recycle, cotangent, member, chains, table, bundle, block):
    tokens, width = row.shape
    count, head, _ = mixed_chunks[0].shape
    groups = bundle[0].shape[0]
    part = width // groups
    wide = bundle[0].shape[3]
    sides = width // wide
    rows, grain, tiles, _ = cotangent[0].shape
    last = tokens // block - 1
    size = count * head

    def kernel(team_ref, m0, m1, m2, m3, row_ref, point_ref, recycle_ref, c0, c1, c2, c3, member_ref, chain_ref,
               table_ref, *rest):
        bundle_refs, rest = rest[: len(bundle)], rest[len(bundle) :]
        near_out_ref, far_out_ref, after_ref, near_ref, far_ref, chain_sum_ref, down_ref = rest[:7]
        grad_refs, (weights, mixed, upstream, sums, turned) = rest[7:-5], rest[-5:]
        team = team_ref[0]
        first = pl.program_id(0) == 0
        unpack(team_ref, bundle_refs, (m0, m1, m2, m3), weights, mixed, first)
        assemble(team_ref, (c0, c1, c2, c3), upstream)

        @pl.when(first)
        def _():
            sums[...] = jnp.zeros_like(sums)
            chain_sum_ref[...] = jnp.zeros_like(chain_sum_ref)

        def work(lines):
            mods = dot(member_ref[lines, :], table_ref[:, 2 * width :])
            attend_gate, feed_shift = mods[:, :width], mods[:, width : 2 * width]
            feed_scale, feed_gate = mods[:, 2 * width : 3 * width], mods[:, 3 * width :]
            attend_out = dot(mixed[:, lines], weights[0], TN)
            yield
            after = row_ref[lines, :].astype(F32)
            after += dot(point_ref[:, lines].astype(BF16), recycle_ref[...], TN)
            after += attend_gate * attend_out
            normed, inverse = normalize(after)
            hidden = (normed * (1.0 + feed_scale) + feed_shift).astype(BF16)
            yield
            gate_pre, lift_pre = dot(hidden, weights[1]), dot(hidden, weights[2])
            yield
            sigma = jax.nn.sigmoid(gate_pre)
            silu = gate_pre * sigma
            inner = (silu * lift_pre).astype(BF16)
            yield
            branch = dot(inner, weights[3])
            g = upstream[lines, :].astype(F32)
            grad_branch = (g * feed_gate).astype(BF16)
            grad_inner = dot(grad_branch, weights[3], NT)
            yield
            upstream[lines, :] = (after * (1.0 / TEAM) + feed_gate * branch).astype(BF16)
            chain = chain_ref[:, lines]

            def by_chain(place, grad):
                lanes = slice(place * width, (place + 1) * width)
                chain_sum_ref[:, lanes] += dot(chain, grad.astype(BF16))

            by_chain(3, g * branch)
            grad_gate = grad_inner * lift_pre * sigma * (1.0 + gate_pre * (1.0 - sigma))
            grad_gate = grad_gate.astype(BF16)
            grad_lift = (grad_inner * silu).astype(BF16)
            yield
            grad_hidden = dot(grad_gate, weights[1], NT) + dot(grad_lift, weights[2], NT)
            sums[0] += dot(inner, grad_branch, TN)
            yield
            by_chain(1, grad_hidden)
            by_chain(2, grad_hidden * normed)
            grad_after = g * (1.0 / TEAM)
            grad_after += norm_back(grad_hidden * (1.0 + feed_scale), normed, inverse)
            after_ref[lines, :] = grad_after
            grad_out = (grad_after * attend_gate).astype(BF16)
            yield
            sums[1] += dot(hidden, grad_gate, TN)
            sums[2] += dot(hidden, grad_lift, TN)
            turned[:, lines] = dot(grad_out, weights[0], NT).T.astype(BF16)
            yield
            sums[3] += dot(mixed[:, lines], grad_out)
            by_chain(0, grad_after * attend_out)

        todo = [work(slice(h * block // 2, (h + 1) * block // 2)) for h in range(2)]
        while todo:
            todo = [x for x in todo if next(x, todo) is None]
        by_owner(team_ref, upstream, near_out_ref, far_out_ref)
        for d in range(TEAM):
            start = pl.multiple_of((team ^ d) * size, size)
            piece = turned[pl.ds(start, size), :].reshape(count, head, block)
            (far_ref if d % 2 else near_ref)[d // 2] = piece

        @pl.when(pl.program_id(0) == last)
        def _():
            for g in range(groups):
                lines = slice(g * part, (g + 1) * part)
                down_ref[g] = sums[0, lines, :].astype(BF16)
                for side, ref in enumerate(grad_refs):
                    start = pl.multiple_of((team_ref[2] ^ side) * wide, wide)
                    for k in range(3):
                        ref[g, k] = sums[1 + k, lines, pl.ds(start, wide)].astype(BF16)

    by_token = pl.BlockSpec((block, width), lambda j, *_: (j, 0))
    by_lane = pl.BlockSpec((8, block), lambda j, *_: (0, j))
    owned = pl.BlockSpec((2, rows, block * grain // tokens, tiles, width), lambda j, *_: (0, 0, j, 0, 0))
    halves = pl.BlockSpec((2, count, head, block), lambda j, *_: (0, 0, 0, j))
    half = jax.ShapeDtypeStruct((2, count, head, tokens), BF16)
    return call(
        kernel,
        (tokens // block,),
        [pl.BlockSpec((count, head, block), lambda j, *_: (0, 0, j))] * 4
        + [by_token, by_lane, whole(recycle.shape)]
        + [pl.BlockSpec((rows, block * grain // tokens, tiles, width), lambda j, *_: (0, j, 0, 0))] * 4
        + [
            pl.BlockSpec((block, member.shape[1]), lambda j, *_: (j, 0)),
            by_lane,
            whole(table.shape),
        ]
        + [whole(x.shape) for x in bundle],
        [owned, owned, by_token, halves, halves, held((8, 4 * width)), held((groups, part, width))]
        + [held((groups, 3, part, wide))] * sides,
        [
            jax.ShapeDtypeStruct((2, rows, grain, tiles, width), BF16),
            jax.ShapeDtypeStruct((2, rows, grain, tiles, width), BF16),
            jax.ShapeDtypeStruct((tokens, width), F32),
            half,
            half,
            jax.ShapeDtypeStruct((8, 4 * width), F32),
            jax.ShapeDtypeStruct((groups, part, width), BF16),
        ]
        + [jax.ShapeDtypeStruct((groups, 3, part, wide), BF16)] * sides,
        [
            pltpu.VMEM((4, width, width), BF16),
            pltpu.VMEM((width, block), BF16),
            pltpu.VMEM((block, width), BF16),
            pltpu.VMEM((4, width, width), F32),
            pltpu.VMEM((width, block), BF16),
        ],
        micros=33,
        mib=56,
        prefetch=1,
    )(team, *mixed_chunks, row, points, recycle, *cotangent, member, chains, table, *bundle)


def finish(spot, hidden, row, points, recycle, grad_after, grads, member, chains, chain_feed, table, weight, slot, rows, tiles, groups, sides, block):
    tokens, width = row.shape
    count, head, _ = grads[0].shape
    size = count * head
    part = width // groups
    wide = 4 * size // sides
    last = tokens // block - 1
    coords = 3
    grain = tokens // (rows * TEAM * tiles)
    per = block * grain // tokens

    def kernel(spot_ref, hidden_ref, row_ref, point_ref, recycle_ref, after_ref, q_ref, k_ref, v_ref, gate_ref,
               member_ref, chain_ref, feed_ref, table_ref, weight_ref,
               near_ref, far_ref, line_ref, *rest):
        *sum_refs, sums, owners, chain_sum_ref, recycle_sum_ref, gate_sum_ref = rest
        first = pl.program_id(0) == 0

        @pl.when(first)
        def _():
            sums[...] = jnp.zeros_like(sums)
            chain_sum_ref[...] = jnp.zeros_like(chain_sum_ref)
            recycle_sum_ref[...] = jnp.zeros_like(recycle_sum_ref)
            gate_sum_ref[...] = jnp.zeros_like(gate_sum_ref)

        stacked = jnp.concatenate(
            [ref[...].reshape(size, block) for ref in (q_ref, k_ref, v_ref, gate_ref)], axis=0
        )
        low = stacked.T
        gate_sum_ref[...] += jnp.sum(low[:, 3 * size :].astype(F32), axis=0, keepdims=True)
        sums[...] += dot(hidden_ref[...], low, TN)
        grad_hidden = dot(low, weight_ref[...], NT)
        mods = dot(member_ref[...], table_ref[:, width : 2 * width])
        normed, inverse = normalize(begin_of(row_ref, point_ref, recycle_ref))
        chain = chain_ref[...]
        chain_sum_ref[:, :width] += dot(chain, grad_hidden.astype(BF16))
        chain_sum_ref[:, width:] += dot(chain, (grad_hidden * normed).astype(BF16))
        grad = after_ref[...] + norm_back(grad_hidden * (1.0 + mods), normed, inverse)
        low_grad = grad.astype(BF16)
        owners[...] = low_grad
        by_owner(spot_ref, owners, near_ref, far_ref)
        recycle_sum_ref[...] += dot(point_ref[...].astype(BF16), low_grad)

        @pl.when(pl.program_id(0) == last)
        def _():
            line_ref[...] = jnp.zeros_like(line_ref)
            line_ref[:, : 2 * width] = chain_sum_ref[...]
            line_ref[:, 2 * width :] = feed_ref[...]
            for k in range(coords):
                lanes = slice(k * width, (k + 1) * width)
                line_ref[RECYCLE : RECYCLE + 1, lanes] = recycle_sum_ref[k : k + 1, :]
            start = pl.multiple_of(slot + spot_ref[0] * 256, 256)
            line_ref[GRADS : GRADS + 1, pl.ds(start, size)] = gate_sum_ref[...]
            for side, ref in enumerate(sum_refs):
                start = pl.multiple_of((spot_ref[2] ^ side) * wide, wide)
                for g in range(groups):
                    ref[g] = sums[g * part : (g + 1) * part, pl.ds(start, wide)].astype(BF16)

    by_token = pl.BlockSpec((block, width), lambda j, *_: (j, 0))
    by_lane = pl.BlockSpec((8, block), lambda j, *_: (0, j))
    by_query = pl.BlockSpec((count, head, block), lambda j, *_: (0, 0, j))
    owned = pl.BlockSpec((2, rows, per, tiles, width), lambda j, *_: (0, 0, j, 0, 0))
    return call(
        kernel,
        (tokens // block,),
        [by_token, by_token, by_lane, whole(recycle.shape), by_token]
        + [by_query] * 4
        + [
            pl.BlockSpec((block, member.shape[1]), lambda j, *_: (j, 0)),
            by_lane,
            whole(chain_feed.shape),
            whole(table.shape),
            whole(weight.shape),
        ],
        [
            owned,
            owned,
            held((8, 6 * width)),
        ]
        + [held((groups, part, wide))] * sides,
        [
            jax.ShapeDtypeStruct((2, rows, grain, tiles, width), BF16),
            jax.ShapeDtypeStruct((2, rows, grain, tiles, width), BF16),
            jax.ShapeDtypeStruct((8, 6 * width), F32),
        ]
        + [jax.ShapeDtypeStruct((groups, part, wide), BF16)] * sides,
        [
            pltpu.VMEM((width, 4 * size), F32),
            pltpu.VMEM((block, width), BF16),
            pltpu.VMEM((8, 2 * width), F32),
            pltpu.VMEM((8, width), F32),
            pltpu.VMEM((1, size), F32),
        ],
        micros=12,
        mib=50,
        prefetch=1,
    )(spot, hidden, row, points, recycle, grad_after, *grads, member, chains, chain_feed, table, weight)


def to_slots(spot, *kinds):
    rows, many = len(kinds[0]), len(kinds)
    grain, tiles, width = kinds[0][0].shape
    local = grain * tiles

    def kernel(spot_ref, *refs):
        inputs, outs, spread = refs[: many * rows], refs[many * rows : -1], refs[-1]
        for k in range(many):
            for d in range(rows):
                row = lax.rem(spot_ref[1] + rows - d, rows)
                for c in range(width // 128):
                    lanes = slice(c * 128, (c + 1) * 128)
                    for j in range(grain):
                        piece = inputs[k * rows + d][j, :, lanes].astype(F32)
                        spread[c, pl.ds(j, tiles, stride=grain), :] = piece
                    outs[k][pl.ds(row, 1), :, lanes] = spread[c].astype(BF16)[None]

    return call(
        kernel,
        (1,),
        [whole((grain, tiles, width))] * (many * rows),
        [held((rows, local, width))] * many,
        [jax.ShapeDtypeStruct((rows, local, width), BF16)] * many,
        [pltpu.VMEM((width // 128, local, 128), F32)],
        micros=2,
        mib=50,
        prefetch=1,
    )(spot, *[x for kind in kinds for x in kind])


def chain_products(spot, lines, weights, modulate, first):
    many, long = lines[0].shape
    count = len(lines)
    width = modulate.shape[0]

    def kernel(spot_ref, *refs):
        line_refs, (weight_ref, modulate_ref, first_ref, rest_ref, back_ref) = refs[:count], refs[count:]
        total = None
        for n, ref in enumerate(line_refs):
            part = dot(weight_ref[n], ref[...])
            total = part if total is None else total + part
            group = lax.rem(spot_ref[3] + count - n, count)
            back_ref[pl.ds(group, 1)] = dot(ref[...], modulate_ref[...], NT)[None]
        first_ref[...] = total[:first]
        rest_ref[...] = total[first:]

    rest = weights.shape[1] - first
    return call(
        kernel,
        (1,),
        [whole((many, long))] * count + [whole(weights.shape), whole(modulate.shape)],
        [held((first, long)), held((rest, long)), held((count, many, width))],
        [
            jax.ShapeDtypeStruct((first, long), F32),
            jax.ShapeDtypeStruct((rest, long), F32),
            jax.ShapeDtypeStruct((count, many, width), F32),
        ],
        micros=5,
        mib=50,
        prefetch=1,
    )(spot, *lines, weights, modulate)


def per_device(
    residues,
    pair_features,
    chain_lengths,
    time_bins,
    fold_class,
    self_flag,
    time_table,
    class_table,
    modulate,
    offset,
    heads,
    pairing,
    gating,
    gating_bias,
    project,
    widen_gate,
    widen_up,
    narrow,
    coordinate,
    recycle,
    cotangent,
):
    blocks = lax.axis_size("blk")
    planes = lax.axis_size("rows")
    myself = lax.axis_index("blk")
    rows, local, width = residues.shape
    row_len = local * blocks
    grain = row_len // pair_features.shape[1]
    tiles = local // grain
    head_count = pairing.shape[1]
    head = width // head_count
    count = head_count // TEAM
    size = count * head
    span = blocks // rows
    parts = span // TEAM
    groups = blocks // TEAM
    tokens = row_len // parts
    block = tokens // grain
    max_chains = chain_lengths.shape[1]
    my_row = myself // span
    my_part = (myself % span) // TEAM
    team = myself % TEAM
    sides = 2 if planes % 2 == 0 else 1
    my_side = lax.axis_index("rows") % sides
    team_ref = jnp.stack([team, my_row, my_side, myself // TEAM]).astype(jnp.int32)
    place = []
    for b in range(blocks):
        r, u, t = b // span, (b % span) // TEAM, b % TEAM
        place.append((u * rows + r) * TEAM + t)

    row_groups = [[r * span + s for r in range(rows)] for s in range(span)]
    same_team = [[g * TEAM + t for g in range(groups)] for t in range(TEAM)]
    teams = [[g * TEAM + t for t in range(TEAM)] for g in range(groups)]
    part_groups = [
        [r * span + u * TEAM + t for u in range(parts)] for r in range(rows) for t in range(TEAM)
    ]

    def swap(x, k):
        return lax.ppermute(x, "blk", [(b, b ^ k) for b in range(blocks)])

    def team_gather(x):
        far = swap(x, 2)
        return x, swap(x, 1), far, swap(far, 1)

    def group_sum(x):
        k = 1
        while k < span:
            x = x + swap(x, k)
            k *= 2
        return x

    def exchange(x, members=None):
        return lax.all_to_all(x, "blk", 0, 0, tiled=True, axis_index_groups=members)

    def pick(x, d):
        return lax.dynamic_index_in_dim(x, team ^ d, 0, False)

    def ordered(x):
        x = list(x)
        for bit in (1, 2):
            moved = (team & bit) != 0
            x = [jnp.where(moved, x[d ^ bit], x[d]) for d in range(TEAM)]
        return x

    def across(x):
        return lax.ppermute(x, "rows", [(p, p ^ 1) for p in range(planes)])

    def my_half(x, axis, other=0):
        wide = x.shape[axis] // sides
        return lax.dynamic_slice_in_dim(x, (my_side ^ other) * wide, wide, axis)

    def unite(x, axis):
        if sides == 1:
            return x
        y = across(x)
        return jnp.concatenate([jnp.where(my_side == 0, x, y), jnp.where(my_side == 0, y, x)], axis)

    def add_planes(x):
        if planes > 2:
            x = lax.psum(x, "rows", axis_index_groups=[list(range(p, planes, 2)) for p in range(2)])
        return x

    def pair_sum(x):
        if sides == 1:
            return x[0]
        return (x[0].astype(F32) + across(x[1]).astype(F32)).astype(BF16)

    def scatter(x):
        x = lax.psum_scatter(
            x, "blk", scatter_dimension=0, axis_index_groups=same_team, tiled=True
        )
        return add_planes(x)

    def after(x, *others):
        return lax.optimization_barrier((x, *others))[0]

    def row_shift(x):
        found = [lax.dynamic_index_in_dim(x, my_row, 0, False)]
        for d in range(1, rows):
            piece = lax.dynamic_index_in_dim(x, (my_row + d) % rows, 0, False)
            pairs = [(b, (b + d * span) % blocks) for b in range(blocks)]
            found.append(lax.ppermute(piece, "blk", pairs))
        return found

    def fold(x):
        return x.reshape(rows, tiles, grain, width).transpose(0, 2, 1, 3)

    depth = heads.shape[0]
    attend_w = jnp.concatenate(
        [heads.reshape(depth, 3, TEAM, size), gating.reshape(depth, 1, TEAM, size)], axis=1
    )
    attend_w = my_half(attend_w.transpose(2, 0, 1, 3).reshape(TEAM, depth, 4 * size), 1)
    attend_w = jnp.broadcast_to(attend_w[None], (groups,) + attend_w.shape)
    attend_w = exchange(attend_w.reshape(blocks, depth // sides, 4 * size))

    units = narrow.shape[0]
    widen = jnp.stack([widen_gate, widen_up], axis=0).reshape(2, depth, groups, TEAM, units)
    widen = my_half(widen, 2).transpose(3, 0, 1, 2, 4).reshape(TEAM, 2, depth, width // sides)
    out_w = my_half(project, 1)[None]
    widen = [pick(widen, d) for d in range(TEAM)]
    widen = [widen[0]] + [swap(widen[d], d) for d in range(1, TEAM)]
    widen = jnp.stack(ordered(widen), axis=1).reshape(2, TEAM * depth, width // sides)
    out_w = jnp.stack(ordered(team_gather(out_w)), axis=1).reshape(1, TEAM * depth, width // sides)
    def gather(x):
        return lax.all_gather(x, "blk", axis=0, axis_index_groups=same_team)

    first_bundle = jnp.concatenate([out_w, widen[:1]], axis=0)
    bundle = [gather(first_bundle)]
    bundle.append(gather(jnp.concatenate([widen[1], narrow], axis=1)))
    if sides == 2:
        bundle += [across(bundle[0]), across(bundle[1][:, :, : width // sides])]

    tile_bias = pair_bias(pair_features, after(pairing, first_bundle))

    hot = lambda ids, n: (ids[:, :, None] == jnp.arange(n, dtype=jnp.int32)).astype(F32)
    ids = jnp.concatenate([time_bins, fold_class], axis=1)
    if planes == 2:
        ids = jnp.concatenate([ids, across(ids)], axis=0)
    time_hot = hot(ids[:, :max_chains], time_table.shape[0])
    class_hot = hot(ids[:, max_chains:], class_table.shape[0])
    condition = jnp.einsum(
        "rcn,nd->rcd", time_hot, time_table.astype(F32), precision=HIGHEST
    ) + jnp.einsum("rcn,nd->rcd", class_hot, class_table.astype(F32), precision=HIGHEST)
    smooth = jax.nn.silu(condition).astype(BF16)
    cond_local = modulate.shape[0]
    my_smooth = lax.dynamic_slice_in_dim(smooth, myself * cond_local, cond_local, axis=2)
    per_chain = jnp.einsum("rcd,dm->rcm", my_smooth[:rows], modulate, preferred_element_type=F32)
    upper = lax.reduce_precision(per_chain, 8, 7)
    both = jnp.stack([upper, per_chain - upper], axis=1).astype(BF16).reshape(rows, -1, width)
    moved = jnp.stack(row_shift(jnp.concatenate([fold(residues).reshape(rows, local, width), both], axis=1)))
    moved = after(moved, tile_bias)
    row_chunks = team_gather(moved[:, :local].reshape(rows, grain, tiles, width))
    per_chain = moved[:, local:].reshape(2 * rows, max_chains, 6 * width).astype(F32)
    per_chain = group_sum(jnp.sum(per_chain, axis=0)) + offset.astype(F32)
    upper = lax.reduce_precision(per_chain, 8, 7)
    table = jnp.concatenate(
        [upper, per_chain - upper, jnp.zeros((16 - 2 * max_chains, per_chain.shape[1]), F32)],
        axis=0,
    ).astype(BF16)

    bias_out = tile_bias.reshape(rows, TEAM, count, tiles, rows, parts, TEAM * tiles)
    bias_out = bias_out.transpose(0, 5, 1, 2, 3, 4, 6).reshape(blocks, count, tiles, block)
    attend_w = unite(attend_w, 1).reshape(width, 4 * size)
    bias = exchange(after(bias_out, attend_w))

    ends = jnp.cumsum(lax.dynamic_index_in_dim(chain_lengths, my_row, 0, False))
    flags = lax.dynamic_index_in_dim(self_flag, my_row, 0, False)

    def slots(part):
        r = jnp.arange(rows, dtype=jnp.int32)[None, :, None, None]
        t = jnp.arange(TEAM, dtype=jnp.int32)[None, None, :, None]
        j = jnp.arange(grain, dtype=jnp.int32)[:, None, None, None]
        a = jnp.arange(tiles, dtype=jnp.int32)[None, None, None, :]
        return (((r * span + part * TEAM + t) * tiles + a) * grain + j).reshape(tokens)

    def chain_of(places):
        return jnp.sum((places[:, None] >= ends[None, :]).astype(jnp.int32), axis=1)

    q_chain = chain_of(slots(my_part))
    k_chain = chain_of(jnp.concatenate([slots(u) for u in range(parts)]))
    q_lines = jnp.broadcast_to(q_chain[None, :], (8, tokens))
    k_lines = jnp.broadcast_to(k_chain[:, None], (parts * tokens, 128))
    ids = jnp.arange(16, dtype=jnp.int32)
    ids = jnp.where(ids < 2 * max_chains, ids % max_chains, -1)
    member = (q_chain[:, None] == ids[None, :]).astype(BF16)
    chain_hot = q_chain[None, :] == jnp.arange(8, dtype=jnp.int32)[:, None]
    chains = chain_hot.astype(BF16)
    flag_lines = jnp.sum(
        jnp.where(chain_hot[:max_chains], flags.astype(F32)[:, None], 0.0), axis=0, keepdims=True
    )
    gate_bias = lax.dynamic_slice_in_dim(gating_bias, team * size, size).astype(F32)
    gate_bias = jnp.broadcast_to(gate_bias[:, None], (size, 128))
    points_w = jnp.pad(coordinate.T, ((0, 8 - coordinate.shape[1]), (0, 0)))
    recycle_w = jnp.pad(recycle, ((0, 8 - recycle.shape[0]), (0, 0)))

    def all_keys(keys, values):
        if parts == 1:
            return keys, values
        keys = lax.all_gather(keys, "blk", axis=0, axis_index_groups=part_groups)
        values = lax.all_gather(values, "blk", axis=0, axis_index_groups=part_groups)
        keys = keys.transpose(1, 0, 2, 3).reshape(count, parts * tokens, head)
        values = values.transpose(1, 2, 0, 3).reshape(count, head, parts * tokens)
        return keys, values

    row, q_one, _, v_one, key_one, _, gate_one = first_rows(
        team_ref, row_chunks, member, table, attend_w, gate_bias, count, head, tokens // 2
    )
    key_one, v_one = all_keys(key_one, v_one)
    upstream = jnp.stack(row_shift(fold(after(cotangent, row))))
    q_lines_one = after(q_lines, bundle[-sides])
    (mixed_one,) = attend(q_one, key_one, v_one, gate_one, bias, q_lines_one, k_lines, place, tiles, block, False)
    mixed_one = team_gather(after(mixed_one, bundle[1]))
    shares = feed_first(
        team_ref, mixed_one, row, member, table, bundle, points_w, tokens // 2
    )
    shares = shares + swap(shares, 1)
    shares = shares + swap(shares, 2)
    points = lax.reduce_precision(shares, 8, 7) * flag_lines

    views = 2 if planes == 2 else 1
    which = [(myself // TEAM + groups - d) % groups // parts for d in range(groups)]
    smooth_rows = smooth.reshape(views, rows, max_chains, -1)
    weights = jnp.stack([lax.dynamic_index_in_dim(smooth_rows, r, 1, False) for r in which])
    weights = jnp.pad(weights, ((0, 0), (0, 0), (0, 8 - max_chains), (0, 0)))
    weights = lax.dynamic_slice_in_dim(weights, myself * cond_local, cond_local, axis=3)
    weights = weights.reshape(groups, views * 8, cond_local)
    kind = jnp.arange(views * 8) % 8
    masks = jnp.stack([kind < max_chains, kind == GRADS, kind == RECYCLE], axis=1).astype(BF16)
    masks = jnp.broadcast_to(masks[None], (groups,) + masks.shape)
    weights = jnp.concatenate([weights, masks], axis=2).transpose(0, 2, 1)
    weights = jnp.pad(weights, ((0, 0), (0, -weights.shape[1] % 8), (0, 0)))

    modulate_full = lax.all_gather(after(modulate, row), "blk", axis=0, tiled=True)
    hidden, q_two, k_two, v_two, key_two, value_two, gate_two = second_rows(
        row, points, after(recycle_w, modulate_full, upstream, weights), member, table, attend_w, gate_bias, count, head, tokens // 2
    )
    key_two, v_all = all_keys(key_two, v_two)
    value_two, k_two = all_keys(value_two, k_two)
    mixed_two, attended, probs, share = attend(
        q_two, key_two, v_all, gate_two, bias, q_lines, k_lines, place, tiles, block, True
    )
    far = swap(after(upstream, points), 2)
    upstream = upstream, swap(upstream, 1), far, swap(after(far, q_two), 1)
    result_near, result_far, grad_after, near, far, chain_feed, down_grads, *feed_grads = feed_both(
        team_ref, team_gather(after(mixed_two, upstream[3])), row, points, recycle_w, upstream, member, chains, table,
        bundle, tokens // 2,
    )

    def near_sum(near, far):
        return (near.astype(F32) + swap(far, 1).astype(F32)).astype(BF16)

    def owner_shift(both, far):
        total = (both[0].astype(F32) + far.astype(F32)).astype(BF16)
        found = [total[0]]
        for d in range(1, rows):
            pairs = [(b, (b + d * span) % blocks) for b in range(blocks)]
            found.append(lax.ppermute(total[d], "blk", pairs))
        return found

    halves = (near.astype(F32) + swap(far, 1).astype(F32)).astype(BF16)
    other_half = swap(halves[1], 2)
    result_both = near_sum(result_near, after(result_far, halves))
    grad_q, grad_k, grad_v, grad_logit, bias_grad = attend_back(
        q_two, k_two, value_two, gate_two, attended, probs, share, halves[0], other_half, place, tiles, block
    )
    result_shift = owner_shift(result_both, swap(after(result_both[1], other_half), 2))
    bias_grad = exchange(bias_grad)
    if parts > 1:
        key_value = jnp.stack([grad_k, grad_v]).reshape(2, count, head, parts, tokens)
        key_value = lax.psum_scatter(
            key_value.transpose(3, 0, 1, 2, 4), "blk", scatter_dimension=0, axis_index_groups=part_groups
        )
        grad_k, grad_v = key_value[0], key_value[1]
    feed_grads = pair_sum(feed_grads)
    down_own = scatter(down_grads)[0]
    wide_own = scatter(feed_grads)[0].reshape(3, TEAM, depth, width // sides)
    gate_slot = head_count * pair_features.shape[3]
    begin_near, begin_far, line, *attend_grads = finish(
        team_ref, hidden, row, points, recycle_w, grad_after, (grad_q, grad_k, grad_v, grad_logit), member, chains, chain_feed,
        table, attend_w, gate_slot, rows, tiles, groups, sides, block,
    )

    stage = lax.optimization_barrier
    both = near_sum(begin_near, after(begin_far, bias_grad, result_shift))
    both_far = swap(both[1], 2)
    bias_grad = bias_grad.reshape(rows, parts, TEAM, count, tiles, rows, TEAM * tiles)
    bias_grad = bias_grad.transpose(0, 2, 3, 4, 5, 1, 6).reshape(rows, head_count, tiles, parts * block)
    grad_pair, line = pair_back(pair_features, pairing, after(bias_grad, both), line)
    attend_far = across(attend_grads[1]) if sides == 2 else attend_grads[0]
    line, attend_far, both_far, down_own = stage((line, attend_far, both_far, down_own))
    attend_own = attend_grads[0]
    if sides == 2:
        attend_own = (attend_own.astype(F32) + attend_far.astype(F32)).astype(BF16)
    attend_own = exchange(attend_own.reshape(blocks, depth, 4 * size // sides))

    line = line + swap(line, 1)
    line_far = swap(line, 2)
    by_shift = owner_shift(both, both_far)
    line = (line + line_far).astype(BF16)
    line_far = across(line) if planes == 2 else line
    line_far, wide_own = stage((line_far, wide_own))
    if planes == 2:
        line = jnp.concatenate([line, line_far], axis=0)
    lines = [line]
    for d in range(1, groups):
        pairs = [(b, (b + d * TEAM) % blocks) for b in range(blocks)]
        lines.append(lax.ppermute(line, "blk", pairs))
    wide = exchange(after(wide_own, attend_own).transpose(1, 0, 2, 3), teams)
    attend_own, wide, by_shift, lines = stage((attend_own, wide, by_shift, lines))

    inner = jnp.sum(attend_own.astype(F32).reshape(groups, TEAM, depth, 4 // sides, size), axis=0)
    inner = add_planes(inner.astype(BF16)).transpose(1, 2, 0, 3).reshape(depth, 4 * width // sides)
    inner = unite(inner, 1).astype(F32)
    if planes == 2:
        grad_narrow = down_own.astype(F32) + across(down_own).astype(F32)
    else:
        grad_narrow = lax.psum(down_own, "rows").astype(F32)
    own_project = jnp.sum(wide[:, 2].astype(F32), axis=0).astype(BF16)
    wide = wide[:, :2].reshape(TEAM, 2, depth, groups // sides, units).transpose(1, 2, 3, 0, 4)
    wide = unite(wide.reshape(2, depth, TEAM * width // sides), 2).astype(F32)
    grad_project = unite(own_project, 1).astype(F32)

    layer_out, grad_residues = to_slots(team_ref, result_shift, by_shift)

    grad_modulate, sums, back = chain_products(team_ref, lines, weights, modulate_full, cond_local)
    grad_offset = sums[0]
    grad_pairing = sums[1, :gate_slot].reshape(head_count, -1).T
    grad_gatebias = sums[1, gate_slot : gate_slot + 256 * TEAM].reshape(TEAM, 256)[:, :size].reshape(width)
    grad_recycle = sums[2, : recycle.size].reshape(recycle.shape)
    grad_smooth = back.reshape(rows, parts, views, 8, -1)[:, :, :, :max_chains].sum(axis=1)
    grad_smooth = grad_smooth.transpose(1, 0, 2, 3).reshape(views * rows, max_chains, -1)
    sigma = jax.nn.sigmoid(condition)
    grad_condition = grad_smooth * sigma * (1.0 + condition * (1.0 - sigma))
    grad_time = jnp.einsum("rcn,rcd->nd", time_hot, grad_condition, precision=HIGHEST)
    grad_class = jnp.einsum("rcn,rcd->nd", class_hot, grad_condition, precision=HIGHEST)
    if planes != 2:
        found = (grad_time, grad_class, grad_modulate, grad_offset, grad_pairing, grad_gatebias, grad_recycle)
        found = lax.psum(found, "rows")
        grad_time, grad_class, grad_modulate, grad_offset, grad_pairing, grad_gatebias, grad_recycle = found
    return (
        layer_out,
        grad_residues,
        grad_pair,
        grad_time,
        grad_class,
        grad_modulate,
        grad_offset,
        inner[:, : 3 * width],
        grad_pairing,
        inner[:, 3 * width :],
        grad_gatebias,
        grad_project,
        wide[0],
        wide[1],
        grad_narrow,
        grad_recycle,
    )


def solution(mesh):
    in_specs = (
        P("rows", "blk", None),
        P("rows", None, "blk", None),
        P("rows", None),
        P("rows", None),
        P("rows", None),
        P("rows", None),
        P(),
        P(),
        P("blk", None),
        P(),
        P("blk", None),
        P(),
        P("blk", None),
        P(),
        P("blk", None),
        P("blk", None),
        P("blk", None),
        P("blk", None),
        P(),
        P(),
        P("rows", "blk", None),
    )
    out_specs = (
        P("rows", "blk", None),
        P("rows", "blk", None),
        P("rows", None, "blk", None),
        P(),
        P(),
        P("blk", None),
        P(),
        P("blk", None),
        P(),
        P("blk", None),
        P(),
        P("blk", None),
        P("blk", None),
        P("blk", None),
        P("blk", None),
        P(),
    )
    return jax.shard_map(
        per_device, mesh=mesh, in_specs=in_specs, out_specs=out_specs, check_vma=False
    )
```

```python
import functools

import jax
import jax.numpy as jnp
from jax import lax
from jax.experimental import pallas as pl
from jax.experimental.pallas import tpu as pltpu
from jax.sharding import PartitionSpec as P

TEAM = 4
F32, BF16 = jnp.float32, jnp.bfloat16
HIGHEST = lax.Precision.HIGHEST
GRADS, RECYCLE = 4, 5


def dot(former, latter, contract=((1,), (0,))):
    return lax.dot_general(former, latter, (contract, ((), ())), preferred_element_type=F32)


NT, TN = ((1,), (1,)), ((0,), (0,))


def normalize(values):
    center = values - jnp.mean(values, axis=-1, keepdims=True)
    inverse = lax.rsqrt(jnp.mean(center * center, axis=-1, keepdims=True) + 1e-06)
    return center * inverse, inverse


def norm_back(grad, normed, inverse):
    first = jnp.mean(grad, axis=-1, keepdims=True)
    second = jnp.mean(grad * normed, axis=-1, keepdims=True)
    return inverse * (grad - first - normed * second)


def call(kernel, grid, ins, outs, out_shape, scratch=(), micros=0, prefetch=0, mib=32):
    return pl.pallas_call(
        kernel,
        grid_spec=pltpu.PrefetchScalarGridSpec(
            num_scalar_prefetch=prefetch,
            grid=grid,
            in_specs=ins,
            out_specs=outs,
            scratch_shapes=list(scratch),
        ),
        out_shape=out_shape,
        cost_estimate=pl.CostEstimate(flops=micros * 1100000000, bytes_accessed=0, transcendentals=0),
        compiler_params=pltpu.CompilerParams(vmem_limit_bytes=mib * 1024 * 1024),
    )


def whole(shape):
    return pl.BlockSpec(shape, lambda *_: (0,) * len(shape), pipeline_mode=pl.Buffered(buffer_count=1))


def held(shape):
    return pl.BlockSpec(shape, lambda *_: (0,) * len(shape))


def pair_bias(pair_features, pairing):
    rows, q_tiles, k_tiles, width = pair_features.shape
    heads = pairing.shape[1]
    padded = jnp.pad(pairing, ((0, 0), (0, 128 - heads)))

    def kernel(pair_ref, weight_ref, out_ref, flat, turned):
        flat[...] = dot(pair_ref[0].reshape(q_tiles * k_tiles, width), weight_ref[...])
        for k in range(k_tiles):
            turned[:, k, :] = flat[pl.ds(k, q_tiles, stride=k_tiles), :].T[:heads]
        out_ref[0] = turned[...].astype(BF16)

    return call(
        kernel,
        (rows,),
        [
            pl.BlockSpec((1, q_tiles, k_tiles, width), lambda r: (r, 0, 0, 0)),
            whole((width, 128)),
        ],
        pl.BlockSpec((1, heads, k_tiles, q_tiles), lambda r: (r, 0, 0, 0)),
        jax.ShapeDtypeStruct((rows, heads, k_tiles, q_tiles), BF16),
        [pltpu.VMEM((q_tiles * k_tiles, 128), F32), pltpu.VMEM((heads, k_tiles, q_tiles), F32)],
        micros=9,
        mib=50,
    )(pair_features, padded)


def pair_back(pair_features, pairing, grad_bias, line):
    rows, q_tiles, k_tiles, width = pair_features.shape
    heads = pairing.shape[1]
    padded = jnp.pad(pairing.T, ((0, 128 - heads), (0, 0)))

    def kernel(pair_ref, weight_ref, grad_ref, line_in_ref, out_ref, line_ref, flat, sums):
        @pl.when(pl.program_id(0) == 0)
        def _():
            sums[...] = jnp.zeros_like(sums)

        grads = grad_ref[0].astype(F32)
        blank = jnp.zeros((128 - heads, q_tiles), F32)
        for k in range(k_tiles):
            piece = jnp.concatenate([grads[:, k, :], blank], axis=0)
            flat[pl.ds(k, q_tiles, stride=k_tiles), :] = piece.T
        low = flat[...].astype(BF16)
        out_ref[0] = dot(low, weight_ref[...]).astype(BF16).reshape(q_tiles, k_tiles, width)
        sums[...] += dot(low, pair_ref[0].reshape(q_tiles * k_tiles, width), TN)

        @pl.when(pl.program_id(0) == rows - 1)
        def _():
            line_ref[...] = line_in_ref[...]
            for h in range(heads):
                line_ref[GRADS : GRADS + 1, h * width : (h + 1) * width] = sums[h : h + 1, :]

    return call(
        kernel,
        (rows,),
        [
            pl.BlockSpec((1, q_tiles, k_tiles, width), lambda r: (r, 0, 0, 0)),
            whole((128, width)),
            pl.BlockSpec((1, heads, k_tiles, q_tiles), lambda r: (r, 0, 0, 0)),
            whole(line.shape),
        ],
        [pl.BlockSpec((1, q_tiles, k_tiles, width), lambda r: (r, 0, 0, 0)), held(line.shape)],
        [
            jax.ShapeDtypeStruct(pair_features.shape, BF16),
            jax.ShapeDtypeStruct(line.shape, F32),
        ],
        [pltpu.VMEM((q_tiles * k_tiles, 128), F32), pltpu.VMEM((128, width), F32)],
        micros=10,
        mib=50,
    )(pair_features, padded, grad_bias, line)


def assemble(spot, chunks, scratch):
    rows, per, tiles, _ = chunks[0].shape
    team, mine = spot[0], spot[1]
    for d, chunk in enumerate(chunks):
        for r in range(rows):
            source = lax.rem(mine + rows - r, rows)
            for j in range(per):
                start = ((j * rows + source) * TEAM + (team ^ d)) * tiles
                scratch[pl.ds(pl.multiple_of(start, tiles), tiles), :] = chunk[r, j]


def by_owner(spot, tokens, near_ref, far_ref):
    _, rows, per, tiles, _ = near_ref.shape
    for d in range(TEAM):
        for r in range(rows):
            source = lax.rem(spot[1] + r, rows)
            for j in range(per):
                start = ((j * rows + source) * TEAM + (spot[0] ^ d)) * tiles
                piece = tokens[pl.ds(pl.multiple_of(start, tiles), tiles), :]
                (far_ref if d % 2 else near_ref)[d // 2, r, j] = piece


def project_rows(begin, member, table_ref, weight_ref, bias_ref, outs, hidden_ref, width, head):
    mods = dot(member, table_ref[:, : 2 * width])
    normed, _ = normalize(begin)
    hidden = (normed * (1.0 + mods[:, width:]) + mods[:, :width]).astype(BF16)
    if hidden_ref is not None:
        hidden_ref[...] = hidden
    both = dot(hidden, weight_ref[...])
    part = both.shape[1] // 4
    low = both[:, : 3 * part].astype(BF16)
    turned = low.T
    count = part // head
    q_ref, k_ref, v_ref, key_ref, value_ref, gate_ref = outs
    q_ref[...] = (turned[:part] * BF16(head**-0.5)).reshape(count, head, -1)
    k_ref[...] = turned[part : 2 * part].reshape(count, head, -1)
    v_ref[...] = turned[2 * part :].reshape(count, head, -1)
    for h in range(count):
        key_ref[h] = low[:, part + h * head : part + (h + 1) * head]
        value_ref[h] = low[:, 2 * part + h * head : 2 * part + (h + 1) * head]
    gate_ref[...] = (both[:, 3 * part :].T + bias_ref[:, :1]).reshape(count, head, -1)


def qkv_specs(count, head, tokens, block):
    wide = pl.BlockSpec((count, head, block), lambda j, *_: (0, 0, j))
    tall = pl.BlockSpec((count, block, head), lambda j, *_: (0, j, 0))
    shapes = [jax.ShapeDtypeStruct((count, head, tokens), BF16)] * 3
    shapes += [jax.ShapeDtypeStruct((count, tokens, head), BF16)] * 2
    shapes += [jax.ShapeDtypeStruct((count, head, tokens), F32)]
    return [wide, wide, wide, tall, tall, wide], shapes


def first_rows(team, chunks, member, table, weight, gate_bias, count, head, block):
    rows, grain, tiles, width = chunks[0].shape
    tokens = rows * grain * tiles * TEAM
    per = block * grain // tokens

    def kernel(team_ref, c0, c1, c2, c3, member_ref, table_ref, weight_ref, bias_ref, row_ref, *rest):
        *outs, scratch = rest
        assemble(team_ref, (c0, c1, c2, c3), scratch)
        row_ref[...] = scratch[...]
        begin = scratch[...].astype(F32)
        project_rows(
            begin, member_ref[...], table_ref, weight_ref, bias_ref, outs, None, width, head
        )

    specs, shapes = qkv_specs(count, head, tokens, block)
    by_token = pl.BlockSpec((block, width), lambda j, *_: (j, 0))
    return call(
        kernel,
        (grain // per,),
        [pl.BlockSpec((rows, per, tiles, width), lambda j, *_: (0, j, 0, 0))] * 4
        + [
            pl.BlockSpec((block, member.shape[1]), lambda j, *_: (j, 0)),
            whole(table.shape),
            whole(weight.shape),
            whole(gate_bias.shape),
        ],
        [by_token] + specs,
        [jax.ShapeDtypeStruct((tokens, width), BF16)] + shapes,
        [pltpu.VMEM((block, width), BF16)],
        micros=8,
        mib=50,
        prefetch=1,
    )(team, *chunks, member, table, weight, gate_bias)


def begin_of(row_ref, point_ref, recycle_ref):
    return row_ref[...].astype(F32) + dot(point_ref[...].astype(BF16), recycle_ref[...], TN)


def second_rows(row, points, recycle, member, table, weight, gate_bias, count, head, block):
    tokens, width = row.shape

    def kernel(row_ref, point_ref, recycle_ref, member_ref, table_ref, weight_ref, bias_ref, hidden_ref, *outs):
        begin = begin_of(row_ref, point_ref, recycle_ref)
        project_rows(
            begin, member_ref[...], table_ref, weight_ref, bias_ref, outs, hidden_ref, width, head
        )

    specs, shapes = qkv_specs(count, head, tokens, block)
    by_token = pl.BlockSpec((block, width), lambda j: (j, 0))
    return call(
        kernel,
        (tokens // block,),
        [
            by_token,
            pl.BlockSpec((8, block), lambda j: (0, j)),
            whole(recycle.shape),
            pl.BlockSpec((block, member.shape[1]), lambda j: (j, 0)),
            whole(table.shape),
            whole(weight.shape),
            whole(gate_bias.shape),
        ],
        [by_token] + specs,
        [jax.ShapeDtypeStruct((tokens, width), BF16)] + shapes,
        micros=6,
        mib=50,
    )(row, points, recycle, member, table, weight, gate_bias)


def attend(queries, keys, values, gate, bias, q_chain, k_chain, place, tiles, block, keep):
    count, head, tokens = queries.shape
    key_tokens = keys.shape[1]
    sources = len(place)
    folds = key_tokens // block
    grain = tokens // block

    def kernel(q_ref, k_ref, v_ref, gate_ref, bias_ref, qc_ref, kc_ref, mixed_ref, *rest):
        if keep:
            attended_ref, probs_ref, share_ref, spread = rest
        else:
            (spread,) = rest

        for b in range(sources):
            spread[place[b] * tiles : (place[b] + 1) * tiles, :] = bias_ref[b, 0].astype(F32)

        def score(i):
            lanes = slice(i * block, (i + 1) * block)
            q, q_chain = q_ref[0, :, lanes], qc_ref[0:1, lanes]
            scores = []
            for f in range(folds):
                lines = slice(f * block, (f + 1) * block)
                part = f // grain
                s = dot(k_ref[0, lines, :], q) + spread[part * block : (part + 1) * block, :]
                same = jnp.concatenate([kc_ref[lines, :]] * (block // 128), axis=1) == q_chain
                scores.append(jnp.where(same, s, -1000000000.0))
            return scores

        def weigh(i, scores):
            lanes = slice(i * block, (i + 1) * block)
            top = functools.reduce(
                jnp.maximum, [jnp.max(s, axis=0, keepdims=True) for s in scores]
            )
            total = jnp.zeros((1, block), F32)
            attended = jnp.zeros((head, block), F32)
            for f in range(folds):
                lines = slice(f * block, (f + 1) * block)
                power = jnp.exp(scores[f] - top)
                total += jnp.sum(power, axis=0, keepdims=True)
                low = power.astype(BF16)
                if keep:
                    probs_ref[0, lines, lanes] = low
                attended += dot(v_ref[0, :, lines], low)
            share = 1.0 / total
            attended *= share
            mixed_ref[0, :, lanes] = (attended * jax.nn.sigmoid(gate_ref[0, :, lanes])).astype(BF16)
            if keep:
                attended_ref[0, :, lanes] = attended
                share_ref[0, :, lanes] = jnp.broadcast_to(share, (8, block))

        now = score(0)
        for i in range(grain):
            later = score(i + 1) if i + 1 < grain else None
            weigh(i, now)
            now = later

    by_head = lambda *shape: pl.BlockSpec((1,) + shape, lambda h: (h,) + (0,) * len(shape))
    outs = [by_head(head, tokens)]
    shapes = [jax.ShapeDtypeStruct((count, head, tokens), BF16)]
    if keep:
        outs += [by_head(head, tokens), by_head(key_tokens, tokens), by_head(8, tokens)]
        shapes += [
            jax.ShapeDtypeStruct((count, head, tokens), F32),
            jax.ShapeDtypeStruct((count, key_tokens, tokens), BF16),
            jax.ShapeDtypeStruct((count, 8, tokens), F32),
        ]
    return call(
        kernel,
        (count,),
        [
            by_head(head, tokens),
            by_head(key_tokens, head),
            by_head(head, key_tokens),
            by_head(head, tokens),
            pl.BlockSpec((sources, 1, tiles, block), lambda h: (0, h, 0, 0)),
            whole(q_chain.shape),
            whole(k_chain.shape),
        ],
        outs,
        shapes,
        [pltpu.VMEM((sources * tiles, block), F32)],
        micros=9 if keep else 6,
        mib=50,
    )(queries, keys, values, gate, bias, q_chain, k_chain)


def attend_back(queries, keys, value_rows, gate, attended, probs, share, own, other, place, tiles, block):
    count, head, tokens = queries.shape
    key_tokens = value_rows.shape[1]
    folds, grain = key_tokens // block, tokens // block
    sources = len(place)

    def kernel(
        q_ref, k_ref, v_ref, gate_ref, attended_ref, probs_ref, share_ref, own_ref, other_ref,
        dq_ref, dk_ref, dv_ref, logit_ref, bias_ref, bias_sum,
    ):
        grad_mixed = own_ref[0].astype(F32) + other_ref[0].astype(F32)
        sigma = jax.nn.sigmoid(gate_ref[0])
        through = grad_mixed * sigma
        upper = through.astype(BF16).astype(F32)
        attended = attended_ref[0]
        logit_ref[0] = (through * attended * (1.0 - sigma)).astype(BF16)
        share = share_ref[0, 0:1, :]
        inner = jnp.sum(upper * attended, axis=0, keepdims=True) * share
        scaled = (upper * share).astype(BF16)
        q = q_ref[0]
        grad_q = jnp.zeros((head, tokens), F32)
        tile_sums = [None] * (folds // grain)
        for f in range(folds):
            lines = slice(f * block, (f + 1) * block)
            power = probs_ref[0, lines, :]
            dv_ref[0, :, lines] = dot(scaled, power, NT).astype(BF16)
            grads = power.astype(F32) * (dot(v_ref[0, lines, :], scaled) - inner)
            low = grads.astype(BF16)
            grad_q += dot(k_ref[0, :, lines], low)
            dk_ref[0, :, lines] = dot(q, low, NT).astype(BF16)
            part = f // grain
            for i in range(grain):
                piece = grads[:, i * block : (i + 1) * block]
                tile_sums[part] = piece if tile_sums[part] is None else tile_sums[part] + piece
        dq_ref[0] = (grad_q * head**-0.5).astype(BF16)
        for part, sums in enumerate(tile_sums):
            bias_sum[part * block : (part + 1) * block, :] = sums
        for b in range(sources):
            lines = slice(place[b] * tiles, (place[b] + 1) * tiles)
            bias_ref[b, 0] = bias_sum[lines, :].astype(BF16)

    by_head = lambda *shape: pl.BlockSpec((1,) + shape, lambda h: (h,) + (0,) * len(shape))
    narrow = jax.ShapeDtypeStruct((count, head, tokens), BF16)
    broad = jax.ShapeDtypeStruct((count, head, key_tokens), BF16)
    return call(
        kernel,
        (count,),
        [
            by_head(head, tokens),
            by_head(head, key_tokens),
            by_head(key_tokens, head),
            by_head(head, tokens),
            by_head(head, tokens),
            by_head(key_tokens, tokens),
            by_head(8, tokens),
            by_head(head, tokens),
            by_head(head, tokens),
        ],
        [
            by_head(head, tokens),
            by_head(head, key_tokens),
            by_head(head, key_tokens),
            by_head(head, tokens),
            pl.BlockSpec((sources, 1, tiles, block), lambda h: (0, h, 0, 0)),
        ],
        [narrow, broad, broad, narrow, jax.ShapeDtypeStruct((sources, count, tiles, block), BF16)],
        [
            pltpu.VMEM((sources * tiles, block), F32),
        ],
        micros=10,
        mib=50,
    )(queries, keys, value_rows, gate, attended, probs, share, own, other)


def unpack(spot, bundle_refs, mixed_refs, weights, mixed, first):
    near, tail, *far = bundle_refs
    groups, _, part, wide = near.shape

    @pl.when(first)
    def _():
        mine = pl.multiple_of(spot[2] * wide, wide)
        other = pl.multiple_of((1 - spot[2]) * wide, wide)
        for g in range(groups):
            lines = slice(g * part, (g + 1) * part)
            for k in range(2):
                weights[k, lines, pl.ds(mine, wide)] = near[g, k]
                if far:
                    weights[k, lines, pl.ds(other, wide)] = far[0][g, k]
            weights[2, lines, pl.ds(mine, wide)] = tail[g, :, :wide]
            if far:
                weights[2, lines, pl.ds(other, wide)] = far[1][g]
            weights[3, lines, :] = tail[g, :, wide:]

    count, head, _ = mixed_refs[0].shape
    size = count * head
    for d, ref in enumerate(mixed_refs):
        start = pl.multiple_of((spot[0] ^ d) * size, size)
        mixed[pl.ds(start, size), :] = ref[...].reshape(size, -1)


def feed_first(team, mixed_chunks, row, member, table, bundle, coordinate, block):
    tokens, width = row.shape
    count, head, _ = mixed_chunks[0].shape

    def kernel(team_ref, m0, m1, m2, m3, row_ref, member_ref, table_ref, coord_ref, *rest):
        *bundle_refs, out_ref, weights, mixed = rest
        unpack(team_ref, bundle_refs, (m0, m1, m2, m3), weights, mixed, pl.program_id(0) == 0)
        mods = dot(member_ref[...], table_ref[:, 2 * width :])
        attend_gate, feed_shift = mods[:, :width], mods[:, width : 2 * width]
        feed_scale, feed_gate = mods[:, 2 * width : 3 * width], mods[:, 3 * width :]
        attend_out = dot(mixed[...], weights[0], TN)
        after = row_ref[...].astype(F32) + attend_gate * attend_out
        normed, _ = normalize(after)
        hidden = (normed * (1.0 + feed_scale) + feed_shift).astype(BF16)
        gate_pre, lift_pre = dot(hidden, weights[1]), dot(hidden, weights[2])
        inner = (gate_pre * jax.nn.sigmoid(gate_pre) * lift_pre).astype(BF16)
        share = after * (1.0 / TEAM) + feed_gate * dot(inner, weights[3])
        out_ref[...] = dot(coord_ref[...], share.astype(BF16), NT)

    by_token = pl.BlockSpec((block, width), lambda j, *_: (j, 0))
    return call(
        kernel,
        (tokens // block,),
        [pl.BlockSpec((count, head, block), lambda j, *_: (0, 0, j))] * 4
        + [
            by_token,
            pl.BlockSpec((block, member.shape[1]), lambda j, *_: (j, 0)),
            whole(table.shape),
            whole(coordinate.shape),
        ]
        + [whole(x.shape) for x in bundle],
        pl.BlockSpec((8, block), lambda j, *_: (0, j)),
        jax.ShapeDtypeStruct((8, tokens), F32),
        [pltpu.VMEM((4, width, width), BF16), pltpu.VMEM((width, block), BF16)],
        micros=12,
        mib=50,
        prefetch=1,
    )(team, *mixed_chunks, row, member, table, coordinate, *bundle)


def feed_both(team, mixed_chunks, row, points, recycle, cotangent, member, chains, table, bundle, block):
    tokens, width = row.shape
    count, head, _ = mixed_chunks[0].shape
    groups = bundle[0].shape[0]
    part = width // groups
    wide = bundle[0].shape[3]
    sides = width // wide
    rows, grain, tiles, _ = cotangent[0].shape
    last = tokens // block - 1
    size = count * head

    def kernel(team_ref, m0, m1, m2, m3, row_ref, point_ref, recycle_ref, c0, c1, c2, c3, member_ref, chain_ref,
               table_ref, *rest):
        bundle_refs, rest = rest[: len(bundle)], rest[len(bundle) :]
        near_out_ref, far_out_ref, after_ref, near_ref, far_ref, chain_sum_ref, down_ref = rest[:7]
        grad_refs, (weights, mixed, upstream, sums, turned) = rest[7:-5], rest[-5:]
        team = team_ref[0]
        first = pl.program_id(0) == 0
        unpack(team_ref, bundle_refs, (m0, m1, m2, m3), weights, mixed, first)
        assemble(team_ref, (c0, c1, c2, c3), upstream)

        @pl.when(first)
        def _():
            sums[...] = jnp.zeros_like(sums)
            chain_sum_ref[...] = jnp.zeros_like(chain_sum_ref)

        def work(lines):
            mods = dot(member_ref[lines, :], table_ref[:, 2 * width :])
            attend_gate, feed_shift = mods[:, :width], mods[:, width : 2 * width]
            feed_scale, feed_gate = mods[:, 2 * width : 3 * width], mods[:, 3 * width :]
            attend_out = dot(mixed[:, lines], weights[0], TN)
            yield
            after = row_ref[lines, :].astype(F32)
            after += dot(point_ref[:, lines].astype(BF16), recycle_ref[...], TN)
            after += attend_gate * attend_out
            normed, inverse = normalize(after)
            hidden = (normed * (1.0 + feed_scale) + feed_shift).astype(BF16)
            yield
            gate_pre, lift_pre = dot(hidden, weights[1]), dot(hidden, weights[2])
            yield
            sigma = jax.nn.sigmoid(gate_pre)
            silu = gate_pre * sigma
            inner = (silu * lift_pre).astype(BF16)
            yield
            branch = dot(inner, weights[3])
            g = upstream[lines, :].astype(F32)
            grad_branch = (g * feed_gate).astype(BF16)
            grad_inner = dot(grad_branch, weights[3], NT)
            yield
            upstream[lines, :] = (after * (1.0 / TEAM) + feed_gate * branch).astype(BF16)
            chain = chain_ref[:, lines]

            def by_chain(place, grad):
                lanes = slice(place * width, (place + 1) * width)
                chain_sum_ref[:, lanes] += dot(chain, grad.astype(BF16))

            by_chain(3, g * branch)
            grad_gate = grad_inner * lift_pre * sigma * (1.0 + gate_pre * (1.0 - sigma))
            grad_gate = grad_gate.astype(BF16)
            grad_lift = (grad_inner * silu).astype(BF16)
            yield
            grad_hidden = dot(grad_gate, weights[1], NT) + dot(grad_lift, weights[2], NT)
            sums[0] += dot(inner, grad_branch, TN)
            yield
            by_chain(1, grad_hidden)
            by_chain(2, grad_hidden * normed)
            grad_after = g * (1.0 / TEAM)
            grad_after += norm_back(grad_hidden * (1.0 + feed_scale), normed, inverse)
            after_ref[lines, :] = grad_after
            grad_out = (grad_after * attend_gate).astype(BF16)
            yield
            sums[1] += dot(hidden, grad_gate, TN)
            sums[2] += dot(hidden, grad_lift, TN)
            turned[:, lines] = dot(grad_out, weights[0], NT).T.astype(BF16)
            yield
            sums[3] += dot(mixed[:, lines], grad_out)
            by_chain(0, grad_after * attend_out)

        todo = [work(slice(h * block // 2, (h + 1) * block // 2)) for h in range(2)]
        while todo:
            todo = [x for x in todo if next(x, todo) is None]
        by_owner(team_ref, upstream, near_out_ref, far_out_ref)
        for d in range(TEAM):
            start = pl.multiple_of((team ^ d) * size, size)
            piece = turned[pl.ds(start, size), :].reshape(count, head, block)
            (far_ref if d % 2 else near_ref)[d // 2] = piece

        @pl.when(pl.program_id(0) == last)
        def _():
            for g in range(groups):
                lines = slice(g * part, (g + 1) * part)
                down_ref[g] = sums[0, lines, :].astype(BF16)
                for side, ref in enumerate(grad_refs):
                    start = pl.multiple_of((team_ref[2] ^ side) * wide, wide)
                    for k in range(3):
                        ref[g, k] = sums[1 + k, lines, pl.ds(start, wide)].astype(BF16)

    by_token = pl.BlockSpec((block, width), lambda j, *_: (j, 0))
    by_lane = pl.BlockSpec((8, block), lambda j, *_: (0, j))
    owned = pl.BlockSpec((2, rows, block * grain // tokens, tiles, width), lambda j, *_: (0, 0, j, 0, 0))
    halves = pl.BlockSpec((2, count, head, block), lambda j, *_: (0, 0, 0, j))
    half = jax.ShapeDtypeStruct((2, count, head, tokens), BF16)
    return call(
        kernel,
        (tokens // block,),
        [pl.BlockSpec((count, head, block), lambda j, *_: (0, 0, j))] * 4
        + [by_token, by_lane, whole(recycle.shape)]
        + [pl.BlockSpec((rows, block * grain // tokens, tiles, width), lambda j, *_: (0, j, 0, 0))] * 4
        + [
            pl.BlockSpec((block, member.shape[1]), lambda j, *_: (j, 0)),
            by_lane,
            whole(table.shape),
        ]
        + [whole(x.shape) for x in bundle],
        [owned, owned, by_token, halves, halves, held((8, 4 * width)), held((groups, part, width))]
        + [held((groups, 3, part, wide))] * sides,
        [
            jax.ShapeDtypeStruct((2, rows, grain, tiles, width), BF16),
            jax.ShapeDtypeStruct((2, rows, grain, tiles, width), BF16),
            jax.ShapeDtypeStruct((tokens, width), F32),
            half,
            half,
            jax.ShapeDtypeStruct((8, 4 * width), F32),
            jax.ShapeDtypeStruct((groups, part, width), BF16),
        ]
        + [jax.ShapeDtypeStruct((groups, 3, part, wide), BF16)] * sides,
        [
            pltpu.VMEM((4, width, width), BF16),
            pltpu.VMEM((width, block), BF16),
            pltpu.VMEM((block, width), BF16),
            pltpu.VMEM((4, width, width), F32),
            pltpu.VMEM((width, block), BF16),
        ],
        micros=31,
        mib=56,
        prefetch=1,
    )(team, *mixed_chunks, row, points, recycle, *cotangent, member, chains, table, *bundle)


def finish(spot, hidden, row, points, recycle, grad_after, grads, member, chains, chain_feed, table, weight, slot, rows, tiles, groups, sides, block):
    tokens, width = row.shape
    count, head, _ = grads[0].shape
    size = count * head
    part = width // groups
    wide = 4 * size // sides
    last = tokens // block - 1
    coords = 3
    grain = tokens // (rows * TEAM * tiles)
    per = block * grain // tokens

    def kernel(spot_ref, hidden_ref, row_ref, point_ref, recycle_ref, after_ref, q_ref, k_ref, v_ref, gate_ref,
               member_ref, chain_ref, feed_ref, table_ref, weight_ref,
               near_ref, far_ref, line_ref, *rest):
        *sum_refs, sums, owners, chain_sum_ref, recycle_sum_ref, gate_sum_ref = rest
        first = pl.program_id(0) == 0

        @pl.when(first)
        def _():
            sums[...] = jnp.zeros_like(sums)
            chain_sum_ref[...] = jnp.zeros_like(chain_sum_ref)
            recycle_sum_ref[...] = jnp.zeros_like(recycle_sum_ref)
            gate_sum_ref[...] = jnp.zeros_like(gate_sum_ref)

        stacked = jnp.concatenate(
            [ref[...].reshape(size, block) for ref in (q_ref, k_ref, v_ref, gate_ref)], axis=0
        )
        low = stacked.T
        gate_sum_ref[...] += jnp.sum(low[:, 3 * size :].astype(F32), axis=0, keepdims=True)
        sums[...] += dot(hidden_ref[...], low, TN)
        grad_hidden = dot(low, weight_ref[...], NT)
        mods = dot(member_ref[...], table_ref[:, width : 2 * width])
        normed, inverse = normalize(begin_of(row_ref, point_ref, recycle_ref))
        chain = chain_ref[...]
        chain_sum_ref[:, :width] += dot(chain, grad_hidden.astype(BF16))
        chain_sum_ref[:, width:] += dot(chain, (grad_hidden * normed).astype(BF16))
        grad = after_ref[...] + norm_back(grad_hidden * (1.0 + mods), normed, inverse)
        low_grad = grad.astype(BF16)
        owners[...] = low_grad
        by_owner(spot_ref, owners, near_ref, far_ref)
        recycle_sum_ref[...] += dot(point_ref[...].astype(BF16), low_grad)

        @pl.when(pl.program_id(0) == last)
        def _():
            line_ref[...] = jnp.zeros_like(line_ref)
            line_ref[:, : 2 * width] = chain_sum_ref[...]
            line_ref[:, 2 * width :] = feed_ref[...]
            for k in range(coords):
                lanes = slice(k * width, (k + 1) * width)
                line_ref[RECYCLE : RECYCLE + 1, lanes] = recycle_sum_ref[k : k + 1, :]
            start = pl.multiple_of(slot + spot_ref[0] * 256, 256)
            line_ref[GRADS : GRADS + 1, pl.ds(start, size)] = gate_sum_ref[...]
            for side, ref in enumerate(sum_refs):
                start = pl.multiple_of((spot_ref[2] ^ side) * wide, wide)
                for g in range(groups):
                    ref[g] = sums[g * part : (g + 1) * part, pl.ds(start, wide)].astype(BF16)

    by_token = pl.BlockSpec((block, width), lambda j, *_: (j, 0))
    by_lane = pl.BlockSpec((8, block), lambda j, *_: (0, j))
    by_query = pl.BlockSpec((count, head, block), lambda j, *_: (0, 0, j))
    owned = pl.BlockSpec((2, rows, per, tiles, width), lambda j, *_: (0, 0, j, 0, 0))
    return call(
        kernel,
        (tokens // block,),
        [by_token, by_token, by_lane, whole(recycle.shape), by_token]
        + [by_query] * 4
        + [
            pl.BlockSpec((block, member.shape[1]), lambda j, *_: (j, 0)),
            by_lane,
            whole(chain_feed.shape),
            whole(table.shape),
            whole(weight.shape),
        ],
        [
            owned,
            owned,
            held((8, 6 * width)),
        ]
        + [held((groups, part, wide))] * sides,
        [
            jax.ShapeDtypeStruct((2, rows, grain, tiles, width), BF16),
            jax.ShapeDtypeStruct((2, rows, grain, tiles, width), BF16),
            jax.ShapeDtypeStruct((8, 6 * width), F32),
        ]
        + [jax.ShapeDtypeStruct((groups, part, wide), BF16)] * sides,
        [
            pltpu.VMEM((width, 4 * size), F32),
            pltpu.VMEM((block, width), BF16),
            pltpu.VMEM((8, 2 * width), F32),
            pltpu.VMEM((8, width), F32),
            pltpu.VMEM((1, size), F32),
        ],
        micros=11,
        mib=50,
        prefetch=1,
    )(spot, hidden, row, points, recycle, grad_after, *grads, member, chains, chain_feed, table, weight)


def to_slots(spot, *kinds):
    rows, many = len(kinds[0]), len(kinds)
    grain, tiles, width = kinds[0][0].shape
    local = grain * tiles

    def kernel(spot_ref, *refs):
        inputs, outs, spread = refs[: many * rows], refs[many * rows : -1], refs[-1]
        for k in range(many):
            for d in range(rows):
                row = lax.rem(spot_ref[1] + rows - d, rows)
                for c in range(width // 128):
                    lanes = slice(c * 128, (c + 1) * 128)
                    for j in range(grain):
                        piece = inputs[k * rows + d][j, :, lanes].astype(F32)
                        spread[c, pl.ds(j, tiles, stride=grain), :] = piece
                    outs[k][pl.ds(row, 1), :, lanes] = spread[c].astype(BF16)[None]

    return call(
        kernel,
        (1,),
        [whole((grain, tiles, width))] * (many * rows),
        [held((rows, local, width))] * many,
        [jax.ShapeDtypeStruct((rows, local, width), BF16)] * many,
        [pltpu.VMEM((width // 128, local, 128), F32)],
        micros=2,
        mib=50,
        prefetch=1,
    )(spot, *[x for kind in kinds for x in kind])


def chain_products(spot, lines, weights, modulate, first):
    many, long = lines[0].shape
    count = len(lines)
    width = modulate.shape[0]

    def kernel(spot_ref, *refs):
        line_refs, (weight_ref, modulate_ref, first_ref, rest_ref, back_ref) = refs[:count], refs[count:]
        total = None
        for n, ref in enumerate(line_refs):
            part = dot(weight_ref[n], ref[...])
            total = part if total is None else total + part
            group = lax.rem(spot_ref[3] + count - n, count)
            back_ref[pl.ds(group, 1)] = dot(ref[...], modulate_ref[...], NT)[None]
        first_ref[...] = total[:first]
        rest_ref[...] = total[first:]

    rest = weights.shape[1] - first
    return call(
        kernel,
        (1,),
        [whole((many, long))] * count + [whole(weights.shape), whole(modulate.shape)],
        [held((first, long)), held((rest, long)), held((count, many, width))],
        [
            jax.ShapeDtypeStruct((first, long), F32),
            jax.ShapeDtypeStruct((rest, long), F32),
            jax.ShapeDtypeStruct((count, many, width), F32),
        ],
        micros=5,
        mib=50,
        prefetch=1,
    )(spot, *lines, weights, modulate)


def per_device(
    residues,
    pair_features,
    chain_lengths,
    time_bins,
    fold_class,
    self_flag,
    time_table,
    class_table,
    modulate,
    offset,
    heads,
    pairing,
    gating,
    gating_bias,
    project,
    widen_gate,
    widen_up,
    narrow,
    coordinate,
    recycle,
    cotangent,
):
    blocks = lax.axis_size("blk")
    planes = lax.axis_size("rows")
    myself = lax.axis_index("blk")
    rows, local, width = residues.shape
    row_len = local * blocks
    grain = row_len // pair_features.shape[1]
    tiles = local // grain
    head_count = pairing.shape[1]
    head = width // head_count
    count = head_count // TEAM
    size = count * head
    span = blocks // rows
    parts = span // TEAM
    groups = blocks // TEAM
    tokens = row_len // parts
    block = tokens // grain
    max_chains = chain_lengths.shape[1]
    my_row = myself // span
    my_part = (myself % span) // TEAM
    team = myself % TEAM
    sides = 2 if planes % 2 == 0 else 1
    my_side = lax.axis_index("rows") % sides
    team_ref = jnp.stack([team, my_row, my_side, myself // TEAM]).astype(jnp.int32)
    place = []
    for b in range(blocks):
        r, u, t = b // span, (b % span) // TEAM, b % TEAM
        place.append((u * rows + r) * TEAM + t)

    row_groups = [[r * span + s for r in range(rows)] for s in range(span)]
    same_team = [[g * TEAM + t for g in range(groups)] for t in range(TEAM)]
    teams = [[g * TEAM + t for t in range(TEAM)] for g in range(groups)]
    part_groups = [
        [r * span + u * TEAM + t for u in range(parts)] for r in range(rows) for t in range(TEAM)
    ]

    def swap(x, k):
        return lax.ppermute(x, "blk", [(b, b ^ k) for b in range(blocks)])

    def team_gather(x):
        far = swap(x, 2)
        return x, swap(x, 1), far, swap(far, 1)

    def group_sum(x):
        k = 1
        while k < span:
            x = x + swap(x, k)
            k *= 2
        return x

    def exchange(x, members=None):
        return lax.all_to_all(x, "blk", 0, 0, tiled=True, axis_index_groups=members)

    def pick(x, d):
        return lax.dynamic_index_in_dim(x, team ^ d, 0, False)

    def ordered(x):
        x = list(x)
        for bit in (1, 2):
            moved = (team & bit) != 0
            x = [jnp.where(moved, x[d ^ bit], x[d]) for d in range(TEAM)]
        return x

    def across(x):
        return lax.ppermute(x, "rows", [(p, p ^ 1) for p in range(planes)])

    def my_half(x, axis, other=0):
        wide = x.shape[axis] // sides
        return lax.dynamic_slice_in_dim(x, (my_side ^ other) * wide, wide, axis)

    def unite(x, axis):
        if sides == 1:
            return x
        y = across(x)
        return jnp.concatenate([jnp.where(my_side == 0, x, y), jnp.where(my_side == 0, y, x)], axis)

    def add_planes(x):
        if planes > 2:
            x = lax.psum(x, "rows", axis_index_groups=[list(range(p, planes, 2)) for p in range(2)])
        return x

    def pair_sum(x):
        if sides == 1:
            return x[0]
        return (x[0].astype(F32) + across(x[1]).astype(F32)).astype(BF16)

    def scatter(x):
        x = lax.psum_scatter(
            x, "blk", scatter_dimension=0, axis_index_groups=same_team, tiled=True
        )
        return add_planes(x)

    def after(x, *others):
        return lax.optimization_barrier((x, *others))[0]

    def row_shift(x):
        found = [lax.dynamic_index_in_dim(x, my_row, 0, False)]
        for d in range(1, rows):
            piece = lax.dynamic_index_in_dim(x, (my_row + d) % rows, 0, False)
            pairs = [(b, (b + d * span) % blocks) for b in range(blocks)]
            found.append(lax.ppermute(piece, "blk", pairs))
        return found

    def fold(x):
        return x.reshape(rows, tiles, grain, width).transpose(0, 2, 1, 3)

    depth = heads.shape[0]
    attend_w = jnp.concatenate(
        [heads.reshape(depth, 3, TEAM, size), gating.reshape(depth, 1, TEAM, size)], axis=1
    )
    attend_w = my_half(attend_w.transpose(2, 0, 1, 3).reshape(TEAM, depth, 4 * size), 1)
    attend_w = jnp.broadcast_to(attend_w[None], (groups,) + attend_w.shape)
    attend_w = exchange(attend_w.reshape(blocks, depth // sides, 4 * size))

    units = narrow.shape[0]
    widen = jnp.stack([widen_gate, widen_up], axis=0).reshape(2, depth, groups, TEAM, units)
    widen = my_half(widen, 2).transpose(3, 0, 1, 2, 4).reshape(TEAM, 2, depth, width // sides)
    out_w = my_half(project, 1)[None]
    widen = [pick(widen, d) for d in range(TEAM)]
    widen = [widen[0]] + [swap(widen[d], d) for d in range(1, TEAM)]
    widen = jnp.stack(ordered(widen), axis=1).reshape(2, TEAM * depth, width // sides)
    out_w = jnp.stack(ordered(team_gather(out_w)), axis=1).reshape(1, TEAM * depth, width // sides)
    def gather(x):
        return lax.all_gather(x, "blk", axis=0, axis_index_groups=same_team)

    first_bundle = jnp.concatenate([out_w, widen[:1]], axis=0)
    bundle = [gather(first_bundle)]
    bundle.append(gather(jnp.concatenate([widen[1], narrow], axis=1)))
    if sides == 2:
        bundle += [across(bundle[0]), across(bundle[1][:, :, : width // sides])]

    tile_bias = pair_bias(pair_features, after(pairing, first_bundle))

    hot = lambda ids, n: (ids[:, :, None] == jnp.arange(n, dtype=jnp.int32)).astype(F32)
    ids = jnp.concatenate([time_bins, fold_class], axis=1)
    if planes == 2:
        ids = jnp.concatenate([ids, across(ids)], axis=0)
    time_hot = hot(ids[:, :max_chains], time_table.shape[0])
    class_hot = hot(ids[:, max_chains:], class_table.shape[0])
    condition = jnp.einsum(
        "rcn,nd->rcd", time_hot, time_table.astype(F32), precision=HIGHEST
    ) + jnp.einsum("rcn,nd->rcd", class_hot, class_table.astype(F32), precision=HIGHEST)
    smooth = jax.nn.silu(condition).astype(BF16)
    cond_local = modulate.shape[0]
    my_smooth = lax.dynamic_slice_in_dim(smooth, myself * cond_local, cond_local, axis=2)
    per_chain = jnp.einsum("rcd,dm->rcm", my_smooth[:rows], modulate, preferred_element_type=F32)
    upper = lax.reduce_precision(per_chain, 8, 7)
    both = jnp.stack([upper, per_chain - upper], axis=1).astype(BF16).reshape(rows, -1, width)
    moved = jnp.stack(row_shift(jnp.concatenate([fold(residues).reshape(rows, local, width), both], axis=1)))
    moved = after(moved, tile_bias)
    row_chunks = team_gather(moved[:, :local].reshape(rows, grain, tiles, width))
    per_chain = moved[:, local:].reshape(2 * rows, max_chains, 6 * width).astype(F32)
    per_chain = group_sum(jnp.sum(per_chain, axis=0)) + offset.astype(F32)
    upper = lax.reduce_precision(per_chain, 8, 7)
    table = jnp.concatenate(
        [upper, per_chain - upper, jnp.zeros((16 - 2 * max_chains, per_chain.shape[1]), F32)],
        axis=0,
    ).astype(BF16)

    bias_out = tile_bias.reshape(rows, TEAM, count, tiles, rows, parts, TEAM * tiles)
    bias_out = bias_out.transpose(0, 5, 1, 2, 3, 4, 6).reshape(blocks, count, tiles, block)
    attend_w = unite(attend_w, 1).reshape(width, 4 * size)
    bias = exchange(after(bias_out, attend_w))

    ends = jnp.cumsum(lax.dynamic_index_in_dim(chain_lengths, my_row, 0, False))
    flags = lax.dynamic_index_in_dim(self_flag, my_row, 0, False)

    def slots(part):
        r = jnp.arange(rows, dtype=jnp.int32)[None, :, None, None]
        t = jnp.arange(TEAM, dtype=jnp.int32)[None, None, :, None]
        j = jnp.arange(grain, dtype=jnp.int32)[:, None, None, None]
        a = jnp.arange(tiles, dtype=jnp.int32)[None, None, None, :]
        return (((r * span + part * TEAM + t) * tiles + a) * grain + j).reshape(tokens)

    def chain_of(places):
        return jnp.sum((places[:, None] >= ends[None, :]).astype(jnp.int32), axis=1)

    q_chain = chain_of(slots(my_part))
    k_chain = chain_of(jnp.concatenate([slots(u) for u in range(parts)]))
    q_lines = jnp.broadcast_to(q_chain[None, :], (8, tokens))
    k_lines = jnp.broadcast_to(k_chain[:, None], (parts * tokens, 128))
    ids = jnp.arange(16, dtype=jnp.int32)
    ids = jnp.where(ids < 2 * max_chains, ids % max_chains, -1)
    member = (q_chain[:, None] == ids[None, :]).astype(BF16)
    chain_hot = q_chain[None, :] == jnp.arange(8, dtype=jnp.int32)[:, None]
    chains = chain_hot.astype(BF16)
    flag_lines = jnp.sum(
        jnp.where(chain_hot[:max_chains], flags.astype(F32)[:, None], 0.0), axis=0, keepdims=True
    )
    gate_bias = lax.dynamic_slice_in_dim(gating_bias, team * size, size).astype(F32)
    gate_bias = jnp.broadcast_to(gate_bias[:, None], (size, 128))
    points_w = jnp.pad(coordinate.T, ((0, 8 - coordinate.shape[1]), (0, 0)))
    recycle_w = jnp.pad(recycle, ((0, 8 - recycle.shape[0]), (0, 0)))

    def all_keys(keys, values):
        if parts == 1:
            return keys, values
        keys = lax.all_gather(keys, "blk", axis=0, axis_index_groups=part_groups)
        values = lax.all_gather(values, "blk", axis=0, axis_index_groups=part_groups)
        keys = keys.transpose(1, 0, 2, 3).reshape(count, parts * tokens, head)
        values = values.transpose(1, 2, 0, 3).reshape(count, head, parts * tokens)
        return keys, values

    row, q_one, _, v_one, key_one, _, gate_one = first_rows(
        team_ref, row_chunks, member, table, attend_w, gate_bias, count, head, tokens // 2
    )
    key_one, v_one = all_keys(key_one, v_one)
    upstream = jnp.stack(row_shift(fold(after(cotangent, row))))
    q_lines_one = after(q_lines, bundle[-sides])
    (mixed_one,) = attend(q_one, key_one, v_one, gate_one, bias, q_lines_one, k_lines, place, tiles, block, False)
    mixed_one = team_gather(after(mixed_one, bundle[1]))
    shares = feed_first(
        team_ref, mixed_one, row, member, table, bundle, points_w, tokens // 2
    )
    shares = shares + swap(shares, 1)
    shares = shares + swap(shares, 2)
    points = lax.reduce_precision(shares, 8, 7) * flag_lines

    views = 2 if planes == 2 else 1
    which = [(myself // TEAM + groups - d) % groups // parts for d in range(groups)]
    smooth_rows = smooth.reshape(views, rows, max_chains, -1)
    weights = jnp.stack([lax.dynamic_index_in_dim(smooth_rows, r, 1, False) for r in which])
    weights = jnp.pad(weights, ((0, 0), (0, 0), (0, 8 - max_chains), (0, 0)))
    weights = lax.dynamic_slice_in_dim(weights, myself * cond_local, cond_local, axis=3)
    weights = weights.reshape(groups, views * 8, cond_local)
    kind = jnp.arange(views * 8) % 8
    masks = jnp.stack([kind < max_chains, kind == GRADS, kind == RECYCLE], axis=1).astype(BF16)
    masks = jnp.broadcast_to(masks[None], (groups,) + masks.shape)
    weights = jnp.concatenate([weights, masks], axis=2).transpose(0, 2, 1)
    weights = jnp.pad(weights, ((0, 0), (0, -weights.shape[1] % 8), (0, 0)))

    modulate_full = lax.all_gather(after(modulate, row), "blk", axis=0, tiled=True)
    hidden, q_two, k_two, v_two, key_two, value_two, gate_two = second_rows(
        row, points, after(recycle_w, modulate_full, upstream, weights), member, table, attend_w, gate_bias, count, head, tokens // 2
    )
    key_two, v_all = all_keys(key_two, v_two)
    value_two, k_two = all_keys(value_two, k_two)
    mixed_two, attended, probs, share = attend(
        q_two, key_two, v_all, gate_two, bias, q_lines, k_lines, place, tiles, block, True
    )
    far = swap(after(upstream, points), 2)
    upstream = upstream, swap(upstream, 1), far, swap(after(far, q_two), 1)
    result_near, result_far, grad_after, near, far, chain_feed, down_grads, *feed_grads = feed_both(
        team_ref, team_gather(after(mixed_two, upstream[3])), row, points, recycle_w, upstream, member, chains, table,
        bundle, tokens // 2,
    )

    def near_sum(near, far):
        return (near.astype(F32) + swap(far, 1).astype(F32)).astype(BF16)

    def owner_shift(both, far):
        total = (both[0].astype(F32) + far.astype(F32)).astype(BF16)
        found = [total[0]]
        for d in range(1, rows):
            pairs = [(b, (b + d * span) % blocks) for b in range(blocks)]
            found.append(lax.ppermute(total[d], "blk", pairs))
        return found

    halves = (near.astype(F32) + swap(far, 1).astype(F32)).astype(BF16)
    other_half = swap(halves[1], 2)
    result_both = near_sum(result_near, after(result_far, halves))
    grad_q, grad_k, grad_v, grad_logit, bias_grad = attend_back(
        q_two, k_two, value_two, gate_two, attended, probs, share, halves[0], other_half, place, tiles, block
    )
    result_shift = owner_shift(result_both, swap(after(result_both[1], other_half), 2))
    bias_grad = exchange(bias_grad)
    if parts > 1:
        key_value = jnp.stack([grad_k, grad_v]).reshape(2, count, head, parts, tokens)
        key_value = lax.psum_scatter(
            key_value.transpose(3, 0, 1, 2, 4), "blk", scatter_dimension=0, axis_index_groups=part_groups
        )
        grad_k, grad_v = key_value[0], key_value[1]
    feed_grads = pair_sum(feed_grads)
    down_own = scatter(down_grads)[0]
    wide_own = scatter(feed_grads)[0].reshape(3, TEAM, depth, width // sides)
    gate_slot = head_count * pair_features.shape[3]
    begin_near, begin_far, line, *attend_grads = finish(
        team_ref, hidden, row, points, recycle_w, grad_after, (grad_q, grad_k, grad_v, grad_logit), member, chains, chain_feed,
        table, attend_w, gate_slot, rows, tiles, groups, sides, block,
    )

    stage = lax.optimization_barrier
    both = near_sum(begin_near, after(begin_far, bias_grad))
    both_far = swap(both[1], 2)
    bias_grad = bias_grad.reshape(rows, parts, TEAM, count, tiles, rows, TEAM * tiles)
    bias_grad = bias_grad.transpose(0, 2, 3, 4, 5, 1, 6).reshape(rows, head_count, tiles, parts * block)
    grad_pair, line = pair_back(pair_features, pairing, after(bias_grad, both), line)
    attend_far = across(attend_grads[1]) if sides == 2 else attend_grads[0]
    line, attend_far, both_far, down_own = stage((line, attend_far, both_far, down_own))
    attend_own = attend_grads[0]
    if sides == 2:
        attend_own = (attend_own.astype(F32) + attend_far.astype(F32)).astype(BF16)
    attend_own = exchange(attend_own.reshape(blocks, depth, 4 * size // sides))

    line = line + swap(line, 1)
    line_far = swap(line, 2)
    by_shift = owner_shift(both, both_far)
    line = (line + line_far).astype(BF16)
    line_far = across(line) if planes == 2 else line
    line_far, wide_own = stage((line_far, wide_own))
    if planes == 2:
        line = jnp.concatenate([line, line_far], axis=0)
    lines = [line]
    for d in range(1, groups):
        pairs = [(b, (b + d * TEAM) % blocks) for b in range(blocks)]
        lines.append(lax.ppermute(line, "blk", pairs))
    wide = exchange(after(wide_own, attend_own).transpose(1, 0, 2, 3), teams)
    attend_own, wide, by_shift, lines = stage((attend_own, wide, by_shift, lines))

    inner = jnp.sum(attend_own.astype(F32).reshape(groups, TEAM, depth, 4 // sides, size), axis=0)
    inner = add_planes(inner.astype(BF16)).transpose(1, 2, 0, 3).reshape(depth, 4 * width // sides)
    inner = unite(inner, 1).astype(F32)
    if planes == 2:
        grad_narrow = down_own.astype(F32) + across(down_own).astype(F32)
    else:
        grad_narrow = lax.psum(down_own, "rows").astype(F32)
    own_project = jnp.sum(wide[:, 2].astype(F32), axis=0).astype(BF16)
    wide = wide[:, :2].reshape(TEAM, 2, depth, groups // sides, units).transpose(1, 2, 3, 0, 4)
    wide = unite(wide.reshape(2, depth, TEAM * width // sides), 2).astype(F32)
    grad_project = unite(own_project, 1).astype(F32)

    layer_out, grad_residues = to_slots(team_ref, result_shift, by_shift)

    grad_modulate, sums, back = chain_products(team_ref, lines, weights, modulate_full, cond_local)
    grad_offset = sums[0]
    grad_pairing = sums[1, :gate_slot].reshape(head_count, -1).T
    grad_gatebias = sums[1, gate_slot : gate_slot + 256 * TEAM].reshape(TEAM, 256)[:, :size].reshape(width)
    grad_recycle = sums[2, : recycle.size].reshape(recycle.shape)
    grad_smooth = back.reshape(rows, parts, views, 8, -1)[:, :, :, :max_chains].sum(axis=1)
    grad_smooth = grad_smooth.transpose(1, 0, 2, 3).reshape(views * rows, max_chains, -1)
    sigma = jax.nn.sigmoid(condition)
    grad_condition = grad_smooth * sigma * (1.0 + condition * (1.0 - sigma))
    grad_time = jnp.einsum("rcn,rcd->nd", time_hot, grad_condition, precision=HIGHEST)
    grad_class = jnp.einsum("rcn,rcd->nd", class_hot, grad_condition, precision=HIGHEST)
    if planes != 2:
        found = (grad_time, grad_class, grad_modulate, grad_offset, grad_pairing, grad_gatebias, grad_recycle)
        found = lax.psum(found, "rows")
        grad_time, grad_class, grad_modulate, grad_offset, grad_pairing, grad_gatebias, grad_recycle = found
    return (
        layer_out,
        grad_residues,
        grad_pair,
        grad_time,
        grad_class,
        grad_modulate,
        grad_offset,
        inner[:, : 3 * width],
        grad_pairing,
        inner[:, 3 * width :],
        grad_gatebias,
        grad_project,
        wide[0],
        wide[1],
        grad_narrow,
        grad_recycle,
    )


def solution(mesh):
    in_specs = (
        P("rows", "blk", None),
        P("rows", None, "blk", None),
        P("rows", None),
        P("rows", None),
        P("rows", None),
        P("rows", None),
        P(),
        P(),
        P("blk", None),
        P(),
        P("blk", None),
        P(),
        P("blk", None),
        P(),
        P("blk", None),
        P("blk", None),
        P("blk", None),
        P("blk", None),
        P(),
        P(),
        P("rows", "blk", None),
    )
    out_specs = (
        P("rows", "blk", None),
        P("rows", "blk", None),
        P("rows", None, "blk", None),
        P(),
        P(),
        P("blk", None),
        P(),
        P("blk", None),
        P(),
        P("blk", None),
        P(),
        P("blk", None),
        P("blk", None),
        P("blk", None),
        P("blk", None),
        P(),
    )
    return jax.shard_map(
        per_device, mesh=mesh, in_specs=in_specs, out_specs=out_specs, check_vma=False
    )
```
